256 devices in a mesh: pipe: 16 (over y, x), tensor: 16 (over z, core).
Axes of the slice: x: 4, y: 4, z: 8, core: 2. Of those that a mesh axis runs over, the one named last changes fastest.
Arguments:
- segment_in: bfloat16 [16, 512, 4096], P('pipe'), may hold values from -8 to 8
- layer_weight: bfloat16 [16, 4096, 4096], P('pipe', None, 'tensor'), may hold values from -0.09375 to 0.09375
- layer_gain: float32 [16, 4096], P('pipe'), may hold values from 0.25 to 1.75
- final_gain: float32 [4096], replicated, may hold values from 0.25 to 1.75
- head_weight: bfloat16 [32000, 4096], P('pipe', 'tensor'), may hold values from -8 to 8
- exit_rows: int32 [16, 32], replicated, may hold values from 0 to 511, as said below
- exit_count: int32 [16], replicated, may hold values from 8 to 32, as said below
- exit_targets: int32 [16, 32], replicated, may hold values from 0 to 31999
- exit_scale: float32 [16], replicated, may hold values from 4 to 32
- out_grad: bfloat16 [16, 512, 4096], P('pipe'), may hold values from -6 to 6
Outputs:
- input_grad: bfloat16 [16, 512, 4096], P('pipe')
- weight_grad: bfloat16 [16, 4096, 4096], P('pipe', None, 'tensor')
- gain_grad: float32 [16, 4096], P('pipe')
- head_grad: bfloat16 [32000, 4096], P('pipe', 'tensor')
The draws below stay inside these ranges and needn't reach their ends.
Inputs may be any that keep to these rules, and one draw needn't show every extreme that they name: `exit_rows`: in each section the entries are distinct token rows; only the first exit_count entries are live, the others are ignored rows. `exit_count`: some section has all 32 slots live in every draw.
All inputs are finite; a program needn't handle non-finite values.
Results may differ from the reference program's by a relative error of at most 0.006.
Values may be sent and summed in bfloat16 or wider, within the bound.
No kernel may reach another device: no remote copies, remote signals or barrier semaphores. Data moves between devices by JAX's collectives and lax.ppermute only.
A program may use at most 128 MiB of HBM per device.

```python
import math
import jax
import jax.numpy as jnp
from jax import lax

D = 4096
VOCAB = 32000
TOK = 512
EXITS = 32
SEGMENTS = 16


def common_sign(key):
    sign_key = jax.random.fold_in(key, 7)
    return jnp.where(jax.random.bernoulli(sign_key, 0.5, (D,)), 1.0, -1.0).astype(jnp.float32)


def draw_segment_in(key, part):
    direction = common_sign(key)
    key = jax.random.fold_in(key, 41)
    weight_key = jax.random.fold_in(key, 2)
    along = jax.random.uniform(weight_key, (SEGMENTS, TOK, 1), jnp.float32, 0.0, 3.0)
    noise = jax.random.truncated_normal(key, -4.0, 4.0, (SEGMENTS, TOK, D), jnp.float32) * 0.5
    return (noise + along * direction).astype(jnp.bfloat16)


def draw_head_weight(key, part):
    key = jax.random.fold_in(key, 11)
    spread = 3.0 / math.sqrt(D)
    values = jax.random.truncated_normal(key, -4.0, 4.0, (VOCAB, D), jnp.float32) * spread
    return jnp.clip(values, -8.0, 8.0).astype(jnp.bfloat16)


def draw_exit_rows(key, part):
    key = jax.random.fold_in(key, 21)
    segment_keys = jax.random.split(key, SEGMENTS)
    picked = jax.vmap(lambda one_key: jax.random.permutation(one_key, TOK)[:EXITS])(segment_keys)
    return picked.astype(jnp.int32)


def draw_exit_count(key, part):
    key = jax.random.fold_in(key, 31)
    counts = jax.random.randint(key, (SEGMENTS,), EXITS // 4, EXITS + 1, dtype=jnp.int32)
    fullest = jax.random.randint(jax.random.fold_in(key, 5), (), 0, SEGMENTS, dtype=jnp.int32)
    return jnp.where(jnp.arange(SEGMENTS, dtype=jnp.int32) == fullest, EXITS, counts).astype(jnp.int32)


def touch_ends(values, rng, low, largest):
    extent = values.shape
    spot = [jax.random.randint(jax.random.fold_in(rng, axis), (), 0, extent[axis]) for axis in range(len(extent))]
    values = values.at[tuple(spot)].set(low)
    longest = extent.index(max(extent))
    spot[longest] = (spot[longest] + 1) % extent[longest]
    return values.at[tuple(spot)].set(largest)


def shard_levels(rng, dims, shards, least, top_value):
    loudness = 1.0
    for dim, shards_of in shards:
        steps = jax.random.uniform(jax.random.fold_in(jax.random.fold_in(rng, 6), dim), (shards_of,), jnp.float32, least / len(shards), top_value / len(shards))
        loudness = loudness * jnp.repeat(jnp.exp(steps), dims[dim] // shards_of).reshape((-1,) + (1,) * (len(dims) - 1 - dim))
    return loudness


def gaussian(stream_key, extent, width, reach, cuts=(), held_as=jnp.bfloat16):
    loudness = shard_levels(stream_key, extent, cuts, -0.22, 0.18) if cuts else 1.0
    values = jax.random.normal(stream_key, extent, jnp.float32) * width * loudness
    return jnp.minimum(jnp.maximum(values, -reach), reach).astype(held_as)


def setup_inputs(seed: int = 0) -> dict:
    streams_of = jax.random.split(jax.random.key(seed), 11)
    segment_in = draw_segment_in(jax.random.fold_in(streams_of[10], 71), 0)
    layer_weight = gaussian(streams_of[1], (SEGMENTS, D, D), D ** -0.5, 0.09375, ((0, 16), (2, 16)))
    layer_gain = jnp.clip(1.0 + 0.15 * jax.random.normal(streams_of[2], (SEGMENTS, D), jnp.float32), 0.25, 1.75)
    final_gain = jnp.clip(1.0 + 0.15 * jax.random.normal(streams_of[3], (D,), jnp.float32), 0.25, 1.75)
    head_weight = draw_head_weight(jax.random.fold_in(streams_of[10], 71), 0)
    exit_rows = draw_exit_rows(jax.random.fold_in(streams_of[10], 71), 0)
    exit_count = draw_exit_count(jax.random.fold_in(streams_of[10], 71), 0)
    exit_targets = touch_ends(jax.random.randint(streams_of[7], (SEGMENTS, EXITS), 0, VOCAB), jax.random.fold_in(streams_of[7], 1), 0, VOCAB - 1).astype(jnp.int32)
    exit_scale = jnp.clip(jnp.exp(jax.random.uniform(streams_of[8], (SEGMENTS,), jnp.float32, math.log(4.0), math.log(32.0))), 4.0, 32.0)
    out_grad = gaussian(streams_of[9], (SEGMENTS, TOK, D), 1.0, 6.0, ((0, 16),))
    return {"segment_in": segment_in, "layer_weight": layer_weight, "layer_gain": layer_gain, "final_gain": final_gain, "head_weight": head_weight, "exit_rows": exit_rows, "exit_count": exit_count, "exit_targets": exit_targets, "exit_scale": exit_scale, "out_grad": out_grad}


def reference(segment_in, layer_weight, layer_gain, final_gain, head_weight, exit_rows, exit_count, exit_targets, exit_scale, out_grad):
    epsilon = 1e-05
    inputs = segment_in.astype(jnp.float32)
    inv_rms = lax.rsqrt(lax.optimization_barrier(jnp.mean(inputs * inputs, axis=-1, keepdims=True)) + epsilon)
    unit = inputs * inv_rms
    normed = (unit * layer_gain[:, None, :]).astype(jnp.bfloat16)
    update = lax.map(lambda pair: jnp.dot(pair[0], pair[1], preferred_element_type=jnp.float32).astype(jnp.bfloat16), (normed, layer_weight))
    hidden = (inputs + update.astype(jnp.float32)).astype(jnp.bfloat16)
    exit_hidden = jnp.take_along_axis(hidden, exit_rows[:, :, None], axis=1).astype(jnp.float32)
    exit_inv = lax.rsqrt(lax.optimization_barrier(jnp.mean(exit_hidden * exit_hidden, axis=-1, keepdims=True)) + epsilon)
    exit_unit = exit_hidden * exit_inv
    exit_normed = (exit_unit * final_gain).astype(jnp.bfloat16).reshape(SEGMENTS * EXITS, D)
    logits = jnp.dot(exit_normed, head_weight.T, preferred_element_type=jnp.float32)
    row_top = lax.optimization_barrier(jnp.max(logits, axis=-1, keepdims=True))
    expo = jnp.exp(logits - row_top)
    probs = expo / lax.optimization_barrier(jnp.sum(expo, axis=-1, keepdims=True))
    slots = jnp.arange(EXITS, dtype=jnp.int32)
    live = slots[None, :] < exit_count[:, None]
    row_weight = jnp.where(live, exit_scale[:, None], jnp.float32(0.0)).astype(jnp.float32).reshape(-1)
    onehot = (jnp.arange(VOCAB, dtype=jnp.int32)[None, :] == exit_targets.reshape(-1)[:, None]).astype(jnp.float32)
    dlogits = (row_weight[:, None] * (probs - onehot)).astype(jnp.bfloat16)
    head_grad = jnp.dot(dlogits.T, exit_normed, preferred_element_type=jnp.float32).astype(jnp.bfloat16)
    exit_grad = jnp.dot(dlogits, head_weight, preferred_element_type=jnp.float32).reshape(SEGMENTS, EXITS, D)
    scaled = exit_grad * final_gain
    exit_back = (scaled - exit_unit * lax.optimization_barrier(jnp.mean(scaled * exit_unit, axis=-1, keepdims=True))) * exit_inv
    segment_ids = jnp.broadcast_to(jnp.arange(SEGMENTS, dtype=jnp.int32)[:, None], (SEGMENTS, EXITS))
    hidden_grad = out_grad.astype(jnp.float32).at[segment_ids, exit_rows].add(exit_back)
    grad_rounded = hidden_grad.astype(jnp.bfloat16)
    weight_grad = lax.map(lambda pair: jnp.dot(pair[0].T, pair[1], preferred_element_type=jnp.float32).astype(jnp.bfloat16), (normed, grad_rounded))
    normed_grad = lax.map(lambda pair: jnp.dot(pair[0], pair[1].T, preferred_element_type=jnp.float32), (grad_rounded, layer_weight))
    gain_grad = lax.optimization_barrier(jnp.sum(normed_grad * unit, axis=1))
    unit_grad = normed_grad * layer_gain[:, None, :]
    input_grad = (hidden_grad + (unit_grad - unit * lax.optimization_barrier(jnp.mean(unit_grad * unit, axis=-1, keepdims=True))) * inv_rms).astype(jnp.bfloat16)
    return (input_grad, weight_grad, gain_grad, head_grad)
```

```python
import jax
import jax.numpy as jnp
from jax import lax
from jax.sharding import Mesh, PartitionSpec as P

F32 = jnp.float32
BF16 = jnp.bfloat16
EPSILON = 1e-05


def rounded(values):
    return lax.reduce_precision(values, 8, 7)


def split3(values):
    first = rounded(values)
    rest = values - first
    second = rounded(rest)
    return [first, second, rest - second]


def spread(values, axis, count):
    return lax.all_to_all(jnp.broadcast_to(values[None], (count,) + values.shape), axis, 0, 0)


def swap(values):
    return lax.ppermute(values, "core", [(0, 1), (1, 0)])


def pair(mine, other, core, axis):
    first = jnp.where(core == 0, mine, other)
    second = jnp.where(core == 0, other, mine)
    return jnp.concatenate([first, second], axis=axis)


def local(
    segment_in,
    layer_weight,
    layer_gain,
    final_gain,
    head_weight,
    exit_rows,
    exit_count,
    exit_targets,
    exit_scale,
    out_grad,
):
    pipe = lax.axis_index("pipe")
    core = lax.axis_index("core")
    z = lax.axis_index("z")
    pipes = lax.axis_size("pipe")
    zs = lax.axis_size("z")
    block = z * 2 + core
    seg = segment_in[0]
    weight = layer_weight[0]
    gain = layer_gain[0]
    grad = out_grad[0]
    tokens, width = seg.shape
    slab = weight.shape[1]
    exits = exit_rows.shape[1]
    rows_all = pipes * exits
    vocab_part = head_weight.shape[0]
    half = vocab_part // 2
    padded = -(-(half + 6) // 128) * 128

    weight_other = swap(weight)
    head_mine = lax.dynamic_slice_in_dim(head_weight, core * half, half, 0)
    head_rest = lax.dynamic_slice_in_dim(head_weight, (1 - core) * half, half, 0)
    head_other = swap(head_rest)
    pad_rows = ((0, padded - half), (0, 0))
    head_mine = jnp.pad(head_mine, pad_rows)
    head_rest = jnp.pad(head_rest, pad_rows)
    head_other = jnp.pad(head_other, pad_rows)

    my_rows = exit_rows[pipe]
    pick = (my_rows[:, None] == jnp.arange(tokens, dtype=jnp.int32)[None, :]).astype(BF16)
    row_in = jnp.dot(pick, seg, preferred_element_type=F32)
    row_inv = lax.rsqrt(jnp.mean(row_in * row_in, axis=-1, keepdims=True) + EPSILON)
    row_unit = row_in * row_inv
    row_normed = (row_unit * gain).astype(BF16)
    row_update = rounded(jnp.dot(row_normed, weight, preferred_element_type=F32))
    row_block = lax.dynamic_slice_in_dim(row_in, block * slab, slab, 1)
    hidden = (row_block + row_update).astype(BF16)

    all_mine = spread(hidden, "pipe", pipes).reshape(rows_all, slab)
    all_other = swap(all_mine)
    gain_mine = lax.dynamic_slice_in_dim(final_gain, block * slab, slab, 0)
    gain_other = lax.dynamic_slice_in_dim(final_gain, (z * 2 + 1 - core) * slab, slab, 0)
    mine32 = all_mine.astype(F32)
    other32 = all_other.astype(F32)
    squares = jnp.sum(mine32 * mine32, axis=-1) + jnp.sum(other32 * other32, axis=-1)
    part = lax.dot_general(
        (mine32 * gain_mine).astype(BF16), head_mine, (((1,), (1,)), ((), ())), preferred_element_type=F32
    ) + lax.dot_general(
        (other32 * gain_other).astype(BF16), head_other, (((1,), (1,)), ((), ())), preferred_element_type=F32
    )
    column = lax.broadcasted_iota(jnp.int32, (1, padded), 1)
    for spot, piece in enumerate(split3(squares)):
        part = jnp.where(column == half + spot, piece[:, None], part)
    own = rows_all // zs
    parts = lax.all_to_all(part.astype(BF16).reshape(zs, own, padded), "z", 0, 0)
    sums = jnp.sum(parts.astype(F32), axis=0)
    own_inv = lax.rsqrt(jnp.sum(sums[:, half : half + 3], axis=-1, keepdims=True) / width + EPSILON)
    logits = sums * own_inv

    live_column = column < half
    index = z * own + jnp.arange(own, dtype=jnp.int32)
    section = index // exits
    target = exit_targets.reshape(-1)[index] - pipe * vocab_part - core * half
    row_weight = jnp.where(index % exits < exit_count[section], exit_scale[section], F32(0.0))[:, None]
    hit = (column == target[:, None]) & live_column
    top = jnp.max(jnp.where(live_column, logits, -jnp.inf), axis=-1)
    shifted = jnp.where(live_column, logits - top[:, None], -jnp.inf)
    expo = jnp.exp(shifted)
    total = jnp.sum(expo, axis=-1)
    along = jnp.sum(jnp.where(live_column, expo * shifted, 0.0), axis=-1)
    at_target = jnp.sum(jnp.where(hit, logits, 0.0), axis=-1)
    mine4 = jnp.stack([top, total, along, at_target])
    stats = jnp.concatenate([mine4, swap(mine4)])
    stats = spread(stats, "pipe", pipes).reshape(pipes * 2, 4, own)
    tops, totals, alongs, targets = [stats[:, i] for i in range(4)]
    row_top = jnp.max(tops, axis=0)
    lower = jnp.exp(tops - row_top)
    row_total = jnp.sum(totals * lower, axis=0)
    row_along = jnp.sum((alongs + (tops - row_top) * totals) * lower, axis=0) / row_total
    row_target = jnp.sum(targets, axis=0) - row_top
    back_mean = row_weight[:, 0] * (row_along - row_target) / width
    probs = jnp.exp(logits - row_top[:, None]) / row_total[:, None]
    dlogits = row_weight * (probs - hit.astype(F32))
    for spot, piece in enumerate(split3(own_inv[:, 0]) + split3(back_mean)):
        dlogits = jnp.where(column == half + spot, piece[:, None], dlogits)
    dl_mine = lax.all_gather(dlogits.astype(BF16), "z", axis=0, tiled=True)
    dl_other = swap(dl_mine)

    exit_part = jnp.dot(dl_mine, head_mine, preferred_element_type=F32) + jnp.dot(
        dl_other, head_rest, preferred_element_type=F32
    )
    extra = dl_mine[:, half : half + 6].astype(F32)
    exit_inv = jnp.sum(extra[:, :3], axis=-1, keepdims=True)
    exit_mean = jnp.sum(extra[:, 3:], axis=-1, keepdims=True)
    exit_normed = (mine32 * exit_inv * gain_mine).astype(BF16)
    over_rows = (((0,), (0,)), ((), ()))
    head_a = lax.dot_general(dl_mine, exit_normed, over_rows, preferred_element_type=F32).astype(BF16)[:half]
    head_b = lax.dot_general(dl_other, exit_normed, over_rows, preferred_element_type=F32).astype(BF16)[:half]
    head_grad = pair(head_a, head_b, core, 0)
    exit_grad = jnp.sum(lax.all_to_all(exit_part.reshape(pipes, exits, slab), "pipe", 0, 0), axis=0)
    my_inv = lax.dynamic_slice_in_dim(exit_inv, pipe * exits, exits, 0)
    my_mean = lax.dynamic_slice_in_dim(exit_mean, pipe * exits, exits, 0)
    exit_unit = hidden.astype(F32) * my_inv
    exit_back = (exit_grad * gain_mine - exit_unit * my_mean) * my_inv
    grad_slab = lax.dynamic_slice_in_dim(grad, block * slab, slab, 1)
    row_grad = jnp.dot(pick, grad_slab, preferred_element_type=F32) + exit_back
    row_rounded = row_grad.astype(BF16)

    inputs = seg.astype(F32)
    inv_rms = lax.rsqrt(jnp.mean(inputs * inputs, axis=-1, keepdims=True) + EPSILON)
    normed = (inputs * inv_rms * gain).astype(BF16)
    is_exit = jnp.any(pick > 0, axis=0)
    held = tokens // (zs * 2)

    def of_core(values):
        grouped = values.reshape((zs, 2, held) + values.shape[1:])
        return lax.dynamic_index_in_dim(grouped, core, 1, keepdims=False)

    grad_core = of_core(grad).reshape(zs * held, width)
    other_block = (z * 2 + 1 - core) * slab
    on_columns = (((1,), (1,)), ((), ()))
    main_part = lax.dot_general(
        lax.dynamic_slice_in_dim(grad_core, block * slab, slab, 1), weight, on_columns, preferred_element_type=F32
    ) + lax.dot_general(
        lax.dynamic_slice_in_dim(grad_core, other_block, slab, 1),
        weight_other,
        on_columns,
        preferred_element_type=F32,
    )
    main_grad = lax.psum_scatter(main_part, "z", scatter_dimension=0, tiled=True)
    first = block * held
    held_in = lax.dynamic_slice_in_dim(seg, first, held, 0).astype(F32)
    held_grad = lax.dynamic_slice_in_dim(grad, first, held, 0).astype(F32)
    held_exit = lax.dynamic_slice_in_dim(is_exit, first, held, 0)

    def layer_back(norm_grad, unit, inv, residual):
        unit_grad = norm_grad * gain
        centre = jnp.mean(unit_grad * unit, axis=-1, keepdims=True)
        return (residual + (unit_grad - unit * centre) * inv).astype(BF16)

    held_inv = lax.rsqrt(jnp.mean(held_in * held_in, axis=-1, keepdims=True) + EPSILON)
    held_unit = held_in * held_inv
    main_out = layer_back(main_grad, held_unit, held_inv, held_grad)
    gain_part = jnp.sum(jnp.where(held_exit[:, None], 0.0, main_grad * held_unit), axis=0)
    main_all = lax.all_gather(main_out, ("z", "core"), axis=0, tiled=True)

    put = pick.T
    slab_rounded = jnp.where(
        is_exit[:, None], jnp.dot(put, row_rounded, preferred_element_type=F32).astype(BF16), grad_slab
    )
    weight_grad = lax.dot_general(normed, slab_rounded, over_rows, preferred_element_type=F32).astype(BF16)
    core_rows = exits // 2
    share = core_rows // zs
    row_other = swap(lax.dynamic_slice_in_dim(row_grad, (1 - core) * core_rows, core_rows, 0))
    row_mine = lax.dynamic_slice_in_dim(row_grad, core * core_rows, core_rows, 0)
    row_part = lax.dot_general(
        row_mine.astype(BF16), weight, on_columns, preferred_element_type=F32
    ) + lax.dot_general(row_other.astype(BF16), weight_other, on_columns, preferred_element_type=F32)
    send = jnp.concatenate([row_part, pair(row_mine, row_other, core, 1)], axis=1)
    got = lax.all_to_all(send.reshape(zs, share, width + 2 * slab), "z", 0, 0)
    norm_grad = jnp.sum(got[:, :, :width], axis=0)
    residual = got[:, :, width:].transpose(1, 0, 2).reshape(share, width)
    at = core * core_rows + z * share
    share_unit = lax.dynamic_slice_in_dim(row_unit, at, share, 0)
    share_inv = lax.dynamic_slice_in_dim(row_inv, at, share, 0)
    share_out = layer_back(norm_grad, share_unit, share_inv, residual)
    gain_part = gain_part + jnp.sum(norm_grad * share_unit, axis=0)
    gain_first = rounded(gain_part)
    gain_rest = gain_part - gain_first
    last = jnp.concatenate([share_out, gain_first.astype(BF16)[None], gain_rest.astype(BF16)[None]])
    last = spread(last, ("z", "core"), zs * 2)
    gain_grad = jnp.sum(last[:, share:].astype(F32), axis=(0, 1))
    row_out = last[:, :share].reshape(zs, 2, share, width).transpose(1, 0, 2, 3).reshape(exits, width)
    input_grad = jnp.where(
        is_exit[:, None], jnp.dot(put, row_out, preferred_element_type=F32).astype(BF16), main_all
    )
    return (input_grad[None], weight_grad[None], gain_grad[None], head_grad)


def solution(mesh):
    pipes, tensors = mesh.devices.shape
    fine = Mesh(mesh.devices.reshape(pipes, tensors // 2, 2), ("pipe", "z", "core"))
    tensor = ("z", "core")
    in_specs = (
        P("pipe", None, None),
        P("pipe", None, tensor),
        P("pipe", None),
        P(),
        P("pipe", tensor),
        P(),
        P(),
        P(),
        P(),
        P("pipe", None, None),
    )
    out_specs = (
        P("pipe", None, None),
        P("pipe", None, tensor),
        P("pipe", None),
        P("pipe", tensor),
    )
    return jax.shard_map(local, mesh=fine, in_specs=in_specs, out_specs=out_specs, check_vma=False)
```

```python
import jax
import jax.numpy as jnp
from jax import lax
from jax.sharding import Mesh, PartitionSpec as P

F32 = jnp.float32
BF16 = jnp.bfloat16
EPSILON = 1e-05


def rounded(values):
    return lax.reduce_precision(values, 8, 7)


def split3(values):
    first = rounded(values)
    rest = values - first
    second = rounded(rest)
    return [first, second, rest - second]


def spread(values, axis, count):
    return lax.all_to_all(jnp.broadcast_to(values[None], (count,) + values.shape), axis, 0, 0)


def swap(values):
    return lax.ppermute(values, "core", [(0, 1), (1, 0)])


def pair(mine, other, core, axis):
    first = jnp.where(core == 0, mine, other)
    second = jnp.where(core == 0, other, mine)
    return jnp.concatenate([first, second], axis=axis)


def local(
    segment_in,
    layer_weight,
    layer_gain,
    final_gain,
    head_weight,
    exit_rows,
    exit_count,
    exit_targets,
    exit_scale,
    out_grad,
):
    pipe = lax.axis_index("pipe")
    core = lax.axis_index("core")
    z = lax.axis_index("z")
    pipes = lax.axis_size("pipe")
    zs = lax.axis_size("z")
    block = z * 2 + core
    seg = segment_in[0]
    weight = layer_weight[0]
    gain = layer_gain[0]
    grad = out_grad[0]
    tokens, width = seg.shape
    slab = weight.shape[1]
    exits = exit_rows.shape[1]
    rows_all = pipes * exits
    vocab_part = head_weight.shape[0]
    half = vocab_part // 2
    padded = -(-(half + 6) // 128) * 128

    weight_other = swap(weight)
    head_mine = lax.dynamic_slice_in_dim(head_weight, core * half, half, 0)
    head_rest = lax.dynamic_slice_in_dim(head_weight, (1 - core) * half, half, 0)
    head_other = swap(head_rest)
    pad_rows = ((0, padded - half), (0, 0))
    head_mine = jnp.pad(head_mine, pad_rows)
    head_rest = jnp.pad(head_rest, pad_rows)
    head_other = jnp.pad(head_other, pad_rows)

    my_rows = exit_rows[pipe]
    pick = (my_rows[:, None] == jnp.arange(tokens, dtype=jnp.int32)[None, :]).astype(BF16)
    row_in = jnp.dot(pick, seg, preferred_element_type=F32)
    row_inv = lax.rsqrt(jnp.mean(row_in * row_in, axis=-1, keepdims=True) + EPSILON)
    row_unit = row_in * row_inv
    row_normed = (row_unit * gain).astype(BF16)
    row_update = rounded(jnp.dot(row_normed, weight, preferred_element_type=F32))
    row_block = lax.dynamic_slice_in_dim(row_in, block * slab, slab, 1)
    hidden = (row_block + row_update).astype(BF16)

    all_mine = spread(hidden, "pipe", pipes).reshape(rows_all, slab)

    inputs = seg.astype(F32)
    inv_rms = lax.rsqrt(jnp.mean(inputs * inputs, axis=-1, keepdims=True) + EPSILON)
    normed = (inputs * inv_rms * gain).astype(BF16)
    is_exit = jnp.any(pick > 0, axis=0)
    held = tokens // (zs * 2)

    def of_core(values):
        grouped = values.reshape((zs, 2, held) + values.shape[1:])
        return lax.dynamic_index_in_dim(grouped, core, 1, keepdims=False)

    grad_core = of_core(grad).reshape(zs * held, width)
    other_block = (z * 2 + 1 - core) * slab
    on_columns = (((1,), (1,)), ((), ()))
    main_part = lax.dot_general(
        lax.dynamic_slice_in_dim(grad_core, block * slab, slab, 1), weight, on_columns, preferred_element_type=F32
    ) + lax.dot_general(
        lax.dynamic_slice_in_dim(grad_core, other_block, slab, 1),
        weight_other,
        on_columns,
        preferred_element_type=F32,
    )
    all_mine, main_part = lax.optimization_barrier((all_mine, main_part))
    main_grad = lax.psum_scatter(main_part, "z", scatter_dimension=0, tiled=True)
    first = block * held
    held_in = lax.dynamic_slice_in_dim(seg, first, held, 0).astype(F32)
    held_grad = lax.dynamic_slice_in_dim(grad, first, held, 0).astype(F32)
    held_exit = lax.dynamic_slice_in_dim(is_exit, first, held, 0)

    def layer_back(norm_grad, unit, inv, residual):
        unit_grad = norm_grad * gain
        centre = jnp.mean(unit_grad * unit, axis=-1, keepdims=True)
        return (residual + (unit_grad - unit * centre) * inv).astype(BF16)

    held_inv = lax.rsqrt(jnp.mean(held_in * held_in, axis=-1, keepdims=True) + EPSILON)
    held_unit = held_in * held_inv
    main_out = layer_back(main_grad, held_unit, held_inv, held_grad)
    gain_part = jnp.sum(jnp.where(held_exit[:, None], 0.0, main_grad * held_unit), axis=0)
    main_all = lax.all_gather(main_out, ("z", "core"), axis=0, tiled=True)


    all_other = swap(all_mine)
    gain_mine = lax.dynamic_slice_in_dim(final_gain, block * slab, slab, 0)
    gain_other = lax.dynamic_slice_in_dim(final_gain, (z * 2 + 1 - core) * slab, slab, 0)
    mine32 = all_mine.astype(F32)
    other32 = all_other.astype(F32)
    squares = jnp.sum(mine32 * mine32, axis=-1) + jnp.sum(other32 * other32, axis=-1)
    part = lax.dot_general(
        (mine32 * gain_mine).astype(BF16), head_mine, (((1,), (1,)), ((), ())), preferred_element_type=F32
    ) + lax.dot_general(
        (other32 * gain_other).astype(BF16), head_other, (((1,), (1,)), ((), ())), preferred_element_type=F32
    )
    column = lax.broadcasted_iota(jnp.int32, (1, padded), 1)
    for spot, piece in enumerate(split3(squares)):
        part = jnp.where(column == half + spot, piece[:, None], part)
    own = rows_all // zs
    parts = lax.all_to_all(part.astype(BF16).reshape(zs, own, padded), "z", 0, 0)
    sums = jnp.sum(parts.astype(F32), axis=0)
    own_inv = lax.rsqrt(jnp.sum(sums[:, half : half + 3], axis=-1, keepdims=True) / width + EPSILON)
    logits = sums * own_inv

    live_column = column < half
    sections = own // exits
    owned = z * sections
    slot = jnp.arange(exits, dtype=jnp.int32)[None, :]
    counts = lax.dynamic_slice_in_dim(exit_count, owned, sections, 0)[:, None]
    scales = lax.dynamic_slice_in_dim(exit_scale, owned, sections, 0)[:, None]
    row_weight = jnp.where(slot < counts, scales, F32(0.0)).reshape(own)
    all_targets = exit_targets.reshape(rows_all)
    target = lax.dynamic_slice_in_dim(all_targets, z * own, own, 0) - pipe * vocab_part - core * half
    hit = (column == target[:, None]) & live_column
    top = jnp.max(jnp.where(live_column, logits, -jnp.inf), axis=-1)
    shifted = jnp.where(live_column, logits - top[:, None], -jnp.inf)
    expo = jnp.exp(shifted)
    total = jnp.sum(expo, axis=-1)
    along = jnp.sum(jnp.where(live_column, expo * shifted, 0.0), axis=-1)
    at_target = jnp.sum(jnp.where(hit, logits, 0.0), axis=-1)
    ex_mine = spread(expo.astype(BF16), "z", zs).reshape(rows_all, padded)
    ex_other = swap(ex_mine)
    mine4 = jnp.stack([top, total, along, at_target])
    other4 = swap(mine4)
    stats = spread(jnp.concatenate([mine4, other4]), "pipe", pipes).reshape(pipes * 2, 4, own)
    tops, totals, alongs, targets = [stats[:, i] for i in range(4)]
    row_top = jnp.max(tops, axis=0)
    lower = jnp.exp(tops - row_top)
    row_total = jnp.sum(totals * lower, axis=0)
    row_along = jnp.sum((alongs + (tops - row_top) * totals) * lower, axis=0) / row_total
    row_target = jnp.sum(targets, axis=0) - row_top
    back_mean = row_weight * (row_along - row_target) / width
    known = jnp.stack(
        [
            row_weight * (jnp.exp(top - row_top) / row_total),
            row_weight * (jnp.exp(other4[0] - row_top) / row_total),
            row_weight * (jnp.exp(row_target) / row_total - 1.0),
            back_mean,
            own_inv[:, 0],
        ]
    )
    known = spread(known, "z", zs).transpose(1, 0, 2).reshape(5, rows_all, 1)
    factor_mine, factor_other, target_grad, exit_mean, exit_inv = [known[i] for i in range(5)]

    def logit_grad(expo, factor, which):
        spot = all_targets[:, None] - pipe * vocab_part - which * half
        return jnp.where((column == spot) & live_column, target_grad, expo.astype(F32) * factor).astype(BF16)

    ex_mine, main_out = lax.optimization_barrier((ex_mine, main_out))
    dl_mine = logit_grad(ex_mine, factor_mine, core)
    dl_other = logit_grad(ex_other, factor_other, 1 - core)

    exit_part = jnp.dot(dl_mine, head_mine, preferred_element_type=F32) + jnp.dot(
        dl_other, head_rest, preferred_element_type=F32
    )
    exit_normed = (mine32 * exit_inv * gain_mine).astype(BF16)
    over_rows = (((0,), (0,)), ((), ()))
    head_a = lax.dot_general(dl_mine, exit_normed, over_rows, preferred_element_type=F32).astype(BF16)[:half]
    head_b = lax.dot_general(dl_other, exit_normed, over_rows, preferred_element_type=F32).astype(BF16)[:half]
    head_grad = pair(head_a, head_b, core, 0)
    exit_grad = jnp.sum(lax.all_to_all(exit_part.reshape(pipes, exits, slab), "pipe", 0, 0), axis=0)
    my_inv = lax.dynamic_slice_in_dim(exit_inv, pipe * exits, exits, 0)
    my_mean = lax.dynamic_slice_in_dim(exit_mean, pipe * exits, exits, 0)
    exit_unit = hidden.astype(F32) * my_inv
    exit_back = (exit_grad * gain_mine - exit_unit * my_mean) * my_inv
    grad_slab = lax.dynamic_slice_in_dim(grad, block * slab, slab, 1)
    row_grad = jnp.dot(pick, grad_slab, preferred_element_type=F32) + exit_back
    row_rounded = row_grad.astype(BF16)

    put = pick.T
    slab_rounded = jnp.where(
        is_exit[:, None], jnp.dot(put, row_rounded, preferred_element_type=F32).astype(BF16), grad_slab
    )
    weight_grad = lax.dot_general(normed, slab_rounded, over_rows, preferred_element_type=F32).astype(BF16)
    core_rows = exits // 2
    share = core_rows // zs
    row_other = swap(lax.dynamic_slice_in_dim(row_grad, (1 - core) * core_rows, core_rows, 0))
    row_mine = lax.dynamic_slice_in_dim(row_grad, core * core_rows, core_rows, 0)
    row_part = lax.dot_general(
        row_mine.astype(BF16), weight, on_columns, preferred_element_type=F32
    ) + lax.dot_general(row_other.astype(BF16), weight_other, on_columns, preferred_element_type=F32)
    core_unit = lax.dynamic_slice_in_dim(row_unit, core * core_rows, core_rows, 0)
    gain_part = gain_part + jnp.sum(row_part * core_unit, axis=0)
    piece = slab * 2 // share
    send = jnp.concatenate(
        [
            row_part.reshape(zs, share, width),
            pair(row_mine, row_other, core, 1).reshape(zs, share, 2 * slab),
            gain_part.reshape(zs, share, piece),
        ],
        axis=2,
    )
    got = lax.all_to_all(send, "z", 0, 0)
    summed = jnp.sum(got, axis=0)
    norm_grad = summed[:, :width]
    residual = got[:, :, width : width + 2 * slab].transpose(1, 0, 2).reshape(share, width)
    at = core * core_rows + z * share
    share_unit = lax.dynamic_slice_in_dim(row_unit, at, share, 0)
    share_inv = lax.dynamic_slice_in_dim(row_inv, at, share, 0)
    share_out = layer_back(norm_grad, share_unit, share_inv, residual)
    gains = [values.astype(BF16) for values in split3(summed[:, width + 2 * slab :])]
    last = spread(jnp.concatenate([share_out] + gains, axis=1), "z", zs)
    last_other = swap(last)
    gain_grad = jnp.sum(
        (last[:, :, width:].astype(F32) + last_other[:, :, width:].astype(F32)).reshape(zs, share, 3, piece), axis=2
    ).reshape(width)
    row_out = pair(last, last_other, core, 0)[:, :, :width].reshape(exits, width)
    input_grad = jnp.where(
        is_exit[:, None], jnp.dot(put, row_out, preferred_element_type=F32).astype(BF16), main_all
    )
    return (input_grad[None], weight_grad[None], gain_grad[None], head_grad)


def solution(mesh):
    pipes, tensors = mesh.devices.shape
    fine = Mesh(mesh.devices.reshape(pipes, tensors // 2, 2), ("pipe", "z", "core"))
    tensor = ("z", "core")
    in_specs = (
        P("pipe", None, None),
        P("pipe", None, tensor),
        P("pipe", None),
        P(),
        P("pipe", tensor),
        P(),
        P(),
        P(),
        P(),
        P("pipe", None, None),
    )
    out_specs = (
        P("pipe", None, None),
        P("pipe", None, tensor),
        P("pipe", None),
        P("pipe", tensor),
    )
    return jax.shard_map(local, mesh=fine, in_specs=in_specs, out_specs=out_specs, check_vma=False)
```

```python
import functools

import jax
import jax.numpy as jnp
from jax import lax
from jax.experimental import pallas as pl
from jax.experimental.pallas import tpu as pltpu
from jax.sharding import Mesh, PartitionSpec as P

F32 = jnp.float32
BF16 = jnp.bfloat16
EPSILON = 1e-05
VMEM = 32 * 1024 * 1024


def rounded(values):
    return lax.reduce_precision(values, 8, 7)


def split3(values):
    first = rounded(values)
    rest = values - first
    second = rounded(rest)
    return [first, second, rest - second]


def spread(values, axis, count):
    return lax.all_to_all(jnp.broadcast_to(values[None], (count,) + values.shape), axis, 0, 0)


def swap(values):
    return lax.ppermute(values, "core", [(0, 1), (1, 0)])


def from_back(piece, count):
    return [piece(0)] + [
        lax.ppermute(piece(k), "z", [(i, (i + k) % count) for i in range(count)]) for k in range(1, count)
    ]


def pair(mine, other, core, axis):
    first = jnp.where(core == 0, mine, other)
    second = jnp.where(core == 0, other, mine)
    return jnp.concatenate([first, second], axis=axis)


def kernel_call(body, out, *operands):
    return pl.pallas_call(
        body,
        out_shape=out,
        in_specs=[
            pl.BlockSpec(memory_space=pltpu.SMEM if i == 0 else pltpu.VMEM) for i in range(len(operands))
        ],
        out_specs=jax.tree.map(lambda _: pl.BlockSpec(memory_space=pltpu.VMEM), out),
        compiler_params=pltpu.CompilerParams(vmem_limit_bytes=VMEM),
    )(*operands)


def shape(dims, dtype):
    return jax.ShapeDtypeStruct(dims, dtype)


def logits_kernel(place, rows, gains, *refs):
    heads, mine, other = refs[:-2], refs[-2], refs[-1]
    z, core = place[0], place[1]
    zs = len(heads)
    total = mine.shape[0] * 2
    part = jnp.zeros((total, heads[0].shape[0]), F32)
    squares = jnp.zeros((total, 1), F32)
    for k in range(zs):
        at = lax.rem(z - k + zs, zs)
        row = rows[:, at].reshape(total, rows.shape[3]).astype(F32)
        squares += jnp.sum(row * row, axis=-1, keepdims=True)
        part += lax.dot_general(
            (row * gains[pl.ds(at, 1), :]).astype(BF16),
            heads[k][...],
            (((1,), (1,)), ((), ())),
            preferred_element_type=F32,
        )
    whole = jnp.concatenate([part, jnp.broadcast_to(squares, (total, 128))], axis=1)
    low, high = whole[: total // 2], whole[total // 2 :]
    mine[...] = jnp.where(core == 0, low, high)
    other[...] = jnp.where(core == 0, high, low)


def softmax_kernel(width, vocab, place, mine, other, targets, expo_out, stats):
    z, start = place[0], place[2]
    columns = expo_out.shape[1]
    whole = mine[...] + other[...]
    inv = lax.rsqrt(whole[:, columns : columns + 1] / width + EPSILON)
    logits = whole[:, :columns] * inv
    column = lax.broadcasted_iota(jnp.int32, logits.shape, 1) + z * columns
    live = column < vocab
    top = jnp.max(jnp.where(live, logits, -jnp.inf), axis=-1, keepdims=True)
    shifted = jnp.where(live, logits - top, -jnp.inf)
    expo = jnp.exp(shifted)
    expo_out[...] = expo.astype(BF16)
    hit = live & (column == targets[...] - start)
    values = [
        top,
        jnp.sum(expo, axis=-1, keepdims=True),
        jnp.sum(jnp.where(live, expo * shifted, 0.0), axis=-1, keepdims=True),
        jnp.sum(jnp.where(hit, logits, 0.0), axis=-1, keepdims=True),
        inv,
    ]
    lane = lax.broadcasted_iota(jnp.int32, (logits.shape[0], 128), 1)
    table = jnp.zeros(lane.shape, F32)
    for i, value in enumerate(values):
        table = jnp.where(lane == i, value, table)
    stats[...] = table.T[: stats.shape[0]]


def merged(stats):
    tops, totals, alongs, hits = [stats[:, i] for i in range(4)]
    top = jnp.max(tops, axis=0, keepdims=True)
    lower = jnp.exp(tops - top)
    total = jnp.sum(totals * lower, axis=0, keepdims=True)
    along = jnp.sum((alongs + (tops - top) * totals) * lower, axis=0, keepdims=True)
    return top, total, along, jnp.sum(hits, axis=0, keepdims=True)


def merge_kernel(place, stats, out):
    values = merged(stats[...])
    out[...] = jnp.concatenate(list(values) + [jnp.zeros((out.shape[0] - 4, out.shape[1]), F32)])


def finish_kernel(width, place, stats, pieces, weights, known):
    top, total, along, hits = merged(stats[...])
    weight = weights[...]
    own = pieces[...]
    factors = weight * (jnp.exp(own[:, 0] - top) / total)
    target = weight * (jnp.exp(hits - top) / total - 1.0)
    mean = weight * (along / total - (hits - top)) / width
    rest = known.shape[0] - own.shape[0] - 3
    known[...] = jnp.concatenate(
        [factors, target, mean, own[0, 4:5], jnp.zeros((rest, known.shape[1]), F32)]
    )


def exit_kernel(zs, vocab, place, head, known_mine, known_other, targets_mine, targets_other, *refs):
    pieces, part, dlogits = refs[:-2], refs[-2], refs[-1]
    z, core, start = place[0], place[1], place[2]
    count, columns = pieces[0].shape
    for side, known, targets in ((0, known_mine, targets_mine), (1, known_other, targets_other)):
        table = known[...].T
        lane = lax.broadcasted_iota(jnp.int32, table.shape, 1)
        target_grad = table[:, zs : zs + 1]
        spot = targets[...] - start
        rows = pl.ds(pl.multiple_of(jnp.where(side == 0, core, 1 - core) * count, count), count)
        total = jnp.zeros((count, head.shape[2]), F32)
        for k in range(zs):
            at = lax.rem(z - k + zs, zs)
            factor = jnp.sum(jnp.where(lane == at, table, 0.0), axis=-1, keepdims=True)
            column = lax.broadcasted_iota(jnp.int32, (count, columns), 1) + at * columns
            hit = (column == spot) & (column < vocab)
            grad = jnp.where(hit, target_grad, pieces[side * zs + k][...].astype(F32) * factor).astype(BF16)
            dlogits[at, rows, :] = grad
            total += jnp.dot(grad, head[at], preferred_element_type=F32)
        part[rows, :] = total


def head_kernel(zs, place, rows, gain, known_mine, known_other, dlogits, out):
    z, core = place[0], place[1]
    count = dlogits.shape[1]
    columns = dlogits.shape[2]
    mine = known_mine[...].T[:, zs + 2 : zs + 3]
    other = known_other[...].T[:, zs + 2 : zs + 3]
    inv = jnp.concatenate([jnp.where(core == 0, mine, other), jnp.where(core == 0, other, mine)])
    row = rows[:, z].reshape(count, rows.shape[3]).astype(F32)
    normed = (row * inv * gain[...]).astype(BF16)
    for at in range(zs):
        held = min(columns, out.shape[0] - at * columns)
        piece = lax.dot_general(dlogits[at], normed, (((0,), (0,)), ((), ())), preferred_element_type=F32)
        out[at * columns : at * columns + held, :] = piece[:held].astype(BF16)


def local(
    segment_in,
    layer_weight,
    layer_gain,
    final_gain,
    head_weight,
    exit_rows,
    exit_count,
    exit_targets,
    exit_scale,
    out_grad,
):
    pipe = lax.axis_index("pipe")
    core = lax.axis_index("core")
    z = lax.axis_index("z")
    pipes = lax.axis_size("pipe")
    zs = lax.axis_size("z")
    block = z * 2 + core
    seg = segment_in[0]
    weight = layer_weight[0]
    gain = layer_gain[0]
    grad = out_grad[0]
    tokens, width = seg.shape
    slab = weight.shape[1]
    exits = exit_rows.shape[1]
    rows_all = pipes * exits
    vocab_part = head_weight.shape[0]
    columns = -(-vocab_part // (zs * 128)) * 128
    place = jnp.stack([z, core, pipe * vocab_part]).astype(jnp.int32)

    weight_other = swap(weight)
    head_pieces = jnp.pad(head_weight, ((0, zs * columns - vocab_part), (0, 0))).reshape(zs, columns, slab)
    heads = from_back(lambda k: lax.dynamic_index_in_dim(head_pieces, (z + k) % zs, 0, keepdims=False), zs)

    my_rows = exit_rows[pipe]
    pick = (my_rows[:, None] == jnp.arange(tokens, dtype=jnp.int32)[None, :]).astype(BF16)
    row_in = jnp.dot(pick, seg, preferred_element_type=F32)
    row_inv = lax.rsqrt(jnp.mean(row_in * row_in, axis=-1, keepdims=True) + EPSILON)
    row_unit = row_in * row_inv
    row_normed = (row_unit * gain).astype(BF16)
    row_update = rounded(jnp.dot(row_normed, weight, preferred_element_type=F32))
    row_block = lax.dynamic_slice_in_dim(row_in, block * slab, slab, 1)
    hidden = (row_block + row_update).astype(BF16)

    inputs = seg.astype(F32)
    inv_rms = lax.rsqrt(jnp.mean(inputs * inputs, axis=-1, keepdims=True) + EPSILON)
    normed = (inputs * inv_rms * gain).astype(BF16)
    is_exit = jnp.any(pick > 0, axis=0)
    grad_slab = lax.dynamic_slice_in_dim(grad, block * slab, slab, 1)
    held = tokens // (zs * 2)

    def of_core(values):
        grouped = values.reshape((zs, 2, held) + values.shape[1:])
        return lax.dynamic_index_in_dim(grouped, core, 1, keepdims=False)

    grad_core = of_core(grad).reshape(zs * held, width)
    other_block = (z * 2 + 1 - core) * slab
    on_columns = (((1,), (1,)), ((), ()))
    over_rows = (((0,), (0,)), ((), ()))
    main_part = lax.dot_general(
        lax.dynamic_slice_in_dim(grad_core, block * slab, slab, 1), weight, on_columns, preferred_element_type=F32
    ) + lax.dot_general(
        lax.dynamic_slice_in_dim(grad_core, other_block, slab, 1),
        weight_other,
        on_columns,
        preferred_element_type=F32,
    )
    column_rows = spread(hidden, "z", zs)
    column_rows, main_part = lax.optimization_barrier((column_rows, main_part))
    main_grad = lax.psum_scatter(main_part.astype(BF16), "z", scatter_dimension=0, tiled=True).astype(F32)
    first = block * held
    held_in = lax.dynamic_slice_in_dim(seg, first, held, 0).astype(F32)
    held_grad = lax.dynamic_slice_in_dim(grad, first, held, 0).astype(F32)
    held_exit = lax.dynamic_slice_in_dim(is_exit, first, held, 0)

    def layer_back(norm_grad, unit, inv, residual):
        unit_grad = norm_grad * gain
        centre = jnp.mean(unit_grad * unit, axis=-1, keepdims=True)
        return (residual + (unit_grad - unit * centre) * inv).astype(BF16)

    held_inv = lax.rsqrt(jnp.mean(held_in * held_in, axis=-1, keepdims=True) + EPSILON)
    held_unit = held_in * held_inv
    main_out = layer_back(main_grad, held_unit, held_inv, held_grad)
    gain_part = jnp.sum(jnp.where(held_exit[:, None], 0.0, main_grad * held_unit), axis=0)


    all_hidden = spread(column_rows, "pipe", pipes)
    gains = lax.dynamic_index_in_dim(final_gain.reshape(zs, 2, slab), core, 1, keepdims=False)
    own = rows_all // 2
    mine, other = kernel_call(
        logits_kernel, [shape((own, columns + 128), F32)] * 2, place, all_hidden, gains, *heads
    )

    all_targets = exit_targets.reshape(2, own, 1)
    targets_mine = lax.dynamic_index_in_dim(all_targets, core, 0, keepdims=False)
    targets_other = lax.dynamic_index_in_dim(all_targets, 1 - core, 0, keepdims=False)
    slot = jnp.arange(exits, dtype=jnp.int32)[None, :]
    weights = jnp.where(slot < exit_count[:, None], exit_scale[:, None], F32(0.0)).reshape(2, 1, own)
    weights = lax.dynamic_index_in_dim(weights, core, 0, keepdims=False)
    expo, stats = kernel_call(
        functools.partial(softmax_kernel, width, vocab_part),
        [shape((own, columns), BF16), shape((8, own), F32)],
        place,
        mine,
        swap(other),
        targets_mine,
    )
    ex_mine = from_back(lambda k: expo, zs)
    ex_other = [swap(piece) for piece in ex_mine]
    pieces = spread(stats, "z", zs)
    merged_stats = kernel_call(merge_kernel, shape((8, own), F32), place, pieces)
    known_mine = kernel_call(
        functools.partial(finish_kernel, width),
        shape((16, own), F32),
        place,
        spread(merged_stats, "pipe", pipes),
        pieces,
        weights,
    )
    known_other = swap(known_mine)

    exit_part, dlogits = kernel_call(
        functools.partial(exit_kernel, zs, vocab_part),
        [shape((rows_all, slab), F32), shape((zs, rows_all, columns), BF16)],
        place,
        head_pieces,
        known_mine,
        known_other,
        targets_mine,
        targets_other,
        *ex_mine,
        *ex_other,
    )
    exit_part, main_out = lax.optimization_barrier((exit_part, main_out))
    main_all = lax.all_gather(main_out, ("z", "core"), axis=0, tiled=True)
    gain_mine = lax.dynamic_slice_in_dim(final_gain, block * slab, slab, 0)
    head_grad = kernel_call(
        functools.partial(head_kernel, zs),
        shape((vocab_part, slab), BF16),
        place,
        all_hidden,
        gain_mine[None],
        known_mine,
        known_other,
        dlogits,
    )
    exit_grad = jnp.sum(lax.all_to_all(exit_part.reshape(pipes, exits, slab), "pipe", 0, 0), axis=0)
    known = pair(known_mine[zs + 1 : zs + 3], known_other[zs + 1 : zs + 3], core, 1)
    my_known = lax.dynamic_slice_in_dim(known, pipe * exits, exits, 1)
    my_mean = my_known[0][:, None]
    my_inv = my_known[1][:, None]
    exit_unit = hidden.astype(F32) * my_inv
    exit_back = (exit_grad * gain_mine - exit_unit * my_mean) * my_inv
    row_grad = jnp.dot(pick, grad_slab, preferred_element_type=F32) + exit_back
    row_rounded = row_grad.astype(BF16)

    put = pick.T
    slab_rounded = jnp.where(
        is_exit[:, None], jnp.dot(put, row_rounded, preferred_element_type=F32).astype(BF16), grad_slab
    )
    weight_grad = lax.dot_general(normed, slab_rounded, over_rows, preferred_element_type=F32).astype(BF16)
    core_rows = exits // 2
    share = core_rows // zs
    row_other = swap(lax.dynamic_slice_in_dim(row_grad, (1 - core) * core_rows, core_rows, 0))
    row_mine = lax.dynamic_slice_in_dim(row_grad, core * core_rows, core_rows, 0)
    row_part = lax.dot_general(
        row_mine.astype(BF16), weight, on_columns, preferred_element_type=F32
    ) + lax.dot_general(row_other.astype(BF16), weight_other, on_columns, preferred_element_type=F32)
    core_unit = lax.dynamic_slice_in_dim(row_unit, core * core_rows, core_rows, 0)
    gain_part = gain_part + jnp.sum(row_part * core_unit, axis=0)
    piece = slab * 2 // share
    send = jnp.concatenate(
        [
            row_part.reshape(zs, share, width),
            pair(row_mine, row_other, core, 1).reshape(zs, share, 2 * slab),
            gain_part.reshape(zs, share, piece),
        ],
        axis=2,
    )
    got = lax.all_to_all(send, "z", 0, 0)
    summed = jnp.sum(got, axis=0)
    norm_grad = summed[:, :width]
    residual = got[:, :, width : width + 2 * slab].transpose(1, 0, 2).reshape(share, width)
    at = core * core_rows + z * share
    share_unit = lax.dynamic_slice_in_dim(row_unit, at, share, 0)
    share_inv = lax.dynamic_slice_in_dim(row_inv, at, share, 0)
    share_out = layer_back(norm_grad, share_unit, share_inv, residual)
    gain_parts = [values.astype(BF16) for values in split3(summed[:, width + 2 * slab :])]
    last = spread(jnp.concatenate([share_out] + gain_parts, axis=1), "z", zs)
    last_other = swap(last)
    gain_grad = jnp.sum(
        (last[:, :, width:].astype(F32) + last_other[:, :, width:].astype(F32)).reshape(zs, share, 3, piece), axis=2
    ).reshape(width)
    row_out = pair(last, last_other, core, 0)[:, :, :width].reshape(exits, width)
    input_grad = jnp.where(
        is_exit[:, None], jnp.dot(put, row_out, preferred_element_type=F32).astype(BF16), main_all
    )
    return (input_grad[None], weight_grad[None], gain_grad[None], head_grad)


def solution(mesh):
    pipes, tensors = mesh.devices.shape
    fine = Mesh(mesh.devices.reshape(pipes, tensors // 2, 2), ("pipe", "z", "core"))
    tensor = ("z", "core")
    in_specs = (
        P("pipe", None, None),
        P("pipe", None, tensor),
        P("pipe", None),
        P(),
        P("pipe", tensor),
        P(),
        P(),
        P(),
        P(),
        P("pipe", None, None),
    )
    out_specs = (
        P("pipe", None, None),
        P("pipe", None, tensor),
        P("pipe", None),
        P("pipe", tensor),
    )
    return jax.shard_map(local, mesh=fine, in_specs=in_specs, out_specs=out_specs, check_vma=False)
```

```python
import functools

import jax
import jax.numpy as jnp
from jax import lax
from jax.experimental import pallas as pl
from jax.experimental.pallas import tpu as pltpu
from jax.sharding import Mesh, PartitionSpec as P

F32 = jnp.float32
BF16 = jnp.bfloat16
EPSILON = 1e-05
VMEM = 32 * 1024 * 1024


def rounded(values):
    return lax.reduce_precision(values, 8, 7)


def split3(values):
    first = rounded(values)
    rest = values - first
    second = rounded(rest)
    return [first, second, rest - second]


def spread(values, axis, count):
    return lax.all_to_all(jnp.broadcast_to(values[None], (count,) + values.shape), axis, 0, 0)


def swap(values):
    return lax.ppermute(values, "core", [(0, 1), (1, 0)])


def from_back(piece, count):
    return [piece(0)] + [
        lax.ppermute(piece(k), "z", [(i, (i + k) % count) for i in range(count)]) for k in range(1, count)
    ]


def pair(mine, other, core, axis):
    first = jnp.where(core == 0, mine, other)
    second = jnp.where(core == 0, other, mine)
    return jnp.concatenate([first, second], axis=axis)


def kernel_call(body, out, *operands):
    return pl.pallas_call(
        body,
        out_shape=out,
        in_specs=[
            pl.BlockSpec(memory_space=pltpu.SMEM if i == 0 else pltpu.VMEM) for i in range(len(operands))
        ],
        out_specs=jax.tree.map(lambda _: pl.BlockSpec(memory_space=pltpu.VMEM), out),
        compiler_params=pltpu.CompilerParams(vmem_limit_bytes=VMEM),
    )(*operands)


def shape(dims, dtype):
    return jax.ShapeDtypeStruct(dims, dtype)


def logits_kernel(place, rows, gains, *refs):
    heads, mine, other = refs[:-2], refs[-2], refs[-1]
    z, core = place[0], place[1]
    zs = len(heads)
    total = mine.shape[0] * 2
    part = jnp.zeros((total, heads[0].shape[0]), F32)
    squares = jnp.zeros((total, 1), F32)
    for k in range(zs):
        at = lax.rem(z - k + zs, zs)
        row = rows[:, at].reshape(total, rows.shape[3]).astype(F32)
        squares += jnp.sum(row * row, axis=-1, keepdims=True)
        part += lax.dot_general(
            (row * gains[pl.ds(at, 1), :]).astype(BF16),
            heads[k][...],
            (((1,), (1,)), ((), ())),
            preferred_element_type=F32,
        )
    whole = jnp.concatenate([part, jnp.broadcast_to(squares, (total, 128))], axis=1)
    low, high = whole[: total // 2], whole[total // 2 :]
    mine[...] = jnp.where(core == 0, low, high)
    other[...] = jnp.where(core == 0, high, low)


def softmax_kernel(width, vocab, place, mine, other, targets, expo_out, stats):
    z, start = place[0], place[2]
    columns = expo_out.shape[1]
    whole = mine[...] + other[...]
    inv = lax.rsqrt(whole[:, columns : columns + 1] / width + EPSILON)
    logits = whole[:, :columns] * inv
    column = lax.broadcasted_iota(jnp.int32, logits.shape, 1) + z * columns
    live = column < vocab
    top = jnp.max(jnp.where(live, logits, -jnp.inf), axis=-1, keepdims=True)
    shifted = jnp.where(live, logits - top, -jnp.inf)
    expo = jnp.exp(shifted)
    expo_out[...] = expo.astype(BF16)
    hit = live & (column == targets[...] - start)
    values = [
        top,
        jnp.sum(expo, axis=-1, keepdims=True),
        jnp.sum(jnp.where(live, expo * shifted, 0.0), axis=-1, keepdims=True),
        jnp.sum(jnp.where(hit, logits, 0.0), axis=-1, keepdims=True),
        inv,
    ]
    lane = lax.broadcasted_iota(jnp.int32, (logits.shape[0], 128), 1)
    table = jnp.zeros(lane.shape, F32)
    for i, value in enumerate(values):
        table = jnp.where(lane == i, value, table)
    stats[...] = table.T[: stats.shape[0]]


def merged(stats):
    tops, totals, alongs, hits = [stats[:, i] for i in range(4)]
    top = jnp.max(tops, axis=0, keepdims=True)
    lower = jnp.exp(tops - top)
    total = jnp.sum(totals * lower, axis=0, keepdims=True)
    along = jnp.sum((alongs + (tops - top) * totals) * lower, axis=0, keepdims=True)
    return top, total, along, jnp.sum(hits, axis=0, keepdims=True)


def merge_kernel(place, stats, out):
    values = merged(stats[...])
    out[...] = jnp.concatenate(list(values) + [jnp.zeros((out.shape[0] - 4, out.shape[1]), F32)])


def finish_kernel(width, place, stats, pieces, weights, known):
    top, total, along, hits = merged(stats[...])
    weight = weights[...]
    own = pieces[...]
    factors = weight * (jnp.exp(own[:, 0] - top) / total)
    target = weight * (jnp.exp(hits - top) / total - 1.0)
    mean = weight * (along / total - (hits - top)) / width
    rest = known.shape[0] - own.shape[0] - 3
    known[...] = jnp.concatenate(
        [factors, target, mean, own[0, 4:5], jnp.zeros((rest, known.shape[1]), F32)]
    )


def exit_kernel(zs, vocab, place, head, known_mine, known_other, targets_mine, targets_other, *refs):
    part, dlogits = refs[2:]
    core, start = place[1], place[2]
    count, columns = refs[0].shape[1:]
    for side, known, targets in ((0, known_mine, targets_mine), (1, known_other, targets_other)):
        table = known[...].T
        target_grad = table[:, zs : zs + 1]
        spot = targets[...] - start
        rows = pl.ds(pl.multiple_of(jnp.where(side == 0, core, 1 - core) * count, count), count)
        total = jnp.zeros((count, head.shape[2]), F32)
        for at in range(zs):
            column = lax.broadcasted_iota(jnp.int32, (count, columns), 1) + at * columns
            hit = (column == spot) & (column < vocab)
            grad = jnp.where(hit, target_grad, refs[side][at].astype(F32) * table[:, at : at + 1]).astype(BF16)
            dlogits[at, rows, :] = grad
            total += jnp.dot(grad, head[at], preferred_element_type=F32)
        part[rows, :] = total


def head_kernel(zs, place, rows, gain, known_mine, known_other, dlogits, out):
    z, core = place[0], place[1]
    count = dlogits.shape[1]
    columns = dlogits.shape[2]
    mine = known_mine[...].T[:, zs + 2 : zs + 3]
    other = known_other[...].T[:, zs + 2 : zs + 3]
    inv = jnp.concatenate([jnp.where(core == 0, mine, other), jnp.where(core == 0, other, mine)])
    row = rows[:, z].reshape(count, rows.shape[3]).astype(F32)
    normed = (row * inv * gain[...]).astype(BF16)
    for at in range(zs):
        held = min(columns, out.shape[0] - at * columns)
        piece = lax.dot_general(dlogits[at], normed, (((0,), (0,)), ((), ())), preferred_element_type=F32)
        out[at * columns : at * columns + held, :] = piece[:held].astype(BF16)


def local(
    segment_in,
    layer_weight,
    layer_gain,
    final_gain,
    head_weight,
    exit_rows,
    exit_count,
    exit_targets,
    exit_scale,
    out_grad,
):
    pipe = lax.axis_index("pipe")
    core = lax.axis_index("core")
    z = lax.axis_index("z")
    pipes = lax.axis_size("pipe")
    zs = lax.axis_size("z")
    block = z * 2 + core
    seg = segment_in[0]
    weight = layer_weight[0]
    gain = layer_gain[0]
    grad = out_grad[0]
    tokens, width = seg.shape
    slab = weight.shape[1]
    exits = exit_rows.shape[1]
    rows_all = pipes * exits
    vocab_part = head_weight.shape[0]
    columns = -(-vocab_part // (zs * 128)) * 128
    place = jnp.stack([z, core, pipe * vocab_part]).astype(jnp.int32)

    weight_other = swap(weight)
    head_pieces = jnp.pad(head_weight, ((0, zs * columns - vocab_part), (0, 0))).reshape(zs, columns, slab)
    heads = from_back(lambda k: lax.dynamic_index_in_dim(head_pieces, (z + k) % zs, 0, keepdims=False), zs)

    my_rows = exit_rows[pipe]
    pick = (my_rows[:, None] == jnp.arange(tokens, dtype=jnp.int32)[None, :]).astype(BF16)
    row_in = jnp.dot(pick, seg, preferred_element_type=F32)
    row_inv = lax.rsqrt(jnp.mean(row_in * row_in, axis=-1, keepdims=True) + EPSILON)
    row_unit = row_in * row_inv
    row_normed = (row_unit * gain).astype(BF16)
    row_update = rounded(jnp.dot(row_normed, weight, preferred_element_type=F32))
    row_block = lax.dynamic_slice_in_dim(row_in, block * slab, slab, 1)
    hidden = (row_block + row_update).astype(BF16)

    inputs = seg.astype(F32)
    inv_rms = lax.rsqrt(jnp.mean(inputs * inputs, axis=-1, keepdims=True) + EPSILON)
    normed = (inputs * inv_rms * gain).astype(BF16)
    is_exit = jnp.any(pick > 0, axis=0)
    grad_slab = lax.dynamic_slice_in_dim(grad, block * slab, slab, 1)
    held = tokens // (zs * 2)

    def of_core(values):
        grouped = values.reshape((zs, 2, held) + values.shape[1:])
        return lax.dynamic_index_in_dim(grouped, core, 1, keepdims=False)

    grad_core = of_core(grad).reshape(zs * held, width)
    other_block = (z * 2 + 1 - core) * slab
    on_columns = (((1,), (1,)), ((), ()))
    over_rows = (((0,), (0,)), ((), ()))
    over_rows = (((0,), (0,)), ((), ()))
    main_part = lax.dot_general(
        lax.dynamic_slice_in_dim(grad_core, block * slab, slab, 1), weight, on_columns, preferred_element_type=F32
    ) + lax.dot_general(
        lax.dynamic_slice_in_dim(grad_core, other_block, slab, 1),
        weight_other,
        on_columns,
        preferred_element_type=F32,
    )
    hidden_ready, heads[1], heads[7] = lax.optimization_barrier((hidden, heads[1], heads[7]))
    column_rows = spread(hidden_ready, "z", zs)
    column_rows, main_part, heads[2], heads[6], heads[3] = lax.optimization_barrier(
        (column_rows, main_part, heads[2], heads[6], heads[3])
    )
    main_grad = lax.psum_scatter(main_part.astype(BF16), "z", scatter_dimension=0, tiled=True).astype(F32)
    first = block * held
    held_in = lax.dynamic_slice_in_dim(seg, first, held, 0).astype(F32)
    held_grad = lax.dynamic_slice_in_dim(grad, first, held, 0).astype(F32)

    def layer_back(norm_grad, unit, inv, residual):
        unit_grad = norm_grad * gain
        centre = jnp.mean(unit_grad * unit, axis=-1, keepdims=True)
        return (residual + (unit_grad - unit * centre) * inv).astype(BF16)

    held_inv = lax.rsqrt(jnp.mean(held_in * held_in, axis=-1, keepdims=True) + EPSILON)
    held_unit = held_in * held_inv
    unit_core = of_core(jnp.where(is_exit[:, None], 0.0, inputs * inv_rms)).reshape(zs * held, width)
    gain_part = jnp.sum(main_part * unit_core, axis=0)


    all_hidden = spread(column_rows, "pipe", pipes)
    all_hidden, gain_part, normed = lax.optimization_barrier((all_hidden, gain_part, normed))
    gains = lax.dynamic_index_in_dim(final_gain.reshape(zs, 2, slab), core, 1, keepdims=False)
    own = rows_all // 2
    mine, other = kernel_call(
        logits_kernel, [shape((own, columns + 128), F32)] * 2, place, all_hidden, gains, *heads
    )

    all_targets = exit_targets.reshape(2, own, 1)
    targets_mine = lax.dynamic_index_in_dim(all_targets, core, 0, keepdims=False)
    targets_other = lax.dynamic_index_in_dim(all_targets, 1 - core, 0, keepdims=False)
    slot = jnp.arange(exits, dtype=jnp.int32)[None, :]
    weights = jnp.where(slot < exit_count[:, None], exit_scale[:, None], F32(0.0)).reshape(2, 1, own)
    weights = lax.dynamic_index_in_dim(weights, core, 0, keepdims=False)
    expo, stats = kernel_call(
        functools.partial(softmax_kernel, width, vocab_part),
        [shape((own, columns), BF16), shape((8, own), F32)],
        place,
        mine,
        swap(other),
        targets_mine,
    )
    expo, main_grad = lax.optimization_barrier((expo, main_grad))
    main_out = layer_back(main_grad, held_unit, held_inv, held_grad)
    ex_mine = lax.all_gather(expo, "z", axis=0)
    ex_other = swap(ex_mine)
    pieces = spread(stats, "z", zs)
    pieces, main_out = lax.optimization_barrier((pieces, main_out))
    merged_stats = kernel_call(merge_kernel, shape((8, own), F32), place, pieces)
    known_mine = kernel_call(
        functools.partial(finish_kernel, width),
        shape((16, own), F32),
        place,
        spread(merged_stats, "pipe", pipes),
        pieces,
        weights,
    )
    known_other = swap(known_mine)

    exit_part, dlogits = kernel_call(
        functools.partial(exit_kernel, zs, vocab_part),
        [shape((rows_all, slab), F32), shape((zs, rows_all, columns), BF16)],
        place,
        head_pieces,
        known_mine,
        known_other,
        targets_mine,
        targets_other,
        ex_mine,
        ex_other,
    )
    main_out, _ = lax.optimization_barrier((main_out, ex_mine))
    main_all = lax.all_gather(main_out, ("z", "core"), axis=0, tiled=True)
    gain_mine = lax.dynamic_slice_in_dim(final_gain, block * slab, slab, 0)
    head_grad = kernel_call(
        functools.partial(head_kernel, zs),
        shape((vocab_part, slab), BF16),
        place,
        all_hidden,
        gain_mine[None],
        known_mine,
        known_other,
        dlogits,
    )
    exit_grad = jnp.sum(lax.all_to_all(exit_part.reshape(pipes, exits, slab), "pipe", 0, 0), axis=0)
    known = pair(known_mine[zs + 1 : zs + 3], known_other[zs + 1 : zs + 3], core, 1)
    my_known = lax.dynamic_slice_in_dim(known, pipe * exits, exits, 1)
    my_mean = my_known[0][:, None]
    my_inv = my_known[1][:, None]
    exit_unit = hidden.astype(F32) * my_inv
    exit_back = (exit_grad * gain_mine - exit_unit * my_mean) * my_inv
    row_grad = jnp.dot(pick, grad_slab, preferred_element_type=F32) + exit_back
    row_rounded = row_grad.astype(BF16)

    put = pick.T
    slab_rounded = jnp.where(
        is_exit[:, None], jnp.dot(put, row_rounded, preferred_element_type=F32).astype(BF16), grad_slab
    )
    weight_grad = lax.dot_general(normed, slab_rounded, over_rows, preferred_element_type=F32).astype(BF16)
    core_rows = exits // 2
    share = core_rows // zs
    row_other = swap(lax.dynamic_slice_in_dim(row_grad, (1 - core) * core_rows, core_rows, 0))
    row_mine = lax.dynamic_slice_in_dim(row_grad, core * core_rows, core_rows, 0)
    row_part = lax.dot_general(
        row_mine.astype(BF16), weight, on_columns, preferred_element_type=F32
    ) + lax.dot_general(row_other.astype(BF16), weight_other, on_columns, preferred_element_type=F32)
    core_unit = lax.dynamic_slice_in_dim(row_unit, core * core_rows, core_rows, 0)
    gain_part = gain_part + jnp.sum(row_part * core_unit, axis=0)
    piece = slab * 2 // share
    send = jnp.concatenate(
        [
            row_part.reshape(zs, share, width),
            pair(row_mine, row_other, core, 1).reshape(zs, share, 2 * slab),
            gain_part.reshape(zs, share, piece),
        ],
        axis=2,
    )
    got = lax.all_to_all(send, "z", 0, 0)
    summed = jnp.sum(got, axis=0)
    norm_grad = summed[:, :width]
    residual = got[:, :, width : width + 2 * slab].transpose(1, 0, 2).reshape(share, width)
    at = core * core_rows + z * share
    share_unit = lax.dynamic_slice_in_dim(row_unit, at, share, 0)
    share_inv = lax.dynamic_slice_in_dim(row_inv, at, share, 0)
    share_out = layer_back(norm_grad, share_unit, share_inv, residual)
    share_out, weight_grad, head_grad = lax.optimization_barrier((share_out, weight_grad, head_grad))
    gain_parts = [values.astype(BF16) for values in split3(summed[:, width + 2 * slab :])]
    last = spread(jnp.concatenate([share_out] + gain_parts, axis=1), "z", zs)
    last_other = swap(last)
    gain_grad = jnp.sum(
        (last[:, :, width:].astype(F32) + last_other[:, :, width:].astype(F32)).reshape(zs, share, 3, piece), axis=2
    ).reshape(width)
    row_out = pair(last, last_other, core, 0)[:, :, :width].reshape(exits, width)
    input_grad = jnp.where(
        is_exit[:, None], jnp.dot(put, row_out, preferred_element_type=F32).astype(BF16), main_all
    )
    return (input_grad[None], weight_grad[None], gain_grad[None], head_grad)


def solution(mesh):
    pipes, tensors = mesh.devices.shape
    fine = Mesh(mesh.devices.reshape(pipes, tensors // 2, 2), ("pipe", "z", "core"))
    tensor = ("z", "core")
    in_specs = (
        P("pipe", None, None),
        P("pipe", None, tensor),
        P("pipe", None),
        P(),
        P("pipe", tensor),
        P(),
        P(),
        P(),
        P(),
        P("pipe", None, None),
    )
    out_specs = (
        P("pipe", None, None),
        P("pipe", None, tensor),
        P("pipe", None),
        P("pipe", tensor),
    )
    return jax.shard_map(local, mesh=fine, in_specs=in_specs, out_specs=out_specs, check_vma=False)
```

```python
import functools

import jax
import jax.numpy as jnp
from jax import lax
from jax.experimental import pallas as pl
from jax.experimental.pallas import tpu as pltpu
from jax.sharding import Mesh, PartitionSpec as P

F32 = jnp.float32
BF16 = jnp.bfloat16
EPSILON = 1e-05
VMEM = 32 * 1024 * 1024


def rounded(values):
    return lax.reduce_precision(values, 8, 7)


def split3(values):
    first = rounded(values)
    rest = values - first
    second = rounded(rest)
    return [first, second, rest - second]


def spread(values, axis, count):
    return lax.all_to_all(jnp.broadcast_to(values[None], (count,) + values.shape), axis, 0, 0)


def swap(values):
    return lax.ppermute(values, "core", [(0, 1), (1, 0)])


def pair(mine, other, core, axis):
    first = jnp.where(core == 0, mine, other)
    second = jnp.where(core == 0, other, mine)
    return jnp.concatenate([first, second], axis=axis)


def kernel_call(body, out, *operands):
    return pl.pallas_call(
        body,
        out_shape=out,
        in_specs=[
            pl.BlockSpec(memory_space=pltpu.SMEM if i == 0 else pltpu.VMEM) for i in range(len(operands))
        ],
        out_specs=jax.tree.map(lambda _: pl.BlockSpec(memory_space=pltpu.VMEM), out),
        compiler_params=pltpu.CompilerParams(vmem_limit_bytes=VMEM),
    )(*operands)


def vmem_call(body, out, *operands):
    return pl.pallas_call(
        body,
        out_shape=out,
        compiler_params=pltpu.CompilerParams(vmem_limit_bytes=VMEM),
    )(*operands)


def shape(dims, dtype):
    return jax.ShapeDtypeStruct(dims, dtype)


def after(values, done):
    return lax.optimization_barrier((values, done))[0]


def pieces3(values):
    first = values.astype(BF16).astype(F32)
    rest = values - first
    second = rest.astype(BF16).astype(F32)
    return [first, second, rest - second]


def logits_kernel(half, mine, other, gain_mine, gain_other, head_mine, head_other, out):
    squares = 0.0
    part = 0.0
    for row, gain, head in ((mine, gain_mine, head_mine), (other, gain_other, head_other)):
        row = row[...].reshape(-1, row.shape[-1]).astype(F32)
        squares += jnp.sum(row * row, axis=-1, keepdims=True)
        part += lax.dot_general(
            (row * gain[...]).astype(BF16), head[...], (((1,), (1,)), ((), ())), preferred_element_type=F32
        )
    column = lax.broadcasted_iota(jnp.int32, part.shape, 1)
    for i, piece in enumerate(pieces3(squares)):
        part = jnp.where(column == half + i, piece, part)
    out[...] = part.astype(BF16).reshape(out.shape)


def softmax_kernel(width, half, vocab, place, parts, targets, logits_out, stats):
    core, start = place[0], place[1]
    total = parts[0].astype(F32)
    for i in range(1, parts.shape[0]):
        total += parts[i].astype(F32)
    inv = lax.rsqrt(jnp.sum(total[:, half : half + 3], axis=-1, keepdims=True) / width + EPSILON)
    logits = total * inv
    logits_out[...] = logits
    column = lax.broadcasted_iota(jnp.int32, logits.shape, 1)
    live = (column < half) & (column + core * half < vocab)
    top = jnp.max(jnp.where(live, logits, -jnp.inf), axis=-1, keepdims=True)
    shifted = jnp.where(live, logits - top, -jnp.inf)
    expo = jnp.exp(shifted)
    hit = live & (column == targets[...] - start)
    values = [
        top,
        jnp.sum(expo, axis=-1, keepdims=True),
        jnp.sum(jnp.where(live, expo * shifted, 0.0), axis=-1, keepdims=True),
        jnp.sum(jnp.where(hit, logits, 0.0), axis=-1, keepdims=True),
        inv,
    ]
    lane = lax.broadcasted_iota(jnp.int32, (logits.shape[0], 128), 1)
    table = jnp.zeros(lane.shape, F32)
    for i, value in enumerate(values):
        table = jnp.where(lane == i, value, table)
    table = jnp.concatenate([table, jnp.zeros((128 - table.shape[0], 128), F32)])
    stats[...] = table.T[: stats.shape[0]]


def dlogits_kernel(width, half, vocab, place, logits_in, targets, weights, stats, own, out):
    core, start = place[0], place[1]
    tops, totals, alongs, hits = [stats[:, i] for i in range(4)]
    top = jnp.max(tops, axis=0, keepdims=True)
    lower = jnp.exp(tops - top)
    total = jnp.sum(totals * lower, axis=0, keepdims=True)
    along = jnp.sum((alongs + (tops - top) * totals) * lower, axis=0, keepdims=True)
    target = jnp.sum(hits, axis=0, keepdims=True) - top
    weight = weights[...]
    mean = weight * (along / total - target) / width
    table = jnp.concatenate([top, total, weight, mean, own[4:5], jnp.zeros((3, 128), F32)]).T
    rows = logits_in.shape[0]
    top, total, weight, mean, inv = [table[:rows, i : i + 1] for i in range(5)]
    column = lax.broadcasted_iota(jnp.int32, logits_in.shape, 1)
    live = (column < half) & (column + core * half < vocab)
    hit = column == targets[...] - start
    probs = jnp.exp(jnp.where(live, logits_in[...] - top, -jnp.inf)) / total
    grad = jnp.where(live, weight * (probs - jnp.where(hit, 1.0, 0.0)), 0.0)
    for i, piece in enumerate(pieces3(inv) + pieces3(mean)):
        grad = jnp.where(column == half + i, piece, grad)
    out[...] = jnp.broadcast_to(grad.astype(BF16)[None], out.shape)


def exit_kernel(dl_mine, dl_other, head_mine, head_rest, part):
    rows = part.shape[0] * part.shape[1]
    total = jnp.dot(dl_mine[...].reshape(rows, -1), head_mine[...], preferred_element_type=F32)
    total += jnp.dot(dl_other[...].reshape(rows, -1), head_rest[...], preferred_element_type=F32)
    part[...] = total.reshape(part.shape)


def head_kernel(half, place, mine, gain, dl_mine, dl_other, out):
    core = place[0]
    row = mine[...].reshape(-1, mine.shape[-1]).astype(F32)
    low = dl_mine[...].reshape(row.shape[0], -1)
    high = dl_other[...].reshape(row.shape[0], -1)
    inv = jnp.sum(low[:, half : half + 3].astype(F32), axis=-1, keepdims=True)
    normed = (row * inv * gain[...]).astype(BF16)
    over_rows = (((0,), (0,)), ((), ()))
    low = lax.dot_general(low, normed, over_rows, preferred_element_type=F32)
    high = lax.dot_general(high, normed, over_rows, preferred_element_type=F32)
    out[:half, :] = jnp.where(core == 0, low, high)[:half].astype(BF16)
    out[half:, :] = jnp.where(core == 0, high, low)[: out.shape[0] - half].astype(BF16)


def first_kernel(chunks, place, seg, ids, gain, weight, unit_out, inv_out, hidden_out, held):
    step = pl.program_id(0)
    token = lax.broadcasted_iota(jnp.int32, (ids.shape[0], seg.shape[0]), 1)
    pick = (ids[...] == token).astype(BF16)
    chunk = seg.shape[1]
    held[:, pl.ds(pl.multiple_of(step * chunk, chunk), chunk)] = jnp.dot(
        pick, seg[...], preferred_element_type=F32
    )

    @pl.when(step == chunks - 1)
    def _():
        rows = held[...]
        inv = lax.rsqrt(jnp.mean(rows * rows, axis=-1, keepdims=True) + EPSILON)
        unit = rows * inv
        unit_out[...] = unit
        inv_out[...] = jnp.broadcast_to(inv, inv_out.shape)
        update = jnp.dot((unit * gain[...]).astype(BF16), weight[...], preferred_element_type=F32)
        slab = weight.shape[1]
        own = held[:, pl.ds(pl.multiple_of(place[2] * slab, slab), slab)]
        hidden = (own + update.astype(BF16).astype(F32)).astype(BF16)
        hidden_out[...] = jnp.broadcast_to(hidden[None], hidden_out.shape)


def row_kernel(at, place, got, hidden, extra, gain, grad_rows, mine, other, whole):
    core = place[0]
    total = got[0]
    for i in range(1, got.shape[0]):
        total += got[i]
    inv = jnp.sum(extra[:, at : at + 3].astype(F32), axis=-1, keepdims=True)
    mean = jnp.sum(extra[:, at + 3 : at + 6].astype(F32), axis=-1, keepdims=True)
    back = (total * gain[...] - hidden[...].astype(F32) * inv * mean) * inv
    rows = grad_rows[...] + back
    whole[...] = rows.astype(BF16)
    half = mine.shape[0]
    mine[...] = jnp.where(core == 0, rows[:half], rows[half:])
    other[...] = jnp.where(core == 0, rows[half:], rows[:half])


def send_kernel(place, mine, other, weight, weight_other, unit, gain_part, out):
    core = place[0]
    columns = (((1,), (1,)), ((), ()))
    part = lax.dot_general(mine[...].astype(BF16), weight[...], columns, preferred_element_type=F32)
    part += lax.dot_general(other[...].astype(BF16), weight_other[...], columns, preferred_element_type=F32)
    gain = gain_part[...] + jnp.sum(part * unit[...], axis=0, keepdims=True)
    low = jnp.where(core == 0, mine[...], other[...])
    high = jnp.where(core == 0, other[...], mine[...])
    count, share, _ = out.shape
    width, slab = weight.shape
    piece = width // (count * share)
    for i in range(count):
        rows = slice(i * share, (i + 1) * share)
        out[i, :, :width] = part[rows]
        out[i, :, width : width + slab] = low[rows]
        out[i, :, width + slab : width + 2 * slab] = high[rows]
        for j in range(share):
            at = (i * share + j) * piece
            out[i, j : j + 1, width + 2 * slab :] = gain[:, at : at + piece]


def share_kernel(slabs, got, gain, unit, inv, out):
    total = got[0]
    for i in range(1, got.shape[0]):
        total += got[i]
    width = gain.shape[1]
    residual = jnp.concatenate([got[i, :, width : width + slabs] for i in range(got.shape[0])], axis=1)
    unit_grad = total[:, :width] * gain[...]
    centre = jnp.mean(unit_grad * unit[...], axis=-1, keepdims=True)
    rows = residual + (unit_grad - unit[...] * centre) * inv[...]
    whole = jnp.concatenate([rows] + pieces3(total[:, width + slabs :]), axis=1)
    out[...] = jnp.broadcast_to(whole.astype(BF16)[None], out.shape)


def last_kernel(main, rows, ids, out):
    count = main.shape[0]
    token = lax.broadcasted_iota(jnp.int32, (count, ids.shape[1]), 0) + pl.program_id(0) * count
    put = token == ids[...]
    placed = jnp.dot(put.astype(BF16), rows[...], preferred_element_type=F32).astype(BF16)
    found = jnp.max(put.astype(F32), axis=-1, keepdims=True) > 0.0
    out[...] = jnp.where(found, placed, main[...])


def local(
    segment_in,
    layer_weight,
    layer_gain,
    final_gain,
    head_weight,
    exit_rows,
    exit_count,
    exit_targets,
    exit_scale,
    out_grad,
):
    pipe = lax.axis_index("pipe")
    core = lax.axis_index("core")
    z = lax.axis_index("z")
    pipes = lax.axis_size("pipe")
    zs = lax.axis_size("z")
    block = z * 2 + core
    seg = segment_in[0]
    weight = layer_weight[0]
    gain = layer_gain[0]
    grad = out_grad[0]
    tokens, width = seg.shape
    slab = weight.shape[1]
    exits = exit_rows.shape[1]
    rows_all = pipes * exits
    vocab_part = head_weight.shape[0]
    half = -(-vocab_part // 32) * 16
    padded = -(-(half + 6) // 128) * 128
    place = jnp.stack([core, pipe * vocab_part + core * half, block]).astype(jnp.int32)

    weight_other = swap(weight)
    halves = jnp.pad(head_weight, ((0, 2 * half - vocab_part), (0, 0))).reshape(2, half, slab)
    halves = jnp.pad(halves, ((0, 0), (0, padded - half), (0, 0)))
    head_mine = lax.dynamic_index_in_dim(halves, core, 0, keepdims=False)
    head_rest = lax.dynamic_index_in_dim(halves, 1 - core, 0, keepdims=False)
    head_other = swap(head_rest)

    my_rows = exit_rows[pipe]
    pick = (my_rows[:, None] == jnp.arange(tokens, dtype=jnp.int32)[None, :]).astype(BF16)
    chunks = 8
    whole = lambda *dims: pl.BlockSpec(dims, lambda i: (0,) * len(dims))
    row_unit, row_inv, hidden_copies = pl.pallas_call(
        functools.partial(first_kernel, chunks),
        grid=(chunks,),
        in_specs=[
            pl.BlockSpec(memory_space=pltpu.SMEM),
            pl.BlockSpec((tokens, width // chunks), lambda i: (0, i)),
            whole(exits, 1),
            whole(1, width),
            whole(width, slab),
        ],
        out_specs=[whole(exits, width), whole(exits, 128), whole(pipes, exits, slab)],
        out_shape=[
            shape((exits, width), F32),
            shape((exits, 128), F32),
            shape((pipes, exits, slab), BF16),
        ],
        scratch_shapes=[pltpu.VMEM((exits, width), F32)],
        compiler_params=pltpu.CompilerParams(vmem_limit_bytes=VMEM),
    )(place, seg, my_rows[:, None], gain[None], weight)
    hidden = hidden_copies[0]

    all_mine = lax.all_to_all(hidden_copies, "pipe", 0, 0)
    held = tokens // (zs * 2)
    on_columns = (((1,), (1,)), ((), ()))
    over_rows = (((0,), (0,)), ((), ()))

    def of_core(values):
        grouped = values.reshape((zs, 2, held) + values.shape[1:])
        return lax.dynamic_index_in_dim(grouped, core, 1, keepdims=False).reshape((zs * held,) + values.shape[1:])

    core_grad = of_core(grad)
    main_part = lax.dot_general(
        lax.dynamic_slice_in_dim(core_grad, block * slab, slab, 1), weight, on_columns, preferred_element_type=F32
    ) + lax.dot_general(
        lax.dynamic_slice_in_dim(core_grad, (z * 2 + 1 - core) * slab, slab, 1),
        weight_other,
        on_columns,
        preferred_element_type=F32,
    )
    main_sent = main_part.astype(BF16)
    all_mine, main_part, main_sent = lax.optimization_barrier((all_mine, main_part, main_sent))
    main_grad = lax.psum_scatter(main_sent, "z", scatter_dimension=0, tiled=True)
    all_other = swap(all_mine)
    gain_mine = lax.dynamic_slice_in_dim(final_gain, block * slab, slab, 0)[None]
    gain_other = lax.dynamic_slice_in_dim(final_gain, (z * 2 + 1 - core) * slab, slab, 0)[None]
    own = rows_all // zs
    part = vmem_call(
        functools.partial(logits_kernel, half),
        shape((zs, own, padded), BF16),
        all_mine,
        all_other,
        gain_mine,
        gain_other,
        head_mine,
        head_other,
    )
    parts = lax.all_to_all(part, "z", 0, 0)

    is_exit = jnp.any(pick > 0, axis=0)
    core_in = of_core(after(seg, part)).astype(F32)
    core_inv = lax.rsqrt(jnp.mean(core_in * core_in, axis=-1, keepdims=True) + EPSILON)
    core_inv = jnp.where(of_core(is_exit)[:, None], 0.0, core_inv)
    gain_part = jnp.sum(main_part * (core_in * core_inv), axis=0)
    grad_slab = lax.dynamic_slice_in_dim(after(grad, part), block * slab, slab, 1)
    grad_rows = jnp.dot(pick, grad_slab, preferred_element_type=F32)
    core_rows = exits // 2
    core_unit = lax.dynamic_slice_in_dim(row_unit, core * core_rows, core_rows, 0)
    all_targets = exit_targets.reshape(rows_all, 1)
    targets = lax.dynamic_slice_in_dim(all_targets, z * own, own, 0)
    slot = jnp.arange(exits, dtype=jnp.int32)[None, :]
    weights = jnp.where(slot < exit_count[:, None], exit_scale[:, None], F32(0.0)).reshape(1, rows_all)
    weights = jnp.pad(lax.dynamic_slice_in_dim(weights, z * own, own, 1), ((0, 0), (0, 128 - own)))
    parts, gain_part, grad_rows = lax.optimization_barrier((parts, gain_part, grad_rows))

    logits, stats = kernel_call(
        functools.partial(softmax_kernel, width, half, vocab_part),
        [shape((own, padded), F32), shape((8, 128), F32)],
        place,
        parts,
        targets,
    )
    all_stats = spread(jnp.stack([stats, swap(stats)]), "pipe", pipes).reshape(pipes * 2, 8, 128)
    dlogits = kernel_call(
        functools.partial(dlogits_kernel, width, half, vocab_part),
        shape((zs, own, padded), BF16),
        place,
        logits,
        targets,
        weights,
        all_stats,
        stats,
    )
    dl_mine = lax.all_to_all(dlogits, "z", 0, 0)

    def layer_back(norm_grad, unit, inv, residual):
        unit_grad = norm_grad * gain
        centre = jnp.mean(unit_grad * unit, axis=-1, keepdims=True)
        return (residual + (unit_grad - unit * centre) * inv).astype(BF16)

    first = block * held
    held_in = lax.dynamic_slice_in_dim(after(seg, dlogits), first, held, 0).astype(F32)
    held_grad = lax.dynamic_slice_in_dim(after(grad, dlogits), first, held, 0).astype(F32)
    held_inv = lax.rsqrt(jnp.mean(held_in * held_in, axis=-1, keepdims=True) + EPSILON)
    main_out = layer_back(main_grad.astype(F32), held_in * held_inv, held_inv, held_grad)
    inputs = after(seg, dlogits).astype(F32)
    inv_rms = lax.rsqrt(jnp.mean(inputs * inputs, axis=-1, keepdims=True) + EPSILON)
    normed = (inputs * inv_rms * gain).astype(BF16)
    dl_mine, main_out, normed = lax.optimization_barrier((dl_mine, main_out, normed))
    main_all = lax.all_gather(main_out, ("z", "core"), axis=0, tiled=True)
    dl_other = swap(dl_mine)

    exit_part = vmem_call(
        exit_kernel, shape((pipes, exits, slab), F32), dl_mine, dl_other, head_mine, head_rest
    )
    exit_got = lax.all_to_all(exit_part, "pipe", 0, 0)
    head_grad = kernel_call(
        functools.partial(head_kernel, half),
        shape((vocab_part, slab), BF16),
        place,
        all_mine,
        gain_mine,
        after(dl_mine, exit_part),
        dl_other,
    )
    tail = half // 128 * 128
    extra = lax.dynamic_slice_in_dim(
        dl_mine.reshape(rows_all, padded)[:, tail : tail + 128], pipe * exits, exits, 0
    )
    exit_got, head_grad, extra = lax.optimization_barrier((exit_got, head_grad, extra))
    row_mine, row_send, row_rounded = kernel_call(
        functools.partial(row_kernel, half - tail),
        [shape((core_rows, slab), F32)] * 2 + [shape((exits, slab), BF16)],
        place,
        exit_got,
        hidden,
        extra,
        gain_mine,
        grad_rows,
    )

    put = pick.T
    share = core_rows // zs
    piece = slab * 2 // share
    send = kernel_call(
        send_kernel,
        shape((zs, share, width + 2 * slab + piece), F32),
        place,
        row_mine,
        swap(row_send),
        weight,
        weight_other,
        core_unit,
        gain_part[None],
    )
    got = lax.all_to_all(send, "z", 0, 0)
    slab_rounded = jnp.where(
        is_exit[:, None], jnp.dot(put, after(row_rounded, send), preferred_element_type=F32).astype(BF16), grad_slab
    )
    weight_grad = lax.dot_general(normed, slab_rounded, over_rows, preferred_element_type=F32).astype(BF16)
    got, weight_grad = lax.optimization_barrier((got, weight_grad))
    at = core * core_rows + z * share
    last = vmem_call(
        functools.partial(share_kernel, 2 * slab),
        shape((zs, share, width + 3 * piece), BF16),
        got,
        gain[None],
        lax.dynamic_slice_in_dim(row_unit, at, share, 0),
        lax.dynamic_slice_in_dim(row_inv[:, :1], at, share, 0),
    )
    last = lax.all_to_all(last, "z", 0, 0)
    last_other = swap(last)
    gain_grad = jnp.sum(
        (last[:, :, width:].astype(F32) + last_other[:, :, width:].astype(F32)).reshape(zs, share, 3, piece), axis=2
    ).reshape(width)
    row_out = pair(last, last_other, core, 0)[:, :, :width].reshape(exits, width)
    steps = 8
    input_grad = pl.pallas_call(
        last_kernel,
        grid=(steps,),
        in_specs=[
            pl.BlockSpec((tokens // steps, width), lambda i: (i, 0)),
            whole(exits, width),
            whole(1, exits),
        ],
        out_specs=pl.BlockSpec((tokens // steps, width), lambda i: (i, 0)),
        out_shape=shape((tokens, width), BF16),
        compiler_params=pltpu.CompilerParams(vmem_limit_bytes=VMEM),
    )(main_all, row_out, my_rows[None])
    return (input_grad[None], weight_grad[None], gain_grad[None], head_grad)


def solution(mesh):
    pipes, tensors = mesh.devices.shape
    fine = Mesh(mesh.devices.reshape(pipes, tensors // 2, 2), ("pipe", "z", "core"))
    tensor = ("z", "core")
    in_specs = (
        P("pipe", None, None),
        P("pipe", None, tensor),
        P("pipe", None),
        P(),
        P("pipe", tensor),
        P(),
        P(),
        P(),
        P(),
        P("pipe", None, None),
    )
    out_specs = (
        P("pipe", None, None),
        P("pipe", None, tensor),
        P("pipe", None),
        P("pipe", tensor),
    )
    return jax.shard_map(local, mesh=fine, in_specs=in_specs, out_specs=out_specs, check_vma=False)
```

```python
import functools

import jax
import jax.numpy as jnp
from jax import lax
from jax.experimental import pallas as pl
from jax.experimental.pallas import tpu as pltpu
from jax.sharding import Mesh, PartitionSpec as P

F32 = jnp.float32
BF16 = jnp.bfloat16
EPSILON = 1e-05
VMEM = 32 * 1024 * 1024
LARGE = 56 * 1024 * 1024


def spread(values, axis, count):
    return lax.all_to_all(jnp.broadcast_to(values[None], (count,) + values.shape), axis, 0, 0)


def swap(values):
    return lax.ppermute(values, "core", [(0, 1), (1, 0)])


def pair(mine, other, core, axis):
    first = jnp.where(core == 0, mine, other)
    second = jnp.where(core == 0, other, mine)
    return jnp.concatenate([first, second], axis=axis)


def kernel_call(body, out, *operands):
    return pl.pallas_call(
        body,
        out_shape=out,
        in_specs=[
            pl.BlockSpec(memory_space=pltpu.SMEM if i == 0 else pltpu.VMEM) for i in range(len(operands))
        ],
        out_specs=jax.tree.map(lambda _: pl.BlockSpec(memory_space=pltpu.VMEM), out),
        compiler_params=pltpu.CompilerParams(vmem_limit_bytes=VMEM),
    )(*operands)


def vmem_call(body, out, *operands):
    return pl.pallas_call(
        body,
        out_shape=out,
        compiler_params=pltpu.CompilerParams(vmem_limit_bytes=VMEM),
    )(*operands)


def shape(dims, dtype):
    return jax.ShapeDtypeStruct(dims, dtype)


def after(values, done):
    return lax.optimization_barrier((values, done))[0]


def pieces3(values):
    first = values.astype(BF16).astype(F32)
    rest = values - first
    second = rest.astype(BF16).astype(F32)
    return [first, second, rest - second]


def first_kernel(chunks, place, seg, ids, gain, weight, head, unit_out, inv_out, sent, held):
    step = pl.program_id(0)
    token = lax.broadcasted_iota(jnp.int32, (ids.shape[0], seg.shape[0]), 1)
    pick = (ids[...] == token).astype(BF16)
    chunk = seg.shape[1]
    held[:, pl.ds(pl.multiple_of(step * chunk, chunk), chunk)] = jnp.dot(
        pick, seg[...], preferred_element_type=F32
    )
    count, rows_sent, slab = sent.shape
    exits = ids.shape[0]
    columns = rows_sent - exits

    @pl.when(step == 0)
    def _():
        for i in range(count):
            live = min(columns, head.shape[0] - i * columns)
            sent[i, exits : exits + live, :] = head[i * columns : i * columns + live, :]
            if live < columns:
                sent[i, exits + live :, :] = jnp.zeros((columns - live, slab), BF16)

    @pl.when(step == chunks - 1)
    def _():
        rows = held[...]
        inv = lax.rsqrt(jnp.mean(rows * rows, axis=-1, keepdims=True) + EPSILON)
        unit = rows * inv
        unit_out[...] = unit
        inv_out[...] = jnp.broadcast_to(inv, inv_out.shape)
        update = jnp.dot((unit * gain[...]).astype(BF16), weight[...], preferred_element_type=F32)
        own = held[:, pl.ds(pl.multiple_of(place[3] * slab, slab), slab)]
        hidden = (own + update.astype(BF16).astype(F32)).astype(BF16)
        for i in range(count):
            sent[i, :exits, :] = hidden


def main_kernel(place, grad, seg, ids, weight, weight_other, sent, gain_out, inverse):
    core = place[1]
    step = pl.program_id(0)
    count, _, held, width = seg.shape
    tokens = count * held
    rows = seg[...].reshape(tokens, width)

    @pl.when(step == 0)
    def _():
        full = rows.astype(F32)
        inv = lax.rsqrt(jnp.mean(full * full, axis=-1, keepdims=True) + EPSILON)
        index = lax.broadcasted_iota(jnp.int32, (tokens, ids.shape[1]), 0)
        index = (index // held * 2 + core) * held + index % held
        found = jnp.max((index == ids[...]).astype(F32), axis=-1, keepdims=True) > 0.0
        inverse[...] = jnp.broadcast_to(jnp.where(found, 0.0, inv), inverse.shape)

    columns = (((1,), (1,)), ((), ()))
    slab = weight.shape[1]
    low = grad[:, 0, :, :slab].reshape(tokens, slab)
    high = grad[:, 0, :, slab:].reshape(tokens, slab)
    part = lax.dot_general(jnp.where(core == 0, low, high), weight[...], columns, preferred_element_type=F32)
    part += lax.dot_general(jnp.where(core == 0, high, low), weight_other[...], columns, preferred_element_type=F32)
    sent[...] = part.astype(BF16)
    chunk = part.shape[1]
    unit = seg[:, 0, :, pl.ds(pl.multiple_of(step * chunk, chunk), chunk)].reshape(tokens, chunk).astype(F32)
    gain_out[...] = jnp.sum(part * (unit * inverse[:, :1]), axis=0, keepdims=True)


def logits_kernel(place, rows, gains, heads, mine, other):
    core = place[1]
    total = mine.shape[0] * 2
    skip = heads.shape[1] - (mine.shape[1] - 128)
    part = jnp.zeros((total, mine.shape[1] - 128), F32)
    squares = jnp.zeros((total, 1), F32)
    for at in range(heads.shape[0]):
        row = rows[:, at].reshape(total, rows.shape[3]).astype(F32)
        squares += jnp.sum(row * row, axis=-1, keepdims=True)
        part += lax.dot_general(
            (row * gains[at : at + 1, :]).astype(BF16),
            heads[at, skip:, :],
            (((1,), (1,)), ((), ())),
            preferred_element_type=F32,
        )
    whole = jnp.concatenate([part, jnp.broadcast_to(squares, (total, 128))], axis=1)
    low, high = whole[: total // 2], whole[total // 2 :]
    mine[...] = jnp.where(core == 0, low, high)
    other[...] = jnp.where(core == 0, high, low)


def softmax_kernel(width, vocab, place, mine, other, targets, expo_out, stats):
    z, start = place[0], place[2]
    columns = expo_out.shape[1]
    whole = mine[...] + other[...]
    inv = lax.rsqrt(whole[:, columns : columns + 1] / width + EPSILON)
    logits = whole[:, :columns] * inv
    column = lax.broadcasted_iota(jnp.int32, logits.shape, 1) + z * columns
    live = column < vocab
    top = jnp.max(jnp.where(live, logits, -jnp.inf), axis=-1, keepdims=True)
    shifted = jnp.where(live, logits - top, -jnp.inf)
    expo = jnp.exp(shifted)
    expo_out[...] = expo.astype(BF16)
    hit = live & (column == targets[...] - start)
    values = [
        top,
        jnp.sum(expo, axis=-1, keepdims=True),
        jnp.sum(jnp.where(live, expo * shifted, 0.0), axis=-1, keepdims=True),
        jnp.sum(jnp.where(hit, logits, 0.0), axis=-1, keepdims=True),
        inv,
    ]
    lane = lax.broadcasted_iota(jnp.int32, (logits.shape[0], 128), 1)
    table = jnp.zeros(lane.shape, F32)
    for i, value in enumerate(values):
        table = jnp.where(lane == i, value, table)
    stats[...] = jnp.broadcast_to(table.T[: stats.shape[1]][None], stats.shape)


def merged(stats):
    tops, totals, alongs, hits = [stats[:, i] for i in range(4)]
    top = jnp.max(tops, axis=0, keepdims=True)
    lower = jnp.exp(tops - top)
    total = jnp.sum(totals * lower, axis=0, keepdims=True)
    along = jnp.sum((alongs + (tops - top) * totals) * lower, axis=0, keepdims=True)
    return top, total, along, jnp.sum(hits, axis=0, keepdims=True)


def merge_kernel(place, stats, out):
    values = merged(stats[...])
    whole = jnp.concatenate(list(values) + [jnp.zeros((out.shape[1] - 4, out.shape[2]), F32)])
    out[...] = jnp.broadcast_to(whole[None], out.shape)


def finish_kernel(width, place, stats, pieces, weights, known):
    top, total, along, hits = merged(stats[...])
    weight = weights[...]
    own = pieces[...]
    factors = weight * (jnp.exp(own[:, 0] - top) / total)
    target = weight * (jnp.exp(hits - top) / total - 1.0)
    mean = weight * (along / total - (hits - top)) / width
    rest = known.shape[0] - own.shape[0] - 3
    known[...] = jnp.concatenate(
        [factors, target, mean, own[0, 4:5], jnp.zeros((rest, known.shape[1]), F32)]
    )


def exit_kernel(zs, vocab, place, head, known_mine, known_other, targets_mine, targets_other, *refs):
    part, dlogits, kept = refs[2:]
    core, start = place[1], place[2]
    count, columns = refs[0].shape[1:]
    for side, known, targets in ((0, known_mine, targets_mine), (1, known_other, targets_other)):
        table = known[...].T
        target_grad = table[:, zs : zs + 1]
        spot = targets[...] - start
        rows = pl.ds(pl.multiple_of(jnp.where(side == 0, core, 1 - core) * count, count), count)
        total = jnp.zeros((count, head.shape[2]), F32)
        for at in range(zs):
            column = lax.broadcasted_iota(jnp.int32, (count, columns), 1) + at * columns
            hit = (column == spot) & (column < vocab)
            grad = jnp.where(hit, target_grad, refs[side][at].astype(F32) * table[:, at : at + 1]).astype(BF16)
            dlogits[at, rows, :] = grad
            total += jnp.dot(grad, head[at], preferred_element_type=F32)
        part[rows, :] = total
        lane = lax.broadcasted_iota(jnp.int32, (count, 128), 1)
        kept[rows, :] = jnp.where(lane == 0, table[:, zs + 1 : zs + 2], table[:, zs + 2 : zs + 3])


def head_kernel(zs, place, rows, gain, known_mine, known_other, dlogits, out):
    z, core = place[0], place[1]
    count = dlogits.shape[1]
    columns = dlogits.shape[2]
    mine = known_mine[...].T[:, zs + 2 : zs + 3]
    other = known_other[...].T[:, zs + 2 : zs + 3]
    inv = jnp.concatenate([jnp.where(core == 0, mine, other), jnp.where(core == 0, other, mine)])
    row = rows[:, z].reshape(count, rows.shape[3]).astype(F32)
    normed = (row * inv * gain[...]).astype(BF16)
    for at in range(zs):
        held = min(columns, out.shape[0] - at * columns)
        piece = lax.dot_general(dlogits[at], normed, (((0,), (0,)), ((), ())), preferred_element_type=F32)
        out[at * columns : at * columns + held, :] = piece[:held].astype(BF16)


def row_kernel(place, got, hidden, kept, gain, grad_rows, mine, other, whole):
    core = place[1]
    total = got[0]
    for i in range(1, got.shape[0]):
        total += got[i]
    mean, inv = kept[:, 0:1], kept[:, 1:2]
    back = (total * gain[...] - hidden[...].astype(F32) * inv * mean) * inv
    rows = grad_rows[...] + back
    whole[...] = rows.astype(BF16)
    half = mine.shape[0]
    mine[...] = jnp.where(core == 0, rows[:half], rows[half:])
    other[...] = jnp.where(core == 0, rows[half:], rows[:half])


def send_kernel(place, mine, other, weight, weight_other, unit, gain_part, out):
    core = place[1]
    columns = (((1,), (1,)), ((), ()))
    part = lax.dot_general(mine[...].astype(BF16), weight[...], columns, preferred_element_type=F32)
    part += lax.dot_general(other[...].astype(BF16), weight_other[...], columns, preferred_element_type=F32)
    gain = gain_part[...] + jnp.sum(part * unit[...], axis=0, keepdims=True)
    low = jnp.where(core == 0, mine[...], other[...])
    high = jnp.where(core == 0, other[...], mine[...])
    count, share, _ = out.shape
    width, slab = weight.shape
    piece = width // (count * share)
    for i in range(count):
        rows = slice(i * share, (i + 1) * share)
        out[i, :, :width] = part[rows]
        out[i, :, width : width + slab] = low[rows]
        out[i, :, width + slab : width + 2 * slab] = high[rows]
        for j in range(share):
            at = (i * share + j) * piece
            out[i, j : j + 1, width + 2 * slab :] = gain[:, at : at + piece]


def share_kernel(slabs, got, gain, unit, inv, out):
    total = got[0]
    for i in range(1, got.shape[0]):
        total += got[i]
    width = gain.shape[1]
    residual = jnp.concatenate([got[i, :, width : width + slabs] for i in range(got.shape[0])], axis=1)
    unit_grad = total[:, :width] * gain[...]
    centre = jnp.mean(unit_grad * unit[...], axis=-1, keepdims=True)
    rows = residual + (unit_grad - unit[...] * centre) * inv[...]
    whole = jnp.concatenate([rows] + pieces3(total[:, width + slabs :]), axis=1)
    out[...] = jnp.broadcast_to(whole.astype(BF16)[None], out.shape)


def last_kernel(main, rows, ids, out):
    count = main.shape[0]
    token = lax.broadcasted_iota(jnp.int32, (count, ids.shape[1]), 0) + pl.program_id(0) * count
    put = token == ids[...]
    placed = jnp.dot(put.astype(BF16), rows[...], preferred_element_type=F32).astype(BF16)
    found = jnp.max(put.astype(F32), axis=-1, keepdims=True) > 0.0
    out[...] = jnp.where(found, placed, main[...])


def local(
    segment_in,
    layer_weight,
    layer_gain,
    final_gain,
    head_weight,
    exit_rows,
    exit_count,
    exit_targets,
    exit_scale,
    out_grad,
):
    pipe = lax.axis_index("pipe")
    core = lax.axis_index("core")
    z = lax.axis_index("z")
    pipes = lax.axis_size("pipe")
    zs = lax.axis_size("z")
    block = z * 2 + core
    seg = segment_in[0]
    weight = layer_weight[0]
    gain = layer_gain[0]
    grad = out_grad[0]
    tokens, width = seg.shape
    slab = weight.shape[1]
    exits = exit_rows.shape[1]
    rows_all = pipes * exits
    vocab_part = head_weight.shape[0]
    columns = -(-vocab_part // (zs * 128)) * 128
    place = jnp.stack([z, core, pipe * vocab_part, block]).astype(jnp.int32)
    my_rows = exit_rows[pipe]
    weight_other = swap(weight)
    whole = lambda *dims: pl.BlockSpec(dims, lambda i, *_: (0,) * len(dims))

    chunks = 8
    row_unit, row_inv, sent = pl.pallas_call(
        functools.partial(first_kernel, chunks),
        grid=(chunks,),
        in_specs=[
            pl.BlockSpec(memory_space=pltpu.SMEM),
            pl.BlockSpec((tokens, width // chunks), lambda i: (0, i)),
            whole(exits, 1),
            whole(1, width),
            whole(width, slab),
            whole(vocab_part, slab),
        ],
        out_specs=[whole(exits, width), whole(exits, 128), whole(zs, exits + columns, slab)],
        out_shape=[
            shape((exits, width), F32),
            shape((exits, 128), F32),
            shape((zs, exits + columns, slab), BF16),
        ],
        scratch_shapes=[pltpu.VMEM((exits, width), F32)],
        compiler_params=pltpu.CompilerParams(vmem_limit_bytes=LARGE),
    )(place, seg, my_rows[:, None], gain[None], weight, head_weight)
    hidden = sent[0, :exits]
    got_first = lax.all_to_all(sent, "z", 0, 0)

    held = tokens // (zs * 2)
    steps = 4
    chunk = width // steps
    main_sent, gain_part = pl.pallas_call(
        main_kernel,
        grid_spec=pltpu.PrefetchScalarGridSpec(
            num_scalar_prefetch=1,
            grid=(steps,),
            in_specs=[
                pl.BlockSpec((zs, 1, held, 2 * slab), lambda i, at: (0, at[1], 0, at[0])),
                pl.BlockSpec((zs, 1, held, width), lambda i, at: (0, at[1], 0, 0)),
                whole(1, exits),
                pl.BlockSpec((chunk, slab), lambda i, at: (i, 0)),
                pl.BlockSpec((chunk, slab), lambda i, at: (i, 0)),
            ],
            out_specs=[
                pl.BlockSpec((zs * held, chunk), lambda i, at: (0, i)),
                pl.BlockSpec((1, chunk), lambda i, at: (0, i)),
            ],
            scratch_shapes=[pltpu.VMEM((zs * held, 128), F32)],
        ),
        out_shape=[shape((zs * held, width), BF16), shape((1, width), F32)],
        compiler_params=pltpu.CompilerParams(vmem_limit_bytes=LARGE),
    )(
        place,
        grad.reshape(zs, 2, held, width),
        seg.reshape(zs, 2, held, width),
        my_rows[None],
        weight,
        weight_other,
    )
    got_first, main_sent = lax.optimization_barrier((got_first, main_sent))
    main_grad = lax.psum_scatter(main_sent, "z", scatter_dimension=0, tiled=True)

    gathered = jnp.broadcast_to(got_first[None, :, :exits], (pipes, zs, exits, slab))
    all_hidden = lax.all_to_all(gathered, "pipe", 0, 0)
    own = rows_all // 2
    pick = (my_rows[:, None] == jnp.arange(tokens, dtype=jnp.int32)[None, :]).astype(BF16)
    is_exit = jnp.any(pick > 0, axis=0)
    inputs = after(seg, gathered).astype(F32)
    inv_rms = lax.rsqrt(jnp.mean(inputs * inputs, axis=-1, keepdims=True) + EPSILON)
    normed = (inputs * inv_rms * gain).astype(BF16)
    grad_slab = lax.dynamic_slice_in_dim(after(grad, gathered), block * slab, slab, 1)
    grad_rows = jnp.dot(pick, grad_slab, preferred_element_type=F32)
    core_rows = exits // 2
    share = core_rows // zs
    core_unit = lax.dynamic_slice_in_dim(row_unit, core * core_rows, core_rows, 0)
    share_at = core * core_rows + z * share
    share_unit = lax.dynamic_slice_in_dim(row_unit, share_at, share, 0)
    share_inv = lax.dynamic_slice_in_dim(row_inv[:, :1], share_at, share, 0)
    gains = lax.dynamic_index_in_dim(final_gain.reshape(zs, 2, slab), core, 1, keepdims=False)
    gain_mine = lax.dynamic_slice_in_dim(final_gain, block * slab, slab, 0)[None]
    all_targets = exit_targets.reshape(2, own, 1)
    targets_mine = lax.dynamic_index_in_dim(all_targets, core, 0, keepdims=False)
    targets_other = lax.dynamic_index_in_dim(all_targets, 1 - core, 0, keepdims=False)
    slot = jnp.arange(exits, dtype=jnp.int32)[None, :]
    weights = jnp.where(slot < exit_count[:, None], exit_scale[:, None], F32(0.0)).reshape(2, 1, own)
    weights = lax.dynamic_index_in_dim(weights, core, 0, keepdims=False)
    (
        all_hidden,
        normed,
        grad_rows,
        core_unit,
        share_unit,
        share_inv,
        targets_mine,
        targets_other,
        weights,
        is_exit,
    ) = lax.optimization_barrier(
        (
            all_hidden,
            normed,
            grad_rows,
            core_unit,
            share_unit,
            share_inv,
            targets_mine,
            targets_other,
            weights,
            is_exit,
        )
    )
    mine, other = kernel_call(
        logits_kernel, [shape((own, columns + 128), F32)] * 2, place, all_hidden, gains, got_first
    )

    expo, stats = kernel_call(
        functools.partial(softmax_kernel, width, vocab_part),
        [shape((own, columns), BF16), shape((zs, 8, own), F32)],
        place,
        mine,
        swap(other),
        targets_mine,
    )
    expo, stats, main_grad = lax.optimization_barrier((expo, stats, main_grad))
    ex_mine = lax.all_gather(expo, "z", axis=0)
    pieces = lax.all_to_all(stats, "z", 0, 0)
    merged_stats = kernel_call(merge_kernel, shape((pipes, 8, own), F32), place, pieces)
    all_stats = lax.all_to_all(merged_stats, "pipe", 0, 0)

    first = block * held
    held_in = lax.dynamic_slice_in_dim(after(seg, stats), first, held, 0).astype(F32)
    held_grad = lax.dynamic_slice_in_dim(after(grad, stats), first, held, 0).astype(F32)
    held_inv = lax.rsqrt(jnp.mean(held_in * held_in, axis=-1, keepdims=True) + EPSILON)
    held_unit = held_in * held_inv
    unit_grad = main_grad.astype(F32) * gain
    centre = jnp.mean(unit_grad * held_unit, axis=-1, keepdims=True)
    main_out = (held_grad + (unit_grad - held_unit * centre) * held_inv).astype(BF16)
    all_stats, main_out = lax.optimization_barrier((all_stats, main_out))
    known_mine = kernel_call(
        functools.partial(finish_kernel, width), shape((16, own), F32), place, all_stats, pieces, weights
    )
    known_other = swap(known_mine)
    ex_mine, main_out = lax.optimization_barrier((after(ex_mine, all_stats), main_out))
    main_all = lax.all_gather(main_out, ("z", "core"), axis=0, tiled=True)
    ex_other = swap(ex_mine)

    exit_part, dlogits, kept = kernel_call(
        functools.partial(exit_kernel, zs, vocab_part),
        [
            shape((rows_all, slab), F32),
            shape((zs, rows_all, columns), BF16),
            shape((rows_all, 128), F32),
        ],
        place,
        sent[:, exits:],
        known_mine,
        known_other,
        targets_mine,
        targets_other,
        ex_mine,
        ex_other,
    )
    exit_got = lax.all_to_all(exit_part.reshape(pipes, exits, slab), "pipe", 0, 0)
    head_grad = kernel_call(
        functools.partial(head_kernel, zs),
        shape((vocab_part, slab), BF16),
        place,
        all_hidden,
        gain_mine,
        known_mine,
        known_other,
        after(dlogits, exit_part),
    )
    kept = lax.dynamic_slice_in_dim(kept, pipe * exits, exits, 0)
    exit_got, head_grad, kept = lax.optimization_barrier((exit_got, head_grad, kept))
    row_mine, row_send, row_rounded = kernel_call(
        row_kernel,
        [shape((core_rows, slab), F32)] * 2 + [shape((exits, slab), BF16)],
        place,
        exit_got,
        hidden,
        kept,
        gain_mine,
        grad_rows,
    )

    piece = slab * 2 // share
    send = kernel_call(
        send_kernel,
        shape((zs, share, width + 2 * slab + piece), F32),
        place,
        row_mine,
        swap(row_send),
        weight,
        weight_other,
        core_unit,
        gain_part,
    )
    got = lax.all_to_all(send, "z", 0, 0)
    put = pick.T
    slab_rounded = jnp.where(
        is_exit[:, None], jnp.dot(put, after(row_rounded, send), preferred_element_type=F32).astype(BF16), grad_slab
    )
    over_rows = (((0,), (0,)), ((), ()))
    weight_grad = lax.dot_general(normed, slab_rounded, over_rows, preferred_element_type=F32).astype(BF16)
    got, weight_grad = lax.optimization_barrier((got, weight_grad))
    last = vmem_call(
        functools.partial(share_kernel, 2 * slab),
        shape((zs, share, width + 3 * piece), BF16),
        got,
        gain[None],
        share_unit,
        share_inv,
    )
    last = lax.all_to_all(last, "z", 0, 0)
    last_other = swap(last)
    gain_grad = jnp.sum(
        (last[:, :, width:].astype(F32) + last_other[:, :, width:].astype(F32)).reshape(zs, share, 3, piece), axis=2
    ).reshape(width)
    row_out = pair(last, last_other, core, 0)[:, :, :width].reshape(exits, width)
    steps = 8
    input_grad = pl.pallas_call(
        last_kernel,
        grid=(steps,),
        in_specs=[
            pl.BlockSpec((tokens // steps, width), lambda i: (i, 0)),
            whole(exits, width),
            whole(1, exits),
        ],
        out_specs=pl.BlockSpec((tokens // steps, width), lambda i: (i, 0)),
        out_shape=shape((tokens, width), BF16),
        compiler_params=pltpu.CompilerParams(vmem_limit_bytes=LARGE),
    )(main_all, row_out, my_rows[None])
    return (input_grad[None], weight_grad[None], gain_grad[None], head_grad)


def solution(mesh):
    pipes, tensors = mesh.devices.shape
    fine = Mesh(mesh.devices.reshape(pipes, tensors // 2, 2), ("pipe", "z", "core"))
    tensor = ("z", "core")
    in_specs = (
        P("pipe", None, None),
        P("pipe", None, tensor),
        P("pipe", None),
        P(),
        P("pipe", tensor),
        P(),
        P(),
        P(),
        P(),
        P("pipe", None, None),
    )
    out_specs = (
        P("pipe", None, None),
        P("pipe", None, tensor),
        P("pipe", None),
        P("pipe", tensor),
    )
    return jax.shard_map(local, mesh=fine, in_specs=in_specs, out_specs=out_specs, check_vma=False)
```

```python
import functools

import jax
import jax.numpy as jnp
from jax import lax
from jax.experimental import pallas as pl
from jax.experimental.pallas import tpu as pltpu
from jax.sharding import Mesh, PartitionSpec as P

F32 = jnp.float32
BF16 = jnp.bfloat16
EPSILON = 1e-05
SMALL = 20 * 1024 * 1024
VMEM = 32 * 1024 * 1024
LARGE = 56 * 1024 * 1024


def spread(values, axis, count):
    return lax.all_to_all(jnp.broadcast_to(values[None], (count,) + values.shape), axis, 0, 0)


def swap(values):
    return lax.ppermute(values, "core", [(0, 1), (1, 0)])


def pair(mine, other, core, axis):
    first = jnp.where(core == 0, mine, other)
    second = jnp.where(core == 0, other, mine)
    return jnp.concatenate([first, second], axis=axis)


def kernel_call(body, out, *operands):
    return pl.pallas_call(
        body,
        out_shape=out,
        in_specs=[
            pl.BlockSpec(memory_space=pltpu.SMEM if i == 0 else pltpu.VMEM) for i in range(len(operands))
        ],
        out_specs=jax.tree.map(lambda _: pl.BlockSpec(memory_space=pltpu.VMEM), out),
        compiler_params=pltpu.CompilerParams(vmem_limit_bytes=VMEM),
    )(*operands)


def vmem_call(body, out, *operands):
    return pl.pallas_call(
        body,
        out_shape=out,
        compiler_params=pltpu.CompilerParams(vmem_limit_bytes=VMEM),
    )(*operands)


def piped_call(body, out, *operands, limit=LARGE):
    specs = [pl.BlockSpec(memory_space=pltpu.SMEM)] + [
        pl.BlockSpec(value.shape, lambda i, n=value.ndim: (0,) * n) for value in operands[1:]
    ]
    return pl.pallas_call(
        body,
        grid=(1,),
        out_shape=out,
        in_specs=specs,
        out_specs=jax.tree.map(lambda value: pl.BlockSpec(value.shape, lambda i, n=len(value.shape): (0,) * n), out),
        compiler_params=pltpu.CompilerParams(vmem_limit_bytes=limit),
    )(*operands)


def shape(dims, dtype):
    return jax.ShapeDtypeStruct(dims, dtype)


def after(values, done):
    return lax.optimization_barrier((values, done))[0]


def pieces3(values):
    first = values.astype(BF16).astype(F32)
    rest = values - first
    second = rest.astype(BF16).astype(F32)
    return [first, second, rest - second]


def chip_term(core, grad, weight, weight_other):
    count, _, held, columns = grad.shape
    slab = columns // 2
    over = (((1,), (1,)), ((), ()))
    low = grad[:, 0, :, :slab].reshape(count * held, slab)
    high = grad[:, 0, :, slab:].reshape(count * held, slab)
    part = lax.dot_general(jnp.where(core == 0, low, high), weight[...], over, preferred_element_type=F32)
    return part + lax.dot_general(
        jnp.where(core == 0, high, low), weight_other[...], over, preferred_element_type=F32
    )


def main_kernel(place, grad, weight, weight_other, sent):
    sent[...] = chip_term(place[1], grad, weight, weight_other).astype(BF16)


def gain_kernel(place, grad, seg, ids, weight, weight_other, gain_out, inverse):
    core = place[1]
    step = pl.program_id(0)
    count, _, held, width = seg.shape
    tokens = count * held

    @pl.when(step == 0)
    def _():
        full = seg[...].reshape(tokens, width).astype(F32)
        inv = lax.rsqrt(jnp.mean(full * full, axis=-1, keepdims=True) + EPSILON)
        index = lax.broadcasted_iota(jnp.int32, (tokens, ids.shape[1]), 0)
        index = (index // held * 2 + core) * held + index % held
        found = jnp.max((index == ids[...]).astype(F32), axis=-1, keepdims=True) > 0.0
        inverse[...] = jnp.broadcast_to(jnp.where(found, 0.0, inv), inverse.shape)

    part = chip_term(core, grad, weight, weight_other)
    chunk = part.shape[1]
    unit = seg[:, 0, :, pl.ds(pl.multiple_of(step * chunk, chunk), chunk)].reshape(tokens, chunk).astype(F32)
    gain_out[...] = jnp.sum(part * (unit * inverse[:, :1]), axis=0, keepdims=True)


def logits_kernel(half, mine, other, gain_mine, gain_other, head_mine, head_other, out):
    squares = 0.0
    part = 0.0
    for row, gain, head in ((mine, gain_mine, head_mine), (other, gain_other, head_other)):
        row = row[...].reshape(-1, row.shape[-1]).astype(F32)
        squares += jnp.sum(row * row, axis=-1, keepdims=True)
        part += lax.dot_general(
            (row * gain[...]).astype(BF16), head[...], (((1,), (1,)), ((), ())), preferred_element_type=F32
        )
    column = lax.broadcasted_iota(jnp.int32, part.shape, 1)
    for i, piece in enumerate(pieces3(squares)):
        part = jnp.where(column == half + i, piece, part)
    out[...] = part.astype(BF16).reshape(out.shape)


def softmax_kernel(width, half, vocab, place, parts, targets, expo_out, stats):
    core, start = place[1], place[2]
    total = parts[0].astype(F32)
    for i in range(1, parts.shape[0]):
        total += parts[i].astype(F32)
    inv = lax.rsqrt(jnp.sum(total[:, half : half + 3], axis=-1, keepdims=True) / width + EPSILON)
    logits = total * inv
    column = lax.broadcasted_iota(jnp.int32, logits.shape, 1)
    live = (column < half) & (column + core * half < vocab)
    top = jnp.max(jnp.where(live, logits, -jnp.inf), axis=-1, keepdims=True)
    shifted = jnp.where(live, logits - top, -jnp.inf)
    expo = jnp.exp(shifted)
    expo_out[...] = expo.astype(BF16)
    hit = live & (column == targets[...] - start)
    values = [
        top,
        jnp.sum(expo, axis=-1, keepdims=True),
        jnp.sum(jnp.where(live, expo * shifted, 0.0), axis=-1, keepdims=True),
        jnp.sum(jnp.where(hit, logits, 0.0), axis=-1, keepdims=True),
        inv,
    ]
    lane = lax.broadcasted_iota(jnp.int32, (logits.shape[0], 128), 1)
    table = jnp.zeros(lane.shape, F32)
    for i, value in enumerate(values):
        table = jnp.where(lane == i, value, table)
    table = jnp.concatenate([table, jnp.zeros((128 - table.shape[0], 128), F32)])
    stats[...] = table.T[: stats.shape[0]]


def merged(stats):
    tops, totals, alongs, hits = [stats[:, i] for i in range(4)]
    top = jnp.max(tops, axis=0, keepdims=True)
    lower = jnp.exp(tops - top)
    total = jnp.sum(totals * lower, axis=0, keepdims=True)
    along = jnp.sum((alongs + (tops - top) * totals) * lower, axis=0, keepdims=True)
    return top, total, along, jnp.sum(hits, axis=0, keepdims=True)


def finish_kernel(width, stats, own, weights, known):
    top, total, along, hits = merged(stats[...])
    weight = weights[...]
    factor = weight * (jnp.exp(own[0:1] - top) / total)
    target = weight * (jnp.exp(hits - top) / total - 1.0)
    mean = weight * (along / total - (hits - top)) / width
    rest = jnp.zeros((known.shape[1] - 4, known.shape[2]), F32)
    known[...] = jnp.broadcast_to(jnp.concatenate([factor, target, mean, own[4:5], rest])[None], known.shape)


def logit_grads(half, vocab, which, start, expo, known, targets, grad, kept):
    count, rows, columns = expo.shape
    column = lax.broadcasted_iota(jnp.int32, (rows, columns), 1)
    lane = lax.broadcasted_iota(jnp.int32, (rows, 128), 1)
    live = (column < half) & (column + which * half < vocab)
    for i in range(count):
        table = jnp.concatenate([known[i], jnp.zeros((128 - known.shape[1], 128), F32)]).T[:rows]
        hit = (column + which * half == targets[i * rows : (i + 1) * rows, :] - start) & live
        grad[i] = jnp.where(hit, table[:, 1:2], expo[i].astype(F32) * table[:, 0:1]).astype(BF16)
        if kept is not None:
            kept[i * rows : (i + 1) * rows, :] = jnp.where(lane == 0, table[:, 2:3], table[:, 3:4])
    return grad[...].reshape(count * rows, columns)


def exit_kernel(half, vocab, place, expo, known, targets, head, part, grad, kept):
    rows = logit_grads(half, vocab, place[1], place[2], expo, known, targets, grad, kept)
    part[...] = jnp.dot(rows, head[...], preferred_element_type=F32)


def exit_rest_kernel(half, vocab, place, expo, known, targets, head, before, part, grad):
    rows = logit_grads(half, vocab, 1 - place[1], place[2], expo, known, targets, grad, None)
    total = before[...] + jnp.dot(rows, head[...], preferred_element_type=F32)
    part[...] = total.astype(BF16).reshape(part.shape)


def head_kernel(half, place, mine, gain, kept, dl_mine, dl_other, out):
    core = place[1]
    row = mine[...].reshape(-1, mine.shape[-1]).astype(F32)
    normed = (row * kept[:, 1:2] * gain[...]).astype(BF16)
    over_rows = (((0,), (0,)), ((), ()))
    low = lax.dot_general(
        dl_mine[...].reshape(row.shape[0], -1), normed, over_rows, preferred_element_type=F32
    )
    high = lax.dot_general(
        dl_other[...].reshape(row.shape[0], -1), normed, over_rows, preferred_element_type=F32
    )
    out[:half, :] = jnp.where(core == 0, low, high)[:half].astype(BF16)
    out[half:, :] = jnp.where(core == 0, high, low)[: out.shape[0] - half].astype(BF16)


def row_kernel(place, got, hidden, kept, gain, grad_rows, mine, other, whole):
    core = place[1]
    total = got[0].astype(F32)
    for i in range(1, got.shape[0]):
        total += got[i].astype(F32)
    mean, inv = kept[:, 0:1], kept[:, 1:2]
    back = (total * gain[...] - hidden[...].astype(F32) * inv * mean) * inv
    rows = grad_rows[...] + back
    whole[...] = rows.astype(BF16)
    half = mine.shape[0]
    mine[...] = jnp.where(core == 0, rows[:half], rows[half:])
    other[...] = jnp.where(core == 0, rows[half:], rows[:half])


def send_kernel(place, mine, other, weight, weight_other, unit, gain_part, out):
    core = place[1]
    columns = (((1,), (1,)), ((), ()))
    part = lax.dot_general(mine[...].astype(BF16), weight[...], columns, preferred_element_type=F32)
    part += lax.dot_general(other[...].astype(BF16), weight_other[...], columns, preferred_element_type=F32)
    gain = gain_part[...] + jnp.sum(part * unit[...], axis=0, keepdims=True)
    low = jnp.where(core == 0, mine[...], other[...])
    high = jnp.where(core == 0, other[...], mine[...])
    rows = jnp.concatenate([low, high], axis=1)
    rounded = rows.astype(BF16)
    rest = (rows - rounded.astype(F32)).astype(BF16)
    part = part.astype(BF16)
    gains = [values.astype(BF16) for values in pieces3(gain)]
    count, share, _ = out.shape
    width, slab = weight.shape
    piece = width // (count * share)
    for i in range(count):
        at = slice(i * share, (i + 1) * share)
        out[i, :, :width] = part[at]
        out[i, :, width : width + 2 * slab] = rounded[at]
        out[i, :, width + 2 * slab : width + 4 * slab] = rest[at]
        for j in range(share):
            first = (i * share + j) * piece
            for k in range(3):
                to = width + 4 * slab + k * piece
                out[i, j : j + 1, to : to + piece] = gains[k][:, first : first + piece]


def share_kernel(slabs, got, gain, unit, inv, out):
    total = got[0].astype(F32)
    for i in range(1, got.shape[0]):
        total += got[i].astype(F32)
    width = gain.shape[1]
    residual = jnp.concatenate(
        [
            got[i, :, width : width + slabs].astype(F32) + got[i, :, width + slabs : width + 2 * slabs].astype(F32)
            for i in range(got.shape[0])
        ],
        axis=1,
    )
    unit_grad = total[:, :width] * gain[...]
    centre = jnp.mean(unit_grad * unit[...], axis=-1, keepdims=True)
    rows = residual + (unit_grad - unit[...] * centre) * inv[...]
    gains = total[:, width + 2 * slabs :]
    piece = gains.shape[1] // 3
    gains = gains[:, :piece] + gains[:, piece : 2 * piece] + gains[:, 2 * piece :]
    whole = jnp.concatenate([rows] + pieces3(gains), axis=1)
    out[...] = jnp.broadcast_to(whole.astype(BF16)[None], out.shape)


def last_kernel(ids, main, rows, out):
    step = pl.program_id(0)
    count = out.shape[0]
    out[...] = main[pl.ds(pl.multiple_of(step * count, count), count), :]
    tile = lax.broadcasted_iota(jnp.int32, (16, out.shape[1]), 0)
    for i in range(rows.shape[0]):
        at = ids[i] - step * count

        @pl.when((at >= 0) & (at < count))
        def _():
            start = pl.multiple_of(at // 16 * 16, 16)
            out[pl.ds(start, 16), :] = jnp.where(tile == at - start, rows[i : i + 1, :], out[pl.ds(start, 16), :])


def local(
    segment_in,
    layer_weight,
    layer_gain,
    final_gain,
    head_weight,
    exit_rows,
    exit_count,
    exit_targets,
    exit_scale,
    out_grad,
):
    pipe = lax.axis_index("pipe")
    core = lax.axis_index("core")
    z = lax.axis_index("z")
    pipes = lax.axis_size("pipe")
    zs = lax.axis_size("z")
    block = z * 2 + core
    seg = segment_in[0]
    weight = layer_weight[0]
    gain = layer_gain[0]
    grad = out_grad[0]
    tokens, width = seg.shape
    slab = weight.shape[1]
    exits = exit_rows.shape[1]
    rows_all = pipes * exits
    vocab_part = head_weight.shape[0]
    half = -(-vocab_part // 32) * 16
    padded = -(-(half + 3) // 128) * 128
    place = jnp.stack([z, core, pipe * vocab_part, block]).astype(jnp.int32)
    whole = lambda *dims: pl.BlockSpec(dims, lambda i, *_: (0,) * len(dims))

    weight_other = swap(weight)
    halves = jnp.pad(head_weight, ((0, 2 * half - vocab_part), (0, 0))).reshape(2, half, slab)
    halves = jnp.pad(halves, ((0, 0), (0, padded - half), (0, 0)))
    head_mine = lax.dynamic_index_in_dim(halves, core, 0, keepdims=False)
    head_rest = lax.dynamic_index_in_dim(halves, 1 - core, 0, keepdims=False)
    head_other = swap(head_rest)

    my_rows = exit_rows[pipe]
    pick = (my_rows[:, None] == jnp.arange(tokens, dtype=jnp.int32)[None, :]).astype(BF16)
    row_in = jnp.dot(pick, seg, preferred_element_type=F32)
    row_inv = lax.rsqrt(jnp.mean(row_in * row_in, axis=-1, keepdims=True) + EPSILON)
    row_unit = row_in * row_inv
    row_normed = (row_unit * gain).astype(BF16)
    row_update = lax.reduce_precision(jnp.dot(row_normed, weight, preferred_element_type=F32), 8, 7)
    row_block = lax.dynamic_slice_in_dim(row_in, block * slab, slab, 1)
    hidden = (row_block + row_update).astype(BF16)

    held = tokens // (zs * 2)
    steps = 4
    chunk = width // steps
    grad_spec = pl.BlockSpec((zs, 1, held, 2 * slab), lambda i, at: (0, at[1], 0, at[0]))
    weight_spec = pl.BlockSpec((chunk, slab), lambda i, at: (i, 0))
    grad_view = grad.reshape(zs, 2, held, width)
    main_sent = pl.pallas_call(
        main_kernel,
        grid_spec=pltpu.PrefetchScalarGridSpec(
            num_scalar_prefetch=1,
            grid=(steps,),
            in_specs=[grad_spec, weight_spec, weight_spec],
            out_specs=pl.BlockSpec((zs * held, chunk), lambda i, at: (0, i)),
        ),
        out_shape=shape((zs * held, width), BF16),
        compiler_params=pltpu.CompilerParams(vmem_limit_bytes=LARGE),
    )(place, grad_view, weight, weight_other)
    hidden, main_sent = lax.optimization_barrier((hidden, main_sent))
    main_grad = lax.psum_scatter(main_sent, "z", scatter_dimension=0, tiled=True)

    all_mine = spread(hidden, "pipe", pipes)
    all_other = swap(all_mine)
    gain_mine = lax.dynamic_slice_in_dim(final_gain, block * slab, slab, 0)[None]
    gain_other = lax.dynamic_slice_in_dim(final_gain, (z * 2 + 1 - core) * slab, slab, 0)[None]
    own = rows_all // zs
    part = vmem_call(
        functools.partial(logits_kernel, half),
        shape((zs, own, padded), BF16),
        all_mine,
        all_other,
        gain_mine,
        gain_other,
        head_mine,
        head_other,
    )
    parts = lax.all_to_all(part, "z", 0, 0)

    gain_part = pl.pallas_call(
        gain_kernel,
        grid_spec=pltpu.PrefetchScalarGridSpec(
            num_scalar_prefetch=1,
            grid=(steps,),
            in_specs=[
                grad_spec,
                pl.BlockSpec((zs, 1, held, width), lambda i, at: (0, at[1], 0, 0)),
                whole(1, exits),
                weight_spec,
                weight_spec,
            ],
            out_specs=pl.BlockSpec((1, chunk), lambda i, at: (0, i)),
            scratch_shapes=[pltpu.VMEM((zs * held, 128), F32)],
        ),
        out_shape=shape((1, width), F32),
        compiler_params=pltpu.CompilerParams(vmem_limit_bytes=LARGE),
    )(
        place,
        after(grad, part).reshape(zs, 2, held, width),
        seg.reshape(zs, 2, held, width),
        my_rows[None],
        weight,
        weight_other,
    )
    all_targets = exit_targets.reshape(rows_all, 1)
    targets = lax.dynamic_slice_in_dim(all_targets, z * own, own, 0)
    slot = jnp.arange(exits, dtype=jnp.int32)[None, :]
    weights = jnp.where(slot < exit_count[:, None], exit_scale[:, None], F32(0.0)).reshape(1, rows_all)
    weights = jnp.pad(lax.dynamic_slice_in_dim(weights, z * own, own, 1), ((0, 0), (0, 128 - own)))
    parts, gain_part = lax.optimization_barrier((parts, gain_part))

    expo, stats = kernel_call(
        functools.partial(softmax_kernel, width, half, vocab_part),
        [shape((own, padded), BF16), shape((8, 128), F32)],
        place,
        parts,
        targets - core * half,
    )
    expo, stats, main_grad = lax.optimization_barrier((expo, stats, main_grad))
    ex_mine = lax.all_gather(expo, "z", axis=0)
    stats_other = swap(stats)
    all_stats = spread(jnp.stack([stats, stats_other]), "pipe", pipes).reshape(pipes * 2, 8, 128)
    known_mine = vmem_call(
        functools.partial(finish_kernel, width), shape((zs, 8, 128), F32), all_stats, stats, weights
    )
    known_sent = known_mine
    known_mine = lax.all_to_all(known_mine, "z", 0, 0)
    known_other = swap(known_mine)

    first = block * held
    held_in = lax.dynamic_slice_in_dim(after(seg, stats_other), first, held, 0).astype(F32)
    held_grad = lax.dynamic_slice_in_dim(after(grad, stats_other), first, held, 0).astype(F32)
    held_inv = lax.rsqrt(jnp.mean(held_in * held_in, axis=-1, keepdims=True) + EPSILON)
    held_unit = held_in * held_inv
    unit_grad = main_grad.astype(F32) * gain
    centre = jnp.mean(unit_grad * held_unit, axis=-1, keepdims=True)
    main_out = (held_grad + (unit_grad - held_unit * centre) * held_inv).astype(BF16)
    all_stats, main_out = lax.optimization_barrier((all_stats, main_out))
    inputs = after(seg, known_sent).astype(F32)
    inv_rms = lax.rsqrt(jnp.mean(inputs * inputs, axis=-1, keepdims=True) + EPSILON)
    normed = (inputs * inv_rms * gain).astype(BF16)
    grad_slab = lax.dynamic_slice_in_dim(after(grad, known_sent), block * slab, slab, 1)
    grad_rows = jnp.dot(pick, grad_slab, preferred_element_type=F32)
    core_rows = exits // 2
    share = core_rows // zs
    core_unit = lax.dynamic_slice_in_dim(after(row_unit, known_sent), core * core_rows, core_rows, 0)
    share_at = core * core_rows + z * share
    share_unit = lax.dynamic_slice_in_dim(core_unit, z * share, share, 0)
    share_inv = lax.dynamic_slice_in_dim(row_inv, share_at, share, 0)
    known_mine, normed, grad_rows, core_unit, share_unit, share_inv = lax.optimization_barrier(
        (known_mine, normed, grad_rows, core_unit, share_unit, share_inv)
    )
    ex_mine, main_out = lax.optimization_barrier((after(ex_mine, known_other), main_out))
    main_all = lax.all_gather(main_out, ("z", "core"), axis=0, tiled=True)
    ex_other = swap(ex_mine)

    exit_first, dl_mine, kept = piped_call(
        functools.partial(exit_kernel, half, vocab_part),
        [shape((rows_all, slab), F32), shape((zs, own, padded), BF16), shape((rows_all, 128), F32)],
        place,
        ex_mine,
        known_mine,
        all_targets,
        head_mine,
    )
    exit_part, dl_other = piped_call(
        functools.partial(exit_rest_kernel, half, vocab_part),
        [shape((pipes, exits, slab), BF16), shape((zs, own, padded), BF16)],
        place,
        ex_other,
        known_other,
        all_targets,
        head_rest,
        exit_first,
    )
    exit_got = lax.all_to_all(exit_part, "pipe", 0, 0)
    kept_all = kept
    kept = lax.dynamic_slice_in_dim(kept, pipe * exits, exits, 0)
    exit_got, kept = lax.optimization_barrier((exit_got, kept))
    row_mine, row_send, row_rounded = kernel_call(
        row_kernel,
        [shape((core_rows, slab), F32)] * 2 + [shape((exits, slab), BF16)],
        place,
        exit_got,
        hidden,
        kept,
        gain_mine,
        grad_rows,
    )

    piece = slab * 2 // share
    send = kernel_call(
        send_kernel,
        shape((zs, share, width + 4 * slab + 3 * piece), BF16),
        place,
        row_mine,
        swap(row_send),
        weight,
        weight_other,
        core_unit,
        gain_part,
    )
    got = lax.all_to_all(send, "z", 0, 0)
    put = pick.T
    is_exit = jnp.any(pick > 0, axis=0)
    slab_rounded = jnp.where(
        is_exit[:, None], jnp.dot(put, after(row_rounded, send), preferred_element_type=F32).astype(BF16), grad_slab
    )
    over_rows = (((0,), (0,)), ((), ()))
    weight_grad = lax.dot_general(normed, slab_rounded, over_rows, preferred_element_type=F32).astype(BF16)
    got, weight_grad = lax.optimization_barrier((got, weight_grad))
    last = vmem_call(
        functools.partial(share_kernel, 2 * slab),
        shape((zs, share, width + 3 * piece), BF16),
        got,
        gain[None],
        share_unit,
        share_inv,
    )
    last, main_all = lax.optimization_barrier((last, main_all))
    head_grad = piped_call(
        functools.partial(head_kernel, half),
        shape((vocab_part, slab), BF16),
        place,
        all_mine,
        gain_mine,
        after(kept_all, last),
        dl_mine,
        dl_other,
        limit=SMALL,
    )
    last = lax.all_to_all(last, "z", 0, 0)
    last, head_grad = lax.optimization_barrier((last, head_grad))
    last_other = swap(last)
    gain_grad = jnp.sum(
        (last[:, :, width:].astype(F32) + last_other[:, :, width:].astype(F32)).reshape(zs, share, 3, piece), axis=2
    ).reshape(width)
    row_out = pair(last, last_other, core, 0)[:, :, :width].reshape(exits, width)
    input_grad = pl.pallas_call(
        last_kernel,
        grid=(steps,),
        out_shape=shape((tokens, width), BF16),
        in_specs=[pl.BlockSpec(memory_space=pltpu.SMEM)] + [pl.BlockSpec(memory_space=pltpu.VMEM)] * 2,
        out_specs=pl.BlockSpec((tokens // steps, width), lambda i: (i, 0)),
        compiler_params=pltpu.CompilerParams(vmem_limit_bytes=SMALL),
    )(my_rows, main_all, row_out)
    return (input_grad[None], weight_grad[None], gain_grad[None], head_grad)


def solution(mesh):
    pipes, tensors = mesh.devices.shape
    fine = Mesh(mesh.devices.reshape(pipes, tensors // 2, 2), ("pipe", "z", "core"))
    tensor = ("z", "core")
    in_specs = (
        P("pipe", None, None),
        P("pipe", None, tensor),
        P("pipe", None),
        P(),
        P("pipe", tensor),
        P(),
        P(),
        P(),
        P(),
        P("pipe", None, None),
    )
    out_specs = (
        P("pipe", None, None),
        P("pipe", None, tensor),
        P("pipe", None),
        P("pipe", tensor),
    )
    return jax.shard_map(local, mesh=fine, in_specs=in_specs, out_specs=out_specs, check_vma=False)
```

```python
import functools

import jax
import jax.numpy as jnp
from jax import lax
from jax.experimental import pallas as pl
from jax.experimental.pallas import tpu as pltpu
from jax.sharding import Mesh, PartitionSpec as P

F32 = jnp.float32
BF16 = jnp.bfloat16
EPSILON = 1e-05
SMALL = 20 * 1024 * 1024
VMEM = 32 * 1024 * 1024
LARGE = 56 * 1024 * 1024


def spread(values, axis, count):
    return lax.all_to_all(jnp.broadcast_to(values[None], (count,) + values.shape), axis, 0, 0)


def swap(values):
    return lax.ppermute(values, "core", [(0, 1), (1, 0)])


def kernel_call(body, out, *operands):
    return pl.pallas_call(
        body,
        out_shape=out,
        in_specs=[
            pl.BlockSpec(memory_space=pltpu.SMEM if i == 0 else pltpu.VMEM) for i in range(len(operands))
        ],
        out_specs=jax.tree.map(lambda _: pl.BlockSpec(memory_space=pltpu.VMEM), out),
        compiler_params=pltpu.CompilerParams(vmem_limit_bytes=VMEM),
    )(*operands)


def vmem_call(body, out, *operands):
    return pl.pallas_call(
        body,
        out_shape=out,
        compiler_params=pltpu.CompilerParams(vmem_limit_bytes=VMEM),
    )(*operands)


def piped_call(body, out, *operands, held=(), scratch=(), limit=LARGE):
    specs = [pl.BlockSpec(memory_space=pltpu.SMEM)] + [
        pl.BlockSpec(memory_space=pltpu.VMEM)
        if i in held
        else pl.BlockSpec(value.shape, lambda i, n=value.ndim: (0,) * n)
        for i, value in enumerate(operands[1:], 1)
    ]
    return pl.pallas_call(
        body,
        grid=(1,),
        out_shape=out,
        in_specs=specs,
        out_specs=jax.tree.map(lambda value: pl.BlockSpec(value.shape, lambda i, n=len(value.shape): (0,) * n), out),
        scratch_shapes=list(scratch),
        compiler_params=pltpu.CompilerParams(vmem_limit_bytes=limit),
    )(*operands)


def shape(dims, dtype):
    return jax.ShapeDtypeStruct(dims, dtype)


def after(values, done):
    return lax.optimization_barrier((values, done))[0]


def pieces3(values):
    first = values.astype(BF16).astype(F32)
    rest = values - first
    second = rest.astype(BF16).astype(F32)
    return [first, second, rest - second]


def chip_term(core, grad, weight, weight_other):
    count, _, held, columns = grad.shape
    slab = columns // 2
    over = (((1,), (1,)), ((), ()))
    low = grad[:, 0, :, :slab].reshape(count * held, slab)
    high = grad[:, 0, :, slab:].reshape(count * held, slab)
    part = lax.dot_general(jnp.where(core == 0, low, high), weight[...], over, preferred_element_type=F32)
    return part + lax.dot_general(
        jnp.where(core == 0, high, low), weight_other[...], over, preferred_element_type=F32
    )


def main_kernel(place, grad, weight, weight_other, sent):
    sent[...] = chip_term(place[1], grad, weight, weight_other).astype(BF16)


def gain_kernel(place, grad, seg, ids, weight, weight_other, gain_out, inverse):
    core = place[1]
    step = pl.program_id(0)
    count, _, held, width = seg.shape
    tokens = count * held

    @pl.when(step == 0)
    def _():
        full = seg[...].reshape(tokens, width).astype(F32)
        inv = lax.rsqrt(jnp.mean(full * full, axis=-1, keepdims=True) + EPSILON)
        index = lax.broadcasted_iota(jnp.int32, (tokens, ids.shape[1]), 0)
        index = (index // held * 2 + core) * held + index % held
        found = jnp.max((index == ids[...]).astype(F32), axis=-1, keepdims=True) > 0.0
        inverse[...] = jnp.broadcast_to(jnp.where(found, 0.0, inv), inverse.shape)

    part = chip_term(core, grad, weight, weight_other)
    chunk = part.shape[1]
    unit = seg[:, 0, :, pl.ds(pl.multiple_of(step * chunk, chunk), chunk)].reshape(tokens, chunk).astype(F32)
    gain_out[...] = jnp.sum(part * (unit * inverse[:, :1]), axis=0, keepdims=True)


def logits_kernel(half, mine, other, gain_mine, gain_other, head_mine, head_other, out):
    squares = 0.0
    part = 0.0
    for row, gain, head in ((mine, gain_mine, head_mine), (other, gain_other, head_other)):
        row = row[...].reshape(-1, row.shape[-1]).astype(F32)
        squares += jnp.sum(row * row, axis=-1, keepdims=True)
        part += lax.dot_general(
            (row * gain[...]).astype(BF16), head[...], (((1,), (1,)), ((), ())), preferred_element_type=F32
        )
    column = lax.broadcasted_iota(jnp.int32, part.shape, 1)
    for i, piece in enumerate(pieces3(squares)):
        part = jnp.where(column == half + i, piece, part)
    out[...] = part.astype(BF16).reshape(out.shape)


def softmax_kernel(width, half, vocab, place, parts, targets, expo_out, stats):
    core, start = place[1], place[2]
    total = parts[0].astype(F32)
    for i in range(1, parts.shape[0]):
        total += parts[i].astype(F32)
    inv = lax.rsqrt(jnp.sum(total[:, half : half + 3], axis=-1, keepdims=True) / width + EPSILON)
    logits = total * inv
    column = lax.broadcasted_iota(jnp.int32, logits.shape, 1)
    live = (column < half) & (column + core * half < vocab)
    top = jnp.max(jnp.where(live, logits, -jnp.inf), axis=-1, keepdims=True)
    shifted = jnp.where(live, logits - top, -jnp.inf)
    expo = jnp.exp(shifted)
    expo_out[...] = expo.astype(BF16)
    hit = live & (column == targets[...] - start)
    values = [
        top,
        jnp.sum(expo, axis=-1, keepdims=True),
        jnp.sum(jnp.where(live, expo * shifted, 0.0), axis=-1, keepdims=True),
        jnp.sum(jnp.where(hit, logits, 0.0), axis=-1, keepdims=True),
        inv,
    ]
    lane = lax.broadcasted_iota(jnp.int32, (logits.shape[0], 128), 1)
    table = jnp.zeros(lane.shape, F32)
    for i, value in enumerate(values):
        table = jnp.where(lane == i, value, table)
    table = jnp.concatenate([table, jnp.zeros((128 - table.shape[0], 128), F32)])
    stats[...] = table.T[: stats.shape[0]]


def merged(stats):
    tops, totals, alongs, hits = [stats[:, i] for i in range(4)]
    top = jnp.max(tops, axis=0, keepdims=True)
    lower = jnp.exp(tops - top)
    total = jnp.sum(totals * lower, axis=0, keepdims=True)
    along = jnp.sum((alongs + (tops - top) * totals) * lower, axis=0, keepdims=True)
    return top, total, along, jnp.sum(hits, axis=0, keepdims=True)


def finish_kernel(width, stats, own, weights, known):
    top, total, along, hits = merged(stats[...])
    weight = weights[...]
    factor = weight * (jnp.exp(own[0:1] - top) / total)
    target = weight * (jnp.exp(hits - top) / total - 1.0)
    mean = weight * (along / total - (hits - top)) / width
    rest = jnp.zeros((known.shape[1] - 4, known.shape[2]), F32)
    known[...] = jnp.broadcast_to(jnp.concatenate([factor, target, mean, own[4:5], rest])[None], known.shape)


def logit_grads(half, vocab, which, start, expo, known, targets, grad, kept):
    count, rows, columns = expo.shape
    column = lax.broadcasted_iota(jnp.int32, (rows, columns), 1)
    lane = lax.broadcasted_iota(jnp.int32, (rows, 128), 1)
    live = (column < half) & (column + which * half < vocab)
    for i in range(count):
        table = jnp.concatenate([known[i], jnp.zeros((128 - known.shape[1], 128), F32)]).T[:rows]
        hit = (column + which * half == targets[i * rows : (i + 1) * rows, :] - start) & live
        grad[i] = jnp.where(hit, table[:, 1:2], expo[i].astype(F32) * table[:, 0:1]).astype(BF16)
        if kept is not None:
            kept[i * rows : (i + 1) * rows, :] = jnp.where(lane == 0, table[:, 2:3], table[:, 3:4])
    return grad[...].reshape(count * rows, columns)


def exit_kernel(half, vocab, place, expo, known, targets, head, part, kept, grad):
    rows = logit_grads(half, vocab, place[1], place[2], expo, known, targets, grad, kept)
    part[...] = jnp.dot(rows, head[...], preferred_element_type=F32)


def exit_rest_kernel(half, vocab, place, expo, known, targets, head, before, part, grad):
    rows = logit_grads(half, vocab, 1 - place[1], place[2], expo, known, targets, grad, None)
    total = before[...] + jnp.dot(rows, head[...], preferred_element_type=F32)
    part[...] = total.astype(BF16).reshape(part.shape)


def head_kernel(half, vocab, place, row, gain, kept, targets, ex_mine, ex_other, known_mine, known_other, out, grad):
    core, start = place[1], place[2]
    row = row[...].reshape(-1, row.shape[-1]).astype(F32)
    normed = (row * kept[:, 1:2] * gain[...]).astype(BF16)
    over_rows = (((0,), (0,)), ((), ()))
    parts = []
    for which, expo, known in ((core, ex_mine, known_mine), (1 - core, ex_other, known_other)):
        rows = logit_grads(half, vocab, which, start, expo, known, targets, grad, None)
        parts.append(lax.dot_general(rows, normed, over_rows, preferred_element_type=F32))
    low, high = parts
    out[:half, :] = jnp.where(core == 0, low, high)[:half].astype(BF16)
    out[half:, :] = jnp.where(core == 0, high, low)[: out.shape[0] - half].astype(BF16)


def row_kernel(place, got, hidden, kept, gain, grad_rows, mine, other, whole):
    core = place[1]
    total = got[0].astype(F32)
    for i in range(1, got.shape[0]):
        total += got[i].astype(F32)
    mean, inv = kept[:, 0:1], kept[:, 1:2]
    back = (total * gain[...] - hidden[...].astype(F32) * inv * mean) * inv
    rows = grad_rows[...] + back
    whole[...] = rows.astype(BF16)
    half = mine.shape[0]
    mine[...] = jnp.where(core == 0, rows[:half], rows[half:])
    other[...] = jnp.where(core == 0, rows[half:], rows[:half])


def send_kernel(place, mine, other, weight, weight_other, unit, gain_part, out):
    core = place[1]
    columns = (((1,), (1,)), ((), ()))
    part = lax.dot_general(mine[...].astype(BF16), weight[...], columns, preferred_element_type=F32)
    part += lax.dot_general(other[...].astype(BF16), weight_other[...], columns, preferred_element_type=F32)
    gain = gain_part[...] + jnp.sum(part * unit[...], axis=0, keepdims=True)
    low = jnp.where(core == 0, mine[...], other[...])
    high = jnp.where(core == 0, other[...], mine[...])
    rows = jnp.concatenate([low, high], axis=1)
    rounded = rows.astype(BF16)
    rest = (rows - rounded.astype(F32)).astype(BF16)
    part = part.astype(BF16)
    gains = [values.astype(BF16) for values in pieces3(gain)]
    count, share, _ = out.shape
    width, slab = weight.shape
    piece = width // (count * share)
    for i in range(count):
        at = slice(i * share, (i + 1) * share)
        out[i, :, :width] = part[at]
        out[i, :, width : width + 2 * slab] = rounded[at]
        out[i, :, width + 2 * slab : width + 4 * slab] = rest[at]
        for j in range(share):
            first = (i * share + j) * piece
            for k in range(3):
                to = width + 4 * slab + k * piece
                out[i, j : j + 1, to : to + piece] = gains[k][:, first : first + piece]


def share_kernel(slabs, got, gain, unit, inv, out):
    total = got[0].astype(F32)
    for i in range(1, got.shape[0]):
        total += got[i].astype(F32)
    width = gain.shape[1]
    residual = jnp.concatenate(
        [
            got[i, :, width : width + slabs].astype(F32) + got[i, :, width + slabs : width + 2 * slabs].astype(F32)
            for i in range(got.shape[0])
        ],
        axis=1,
    )
    unit_grad = total[:, :width] * gain[...]
    centre = jnp.mean(unit_grad * unit[...], axis=-1, keepdims=True)
    rows = residual + (unit_grad - unit[...] * centre) * inv[...]
    gains = total[:, width + 2 * slabs :]
    piece = gains.shape[1] // 3
    gains = gains[:, :piece] + gains[:, piece : 2 * piece] + gains[:, 2 * piece :]
    whole = jnp.concatenate([rows] + pieces3(gains), axis=1)
    out[...] = jnp.broadcast_to(whole.astype(BF16)[None], out.shape)


def last_kernel(parts, place, ids, mine, other, main, out, gain_out, block, into, outof):
    core = place[1]
    tokens, width = block.shape
    count = tokens // parts

    def copies(source, target, done):
        return [
            pltpu.make_async_copy(
                source.at[pl.ds(i * count, count)], target.at[pl.ds(i * count, count)], done.at[i]
            )
            for i in range(parts)
        ]

    loads = copies(main, block, into)
    stores = copies(block, out, outof)
    for load in loads:
        load.start()
    groups, share = mine.shape[:2]
    piece = (mine.shape[2] - width) // 3
    total = mine[:, :, width:].astype(F32) + other[:, :, width:].astype(F32)
    total = total[:, :, :piece] + total[:, :, piece : 2 * piece] + total[:, :, 2 * piece :]
    for i in range(groups):
        for j in range(share):
            at = (i * share + j) * piece
            gain_out[:, at : at + piece] = total[i, j : j + 1]
    tile = lax.broadcasted_iota(jnp.int32, (16, width), 0)
    for k in range(parts):
        loads[k].wait()
        for rows, first in ((mine, core), (other, 1 - core)):
            for i in range(groups):
                for j in range(share):
                    at = ids[first * groups * share + i * share + j]

                    @pl.when(at // count == k)
                    def _():
                        start = pl.multiple_of(at // 16 * 16, 16)
                        row = rows[i, j : j + 1, :width]
                        block[pl.ds(start, 16), :] = jnp.where(tile == at - start, row, block[pl.ds(start, 16), :])

        stores[k].start()
    for store in stores:
        store.wait()


def local(
    segment_in,
    layer_weight,
    layer_gain,
    final_gain,
    head_weight,
    exit_rows,
    exit_count,
    exit_targets,
    exit_scale,
    out_grad,
):
    pipe = lax.axis_index("pipe")
    core = lax.axis_index("core")
    z = lax.axis_index("z")
    pipes = lax.axis_size("pipe")
    zs = lax.axis_size("z")
    block = z * 2 + core
    seg = segment_in[0]
    weight = layer_weight[0]
    gain = layer_gain[0]
    grad = out_grad[0]
    tokens, width = seg.shape
    slab = weight.shape[1]
    exits = exit_rows.shape[1]
    rows_all = pipes * exits
    vocab_part = head_weight.shape[0]
    half = -(-vocab_part // 32) * 16
    padded = -(-(half + 3) // 128) * 128
    place = jnp.stack([z, core, pipe * vocab_part, block]).astype(jnp.int32)
    whole = lambda *dims: pl.BlockSpec(dims, lambda i, *_: (0,) * len(dims))

    weight_other = swap(weight)
    halves = jnp.pad(head_weight, ((0, 2 * half - vocab_part), (0, 0))).reshape(2, half, slab)
    halves = jnp.pad(halves, ((0, 0), (0, padded - half), (0, 0)))
    head_mine = lax.dynamic_index_in_dim(halves, core, 0, keepdims=False)
    head_rest = lax.dynamic_index_in_dim(halves, 1 - core, 0, keepdims=False)
    head_other = swap(head_rest)

    my_rows = exit_rows[pipe]
    pick = (my_rows[:, None] == jnp.arange(tokens, dtype=jnp.int32)[None, :]).astype(BF16)
    row_in = jnp.dot(pick, seg, preferred_element_type=F32)
    row_inv = lax.rsqrt(jnp.mean(row_in * row_in, axis=-1, keepdims=True) + EPSILON)
    row_unit = row_in * row_inv
    row_normed = (row_unit * gain).astype(BF16)
    row_update = lax.reduce_precision(jnp.dot(row_normed, weight, preferred_element_type=F32), 8, 7)
    row_block = lax.dynamic_slice_in_dim(row_in, block * slab, slab, 1)
    hidden = (row_block + row_update).astype(BF16)

    held = tokens // (zs * 2)
    steps = 4
    chunk = width // steps
    grad_spec = pl.BlockSpec((zs, 1, held, 2 * slab), lambda i, at: (0, at[1], 0, at[0]))
    weight_spec = pl.BlockSpec((chunk, slab), lambda i, at: (i, 0))
    grad_view = grad.reshape(zs, 2, held, width)
    main_sent = pl.pallas_call(
        main_kernel,
        grid_spec=pltpu.PrefetchScalarGridSpec(
            num_scalar_prefetch=1,
            grid=(steps,),
            in_specs=[grad_spec, weight_spec, weight_spec],
            out_specs=pl.BlockSpec((zs * held, chunk), lambda i, at: (0, i)),
        ),
        out_shape=shape((zs * held, width), BF16),
        compiler_params=pltpu.CompilerParams(vmem_limit_bytes=LARGE),
    )(place, grad_view, weight, weight_other)
    hidden, main_sent = lax.optimization_barrier((hidden, main_sent))
    main_grad = lax.psum_scatter(main_sent, "z", scatter_dimension=0, tiled=True)

    all_mine = spread(hidden, "pipe", pipes)
    all_other = swap(all_mine)
    gain_mine = lax.dynamic_slice_in_dim(final_gain, block * slab, slab, 0)[None]
    gain_other = lax.dynamic_slice_in_dim(final_gain, (z * 2 + 1 - core) * slab, slab, 0)[None]
    own = rows_all // zs
    part = vmem_call(
        functools.partial(logits_kernel, half),
        shape((zs, own, padded), BF16),
        all_mine,
        all_other,
        gain_mine,
        gain_other,
        head_mine,
        head_other,
    )
    parts = lax.all_to_all(part, "z", 0, 0)

    gain_part = pl.pallas_call(
        gain_kernel,
        grid_spec=pltpu.PrefetchScalarGridSpec(
            num_scalar_prefetch=1,
            grid=(steps,),
            in_specs=[
                grad_spec,
                pl.BlockSpec((zs, 1, held, width), lambda i, at: (0, at[1], 0, 0)),
                whole(1, exits),
                weight_spec,
                weight_spec,
            ],
            out_specs=pl.BlockSpec((1, chunk), lambda i, at: (0, i)),
            scratch_shapes=[pltpu.VMEM((zs * held, 128), F32)],
        ),
        out_shape=shape((1, width), F32),
        compiler_params=pltpu.CompilerParams(vmem_limit_bytes=LARGE),
    )(
        place,
        after(grad, part).reshape(zs, 2, held, width),
        seg.reshape(zs, 2, held, width),
        my_rows[None],
        weight,
        weight_other,
    )
    all_targets = exit_targets.reshape(rows_all, 1)
    targets = lax.dynamic_slice_in_dim(all_targets, z * own, own, 0)
    slot = jnp.arange(exits, dtype=jnp.int32)[None, :]
    weights = jnp.where(slot < exit_count[:, None], exit_scale[:, None], F32(0.0)).reshape(1, rows_all)
    weights = jnp.pad(lax.dynamic_slice_in_dim(weights, z * own, own, 1), ((0, 0), (0, 128 - own)))
    parts, gain_part = lax.optimization_barrier((parts, gain_part))

    expo, stats = kernel_call(
        functools.partial(softmax_kernel, width, half, vocab_part),
        [shape((own, padded), BF16), shape((8, 128), F32)],
        place,
        parts,
        targets - core * half,
    )
    expo, stats, main_grad = lax.optimization_barrier((expo, stats, main_grad))
    ex_mine = lax.all_gather(expo, "z", axis=0)
    stats_other = swap(stats)
    all_stats = spread(jnp.stack([stats, stats_other]), "pipe", pipes).reshape(pipes * 2, 8, 128)
    known_mine = vmem_call(
        functools.partial(finish_kernel, width), shape((zs, 8, 128), F32), all_stats, stats, weights
    )
    known_sent = known_mine
    known_mine = lax.all_to_all(known_mine, "z", 0, 0)

    first = block * held
    held_in = lax.dynamic_slice_in_dim(after(seg, stats_other), first, held, 0).astype(F32)
    held_grad = lax.dynamic_slice_in_dim(after(grad, stats_other), first, held, 0).astype(F32)
    held_inv = lax.rsqrt(jnp.mean(held_in * held_in, axis=-1, keepdims=True) + EPSILON)
    held_unit = held_in * held_inv
    unit_grad = main_grad.astype(F32) * gain
    centre = jnp.mean(unit_grad * held_unit, axis=-1, keepdims=True)
    main_out = (held_grad + (unit_grad - held_unit * centre) * held_inv).astype(BF16)
    all_stats, main_out = lax.optimization_barrier((all_stats, main_out))
    inputs = after(seg, known_sent).astype(F32)
    inv_rms = lax.rsqrt(jnp.mean(inputs * inputs, axis=-1, keepdims=True) + EPSILON)
    normed = (inputs * inv_rms * gain).astype(BF16)
    grad_slab = lax.dynamic_slice_in_dim(after(grad, known_sent), block * slab, slab, 1)
    grad_rows = jnp.dot(pick, grad_slab, preferred_element_type=F32)
    core_rows = exits // 2
    share = core_rows // zs
    core_unit = lax.dynamic_slice_in_dim(after(row_unit, known_sent), core * core_rows, core_rows, 0)
    share_at = core * core_rows + z * share
    share_unit = lax.dynamic_slice_in_dim(core_unit, z * share, share, 0)
    share_inv = lax.dynamic_slice_in_dim(row_inv, share_at, share, 0)
    known_mine, normed, grad_rows, core_unit, share_unit, share_inv = lax.optimization_barrier(
        (known_mine, normed, grad_rows, core_unit, share_unit, share_inv)
    )
    known_other = swap(known_mine)
    ex_mine, main_out = lax.optimization_barrier((after(ex_mine, known_other), main_out))
    main_all = lax.all_gather(main_out, ("z", "core"), axis=0, tiled=True)
    ex_other = swap(ex_mine)

    grads = [pltpu.VMEM((zs, own, padded), BF16)]
    exit_first, kept = piped_call(
        functools.partial(exit_kernel, half, vocab_part),
        [shape((rows_all, slab), F32), shape((rows_all, 128), F32)],
        place,
        ex_mine,
        known_mine,
        all_targets,
        head_mine,
        scratch=grads,
    )
    exit_part = piped_call(
        functools.partial(exit_rest_kernel, half, vocab_part),
        shape((pipes, exits, slab), BF16),
        place,
        ex_other,
        known_other,
        all_targets,
        head_rest,
        exit_first,
        held=(1, 5),
        scratch=grads,
    )
    exit_got = lax.all_to_all(exit_part, "pipe", 0, 0)
    kept_all = kept
    kept = lax.dynamic_slice_in_dim(kept, pipe * exits, exits, 0)
    exit_got, kept = lax.optimization_barrier((exit_got, kept))
    row_mine, row_send, row_rounded = kernel_call(
        row_kernel,
        [shape((core_rows, slab), F32)] * 2 + [shape((exits, slab), BF16)],
        place,
        exit_got,
        hidden,
        kept,
        gain_mine,
        grad_rows,
    )

    piece = slab * 2 // share
    send = kernel_call(
        send_kernel,
        shape((zs, share, width + 4 * slab + 3 * piece), BF16),
        place,
        row_mine,
        swap(row_send),
        weight,
        weight_other,
        core_unit,
        gain_part,
    )
    got = lax.all_to_all(send, "z", 0, 0)
    put = pick.T
    is_exit = jnp.any(pick > 0, axis=0)
    slab_rounded = jnp.where(
        is_exit[:, None], jnp.dot(put, after(row_rounded, send), preferred_element_type=F32).astype(BF16), grad_slab
    )
    over_rows = (((0,), (0,)), ((), ()))
    weight_grad = lax.dot_general(normed, slab_rounded, over_rows, preferred_element_type=F32).astype(BF16)
    got, weight_grad = lax.optimization_barrier((got, weight_grad))
    last = vmem_call(
        functools.partial(share_kernel, 2 * slab),
        shape((zs, share, width + 3 * piece), BF16),
        got,
        gain[None],
        share_unit,
        share_inv,
    )
    last, main_all = lax.optimization_barrier((last, main_all))
    head_grad = piped_call(
        functools.partial(head_kernel, half, vocab_part),
        shape((vocab_part, slab), BF16),
        place,
        all_mine,
        gain_mine,
        after(kept_all, last),
        all_targets,
        ex_mine,
        ex_other,
        known_mine,
        known_other,
        scratch=grads,
    )
    last = lax.all_to_all(last, "z", 0, 0)
    last, head_grad = lax.optimization_barrier((last, head_grad))
    last_other = swap(last)
    parts = 4
    input_grad, gain_grad = pl.pallas_call(
        functools.partial(last_kernel, parts),
        in_specs=[pl.BlockSpec(memory_space=pltpu.SMEM)] * 2
        + [pl.BlockSpec(memory_space=pltpu.VMEM)] * 2
        + [pl.BlockSpec(memory_space=pl.ANY)],
        out_specs=[pl.BlockSpec(memory_space=pl.ANY), pl.BlockSpec(memory_space=pltpu.VMEM)],
        out_shape=[shape((tokens, width), BF16), shape((1, width), F32)],
        scratch_shapes=[
            pltpu.VMEM((tokens, width), BF16),
            pltpu.SemaphoreType.DMA((parts,)),
            pltpu.SemaphoreType.DMA((parts,)),
        ],
        compiler_params=pltpu.CompilerParams(vmem_limit_bytes=LARGE),
    )(place, my_rows, last, last_other, main_all)
    return (input_grad[None], weight_grad[None], gain_grad, head_grad)


def solution(mesh):
    pipes, tensors = mesh.devices.shape
    fine = Mesh(mesh.devices.reshape(pipes, tensors // 2, 2), ("pipe", "z", "core"))
    tensor = ("z", "core")
    in_specs = (
        P("pipe", None, None),
        P("pipe", None, tensor),
        P("pipe", None),
        P(),
        P("pipe", tensor),
        P(),
        P(),
        P(),
        P(),
        P("pipe", None, None),
    )
    out_specs = (
        P("pipe", None, None),
        P("pipe", None, tensor),
        P("pipe", None),
        P("pipe", tensor),
    )
    return jax.shard_map(local, mesh=fine, in_specs=in_specs, out_specs=out_specs, check_vma=False)
```

```python
import functools

import jax
import jax.numpy as jnp
from jax import lax
from jax.experimental import pallas as pl
from jax.experimental.pallas import tpu as pltpu
from jax.sharding import Mesh, PartitionSpec as P

F32 = jnp.float32
BF16 = jnp.bfloat16
EPSILON = 1e-05
SMALL = 20 * 1024 * 1024
VMEM = 32 * 1024 * 1024
LARGE = 56 * 1024 * 1024


def spread(values, axis, count):
    return lax.all_to_all(jnp.broadcast_to(values[None], (count,) + values.shape), axis, 0, 0)


def swap(values):
    return lax.ppermute(values, "core", [(0, 1), (1, 0)])


def kernel_call(body, out, *operands):
    return pl.pallas_call(
        body,
        out_shape=out,
        in_specs=[
            pl.BlockSpec(memory_space=pltpu.SMEM if i == 0 else pltpu.VMEM) for i in range(len(operands))
        ],
        out_specs=jax.tree.map(lambda _: pl.BlockSpec(memory_space=pltpu.VMEM), out),
        compiler_params=pltpu.CompilerParams(vmem_limit_bytes=VMEM),
    )(*operands)


def vmem_call(body, out, *operands):
    return pl.pallas_call(
        body,
        out_shape=out,
        compiler_params=pltpu.CompilerParams(vmem_limit_bytes=VMEM),
    )(*operands)


def piped_call(body, out, *operands, held=(), kept=(), scratch=(), limit=LARGE):
    def spec(value, stays):
        if stays:
            return pl.BlockSpec(memory_space=pltpu.VMEM)
        return pl.BlockSpec(value.shape, lambda i: (0,) * len(value.shape))

    return pl.pallas_call(
        body,
        grid=(1,),
        out_shape=out,
        in_specs=[pl.BlockSpec(memory_space=pltpu.SMEM)]
        + [spec(value, i in held) for i, value in enumerate(operands[1:], 1)],
        out_specs=[spec(value, i in kept) for i, value in enumerate(out)],
        scratch_shapes=list(scratch),
        compiler_params=pltpu.CompilerParams(vmem_limit_bytes=limit),
    )(*operands)


def shape(dims, dtype):
    return jax.ShapeDtypeStruct(dims, dtype)


def after(values, done):
    return lax.optimization_barrier((values, done))[0]


def pieces3(values):
    first = values.astype(BF16).astype(F32)
    rest = values - first
    second = rest.astype(BF16).astype(F32)
    return [first, second, rest - second]


def chip_term(core, grad, weight, weight_other):
    count, _, held, columns = grad.shape
    slab = columns // 2
    over = (((1,), (1,)), ((), ()))
    low = grad[:, 0, :, :slab].reshape(count * held, slab)
    high = grad[:, 0, :, slab:].reshape(count * held, slab)
    part = lax.dot_general(jnp.where(core == 0, low, high), weight[...], over, preferred_element_type=F32)
    return part + lax.dot_general(
        jnp.where(core == 0, high, low), weight_other[...], over, preferred_element_type=F32
    )


def gain_kernel(place, grad, seg, ids, weight, weight_other, gain_out, inverse):
    core = place[1]
    step = pl.program_id(0)
    count, _, held, width = seg.shape
    tokens = count * held

    @pl.when(step == 0)
    def _():
        full = seg[...].reshape(tokens, width).astype(F32)
        inv = lax.rsqrt(jnp.mean(full * full, axis=-1, keepdims=True) + EPSILON)
        index = lax.broadcasted_iota(jnp.int32, (tokens, ids.shape[1]), 0)
        index = (index // held * 2 + core) * held + index % held
        found = jnp.max((index == ids[...]).astype(F32), axis=-1, keepdims=True) > 0.0
        inverse[...] = jnp.broadcast_to(jnp.where(found, 0.0, inv), inverse.shape)

    part = chip_term(core, grad, weight, weight_other)
    chunk = part.shape[1]
    unit = seg[:, 0, :, pl.ds(pl.multiple_of(step * chunk, chunk), chunk)].reshape(tokens, chunk).astype(F32)
    gain_out[...] = jnp.sum(part * (unit * inverse[:, :1]), axis=0, keepdims=True)


def logits_kernel(half, mine, other, gain_mine, gain_other, head_mine, head_other, out):
    squares = 0.0
    part = 0.0
    for row, gain, head in ((mine, gain_mine, head_mine), (other, gain_other, head_other)):
        row = row[...].reshape(-1, row.shape[-1]).astype(F32)
        squares += jnp.sum(row * row, axis=-1, keepdims=True)
        part += lax.dot_general(
            (row * gain[...]).astype(BF16), head[...], (((1,), (1,)), ((), ())), preferred_element_type=F32
        )
    column = lax.broadcasted_iota(jnp.int32, part.shape, 1)
    for i, piece in enumerate(pieces3(squares)):
        part = jnp.where(column == half + i, piece, part)
    out[...] = part.astype(BF16).reshape(out.shape)


def softmax_kernel(width, half, vocab, place, parts, targets, expo_out, stats):
    core, start = place[1], place[2]
    total = parts[0].astype(F32)
    for i in range(1, parts.shape[0]):
        total += parts[i].astype(F32)
    inv = lax.rsqrt(jnp.sum(total[:, half : half + 3], axis=-1, keepdims=True) / width + EPSILON)
    logits = total * inv
    column = lax.broadcasted_iota(jnp.int32, logits.shape, 1)
    live = (column < half) & (column + core * half < vocab)
    top = jnp.max(jnp.where(live, logits, -jnp.inf), axis=-1, keepdims=True)
    shifted = jnp.where(live, logits - top, -jnp.inf)
    expo = jnp.exp(shifted)
    expo_out[...] = expo.astype(BF16)
    hit = live & (column == targets[...] - start)
    values = [
        top,
        jnp.sum(expo, axis=-1, keepdims=True),
        jnp.sum(jnp.where(live, expo * shifted, 0.0), axis=-1, keepdims=True),
        jnp.sum(jnp.where(hit, logits, 0.0), axis=-1, keepdims=True),
        inv,
    ]
    lane = lax.broadcasted_iota(jnp.int32, (logits.shape[0], 128), 1)
    table = jnp.zeros(lane.shape, F32)
    for i, value in enumerate(values):
        table = jnp.where(lane == i, value, table)
    table = jnp.concatenate([table, jnp.zeros((128 - table.shape[0], 128), F32)])
    stats[...] = table.T[: stats.shape[0]]


def merged(stats):
    tops, totals, alongs, hits = [stats[:, i] for i in range(4)]
    top = jnp.max(tops, axis=0, keepdims=True)
    lower = jnp.exp(tops - top)
    total = jnp.sum(totals * lower, axis=0, keepdims=True)
    along = jnp.sum((alongs + (tops - top) * totals) * lower, axis=0, keepdims=True)
    return top, total, along, jnp.sum(hits, axis=0, keepdims=True)


def finish_kernel(width, stats, own, weights, known):
    top, total, along, hits = merged(stats[...])
    weight = weights[...]
    factor = weight * (jnp.exp(own[0:1] - top) / total)
    target = weight * (jnp.exp(hits - top) / total - 1.0)
    mean = weight * (along / total - (hits - top)) / width
    rest = jnp.zeros((known.shape[1] - 4, known.shape[2]), F32)
    known[...] = jnp.broadcast_to(jnp.concatenate([factor, target, mean, own[4:5], rest])[None], known.shape)


def logit_grads(half, vocab, which, start, expo, known, targets, grad, kept):
    count, rows, columns = expo.shape
    column = lax.broadcasted_iota(jnp.int32, (rows, columns), 1)
    lane = lax.broadcasted_iota(jnp.int32, (rows, 128), 1)
    live = (column < half) & (column + which * half < vocab)
    for i in range(count):
        table = jnp.concatenate([known[i], jnp.zeros((128 - known.shape[1], 128), F32)]).T[:rows]
        hit = (column + which * half == targets[i * rows : (i + 1) * rows, :] - start) & live
        grad[i] = jnp.where(hit, table[:, 1:2], expo[i].astype(F32) * table[:, 0:1]).astype(BF16)
        if kept is not None:
            kept[i * rows : (i + 1) * rows, :] = jnp.where(lane == 0, table[:, 2:3], table[:, 3:4])
    return grad[...].reshape(count * rows, columns)


def exit_kernel(half, vocab, place, expo, known, targets, head, part, kept, grad):
    rows = logit_grads(half, vocab, place[1], place[2], expo, known, targets, grad, kept)
    part[...] = jnp.dot(rows, head[...], preferred_element_type=F32)


def exit_rest_kernel(half, vocab, place, expo, known, targets, head, before, part, grad):
    rows = logit_grads(half, vocab, 1 - place[1], place[2], expo, known, targets, grad, None)
    total = before[...] + jnp.dot(rows, head[...], preferred_element_type=F32)
    part[...] = total.astype(BF16).reshape(part.shape)


def head_kernel(half, vocab, place, row, gain, kept, targets, ex_mine, ex_other, known_mine, known_other, out, grad):
    core, start = place[1], place[2]
    row = row[...].reshape(-1, row.shape[-1]).astype(F32)
    normed = (row * kept[:, 1:2] * gain[...]).astype(BF16)
    over_rows = (((0,), (0,)), ((), ()))
    parts = []
    for which, expo, known in ((core, ex_mine, known_mine), (1 - core, ex_other, known_other)):
        rows = logit_grads(half, vocab, which, start, expo, known, targets, grad, None)
        parts.append(lax.dot_general(rows, normed, over_rows, preferred_element_type=F32))
    low, high = parts
    out[:half, :] = jnp.where(core == 0, low, high)[:half].astype(BF16)
    out[half:, :] = jnp.where(core == 0, high, low)[: out.shape[0] - half].astype(BF16)


def row_kernel(place, got, hidden, kept, gain, grad_rows, mine, other, whole):
    core = place[1]
    total = got[0].astype(F32)
    for i in range(1, got.shape[0]):
        total += got[i].astype(F32)
    mean, inv = kept[:, 0:1], kept[:, 1:2]
    back = (total * gain[...] - hidden[...].astype(F32) * inv * mean) * inv
    rows = grad_rows[...] + back
    whole[...] = rows.astype(BF16)
    half = mine.shape[0]
    mine[...] = jnp.where(core == 0, rows[:half], rows[half:])
    other[...] = jnp.where(core == 0, rows[half:], rows[:half])


def send_kernel(place, part, mine, other, unit, gain_part, out):
    core = place[1]
    part = part[...]
    gain = gain_part[...] + jnp.sum(part * unit[...], axis=0, keepdims=True)
    low = jnp.where(core == 0, mine[...], other[...])
    high = jnp.where(core == 0, other[...], mine[...])
    rows = jnp.concatenate([low, high], axis=1)
    rounded = rows.astype(BF16)
    rest = (rows - rounded.astype(F32)).astype(BF16)
    part = part.astype(BF16)
    gains = [values.astype(BF16) for values in pieces3(gain)]
    count, share, _ = out.shape
    width, slab = part.shape[1], mine.shape[1]
    piece = width // (count * share)
    for i in range(count):
        at = slice(i * share, (i + 1) * share)
        out[i, :, :width] = part[at]
        out[i, :, width : width + 2 * slab] = rounded[at]
        out[i, :, width + 2 * slab : width + 4 * slab] = rest[at]
        for j in range(share):
            first = (i * share + j) * piece
            for k in range(3):
                to = width + 4 * slab + k * piece
                out[i, j : j + 1, to : to + piece] = gains[k][:, first : first + piece]


def share_kernel(slabs, got, gain, unit, inv, out):
    total = got[0].astype(F32)
    for i in range(1, got.shape[0]):
        total += got[i].astype(F32)
    width = gain.shape[1]
    residual = jnp.concatenate(
        [
            got[i, :, width : width + slabs].astype(F32) + got[i, :, width + slabs : width + 2 * slabs].astype(F32)
            for i in range(got.shape[0])
        ],
        axis=1,
    )
    unit_grad = total[:, :width] * gain[...]
    centre = jnp.mean(unit_grad * unit[...], axis=-1, keepdims=True)
    rows = residual + (unit_grad - unit[...] * centre) * inv[...]
    gains = total[:, width + 2 * slabs :]
    piece = gains.shape[1] // 3
    gains = gains[:, :piece] + gains[:, piece : 2 * piece] + gains[:, 2 * piece :]
    whole = jnp.concatenate([rows] + pieces3(gains), axis=1)
    out[...] = jnp.broadcast_to(whole.astype(BF16)[None], out.shape)


def fetch_kernel(source, out, done):
    parts = done.shape[0]
    count = out.shape[0] // parts
    copies = [
        pltpu.make_async_copy(source.at[pl.ds(i * count, count)], out.at[pl.ds(i * count, count)], done.at[i])
        for i in range(parts)
    ]
    for copy in copies:
        copy.start()
    for copy in copies:
        copy.wait()


def last_kernel(place, ids, mine, other, main, out, gain_out, block, done):
    core = place[1]
    tokens, width = block.shape
    groups, share = mine.shape[:2]
    tile = lax.broadcasted_iota(jnp.int32, (16, width), 0)
    for rows, first in ((mine, core), (other, 1 - core)):
        for i in range(groups):
            for j in range(share):
                at = ids[first * groups * share + i * share + j]
                start = pl.multiple_of(at // 16 * 16, 16)
                row = rows[i, j : j + 1, :width]
                block[pl.ds(start, 16), :] = jnp.where(tile == at - start, row, block[pl.ds(start, 16), :])
    parts = done.shape[0]
    count = tokens // parts
    copies = [
        pltpu.make_async_copy(block.at[pl.ds(i * count, count)], out.at[pl.ds(i * count, count)], done.at[i])
        for i in range(parts)
    ]
    for copy in copies:
        copy.start()
    piece = (mine.shape[2] - width) // 3
    total = mine[:, :, width:].astype(F32) + other[:, :, width:].astype(F32)
    total = total[:, :, :piece] + total[:, :, piece : 2 * piece] + total[:, :, 2 * piece :]
    for i in range(groups):
        for j in range(share):
            at = (i * share + j) * piece
            gain_out[:, at : at + piece] = total[i, j : j + 1]
    for copy in copies:
        copy.wait()


def local(
    segment_in,
    layer_weight,
    layer_gain,
    final_gain,
    head_weight,
    exit_rows,
    exit_count,
    exit_targets,
    exit_scale,
    out_grad,
):
    pipe = lax.axis_index("pipe")
    core = lax.axis_index("core")
    z = lax.axis_index("z")
    pipes = lax.axis_size("pipe")
    zs = lax.axis_size("z")
    block = z * 2 + core
    seg = segment_in[0]
    weight = layer_weight[0]
    gain = layer_gain[0]
    grad = out_grad[0]
    tokens, width = seg.shape
    slab = weight.shape[1]
    exits = exit_rows.shape[1]
    rows_all = pipes * exits
    vocab_part = head_weight.shape[0]
    half = -(-vocab_part // 32) * 16
    padded = -(-(half + 3) // 128) * 128
    place = jnp.stack([z, core, pipe * vocab_part, block]).astype(jnp.int32)
    whole = lambda *dims: pl.BlockSpec(dims, lambda i, *_: (0,) * len(dims))

    weight_other = swap(weight)
    halves = jnp.pad(head_weight, ((0, 2 * half - vocab_part), (0, 0))).reshape(2, half, slab)
    halves = jnp.pad(halves, ((0, 0), (0, padded - half), (0, 0)))
    head_mine = lax.dynamic_index_in_dim(halves, core, 0, keepdims=False)
    head_rest = lax.dynamic_index_in_dim(halves, 1 - core, 0, keepdims=False)
    head_other = swap(head_rest)

    my_rows = exit_rows[pipe]
    pick = (my_rows[:, None] == jnp.arange(tokens, dtype=jnp.int32)[None, :]).astype(BF16)
    row_in = jnp.dot(pick, seg, preferred_element_type=F32)
    row_inv = lax.rsqrt(jnp.mean(row_in * row_in, axis=-1, keepdims=True) + EPSILON)
    row_unit = row_in * row_inv
    row_normed = (row_unit * gain).astype(BF16)
    row_update = lax.reduce_precision(jnp.dot(row_normed, weight, preferred_element_type=F32), 8, 7)
    row_block = lax.dynamic_slice_in_dim(row_in, block * slab, slab, 1)
    hidden = (row_block + row_update).astype(BF16)

    held = tokens // (zs * 2)
    steps = 4
    chunk = width // steps
    grad_spec = pl.BlockSpec((zs, 1, held, 2 * slab), lambda i, at: (0, at[1], 0, at[0]))
    weight_spec = pl.BlockSpec((chunk, slab), lambda i, at: (i, 0))
    grad_view = grad.reshape(zs, 2, held, width)
    joined = jnp.concatenate([weight, weight_other], axis=1)
    chip_grad = lax.dynamic_slice(grad_view, (0, core, 0, z * 2 * slab), (zs, 1, held, 2 * slab))
    on_columns = (((1,), (1,)), ((), ()))

    def own_first(values):
        return jnp.where(core == 0, values, jnp.roll(values, slab, axis=1))

    main_sent = lax.dot_general(
        own_first(chip_grad.reshape(zs * held, 2 * slab)), joined, on_columns, preferred_element_type=F32
    ).astype(BF16)
    hidden, main_sent = lax.optimization_barrier((hidden, main_sent))
    main_grad = lax.psum_scatter(main_sent, "z", scatter_dimension=0, tiled=True)

    all_mine = spread(hidden, "pipe", pipes)
    all_other = swap(all_mine)
    gain_mine = lax.dynamic_slice_in_dim(final_gain, block * slab, slab, 0)[None]
    gain_other = lax.dynamic_slice_in_dim(final_gain, (z * 2 + 1 - core) * slab, slab, 0)[None]
    own = rows_all // zs
    part = vmem_call(
        functools.partial(logits_kernel, half),
        shape((zs, own, padded), BF16),
        all_mine,
        all_other,
        gain_mine,
        gain_other,
        head_mine,
        head_other,
    )
    parts = lax.all_to_all(part, "z", 0, 0)

    gain_part = pl.pallas_call(
        gain_kernel,
        grid_spec=pltpu.PrefetchScalarGridSpec(
            num_scalar_prefetch=1,
            grid=(steps,),
            in_specs=[
                grad_spec,
                pl.BlockSpec((zs, 1, held, width), lambda i, at: (0, at[1], 0, 0)),
                whole(1, exits),
                weight_spec,
                weight_spec,
            ],
            out_specs=pl.BlockSpec((1, chunk), lambda i, at: (0, i)),
            scratch_shapes=[pltpu.VMEM((zs * held, 128), F32)],
        ),
        out_shape=shape((1, width), F32),
        compiler_params=pltpu.CompilerParams(vmem_limit_bytes=LARGE),
    )(
        place,
        after(grad, part).reshape(zs, 2, held, width),
        seg.reshape(zs, 2, held, width),
        my_rows[None],
        weight,
        weight_other,
    )
    all_targets = exit_targets.reshape(rows_all, 1)
    targets = lax.dynamic_slice_in_dim(all_targets, z * own, own, 0)
    slot = jnp.arange(exits, dtype=jnp.int32)[None, :]
    weights = jnp.where(slot < exit_count[:, None], exit_scale[:, None], F32(0.0)).reshape(1, rows_all)
    weights = jnp.pad(lax.dynamic_slice_in_dim(weights, z * own, own, 1), ((0, 0), (0, 128 - own)))
    parts, gain_part = lax.optimization_barrier((parts, gain_part))

    expo, stats = kernel_call(
        functools.partial(softmax_kernel, width, half, vocab_part),
        [shape((own, padded), BF16), shape((8, 128), F32)],
        place,
        parts,
        targets - core * half,
    )
    expo, stats, main_grad = lax.optimization_barrier((expo, stats, main_grad))
    ex_mine = lax.all_gather(expo, "z", axis=0)
    stats_other = swap(stats)
    all_stats = spread(jnp.stack([stats, stats_other]), "pipe", pipes).reshape(pipes * 2, 8, 128)
    known_mine = vmem_call(
        functools.partial(finish_kernel, width), shape((zs, 8, 128), F32), all_stats, stats, weights
    )
    known_sent = known_mine
    known_mine = lax.all_to_all(known_mine, "z", 0, 0)

    first = block * held
    held_in = lax.dynamic_slice_in_dim(after(seg, stats_other), first, held, 0).astype(F32)
    held_grad = lax.dynamic_slice_in_dim(after(grad, stats_other), first, held, 0).astype(F32)
    held_inv = lax.rsqrt(jnp.mean(held_in * held_in, axis=-1, keepdims=True) + EPSILON)
    held_unit = held_in * held_inv
    unit_grad = main_grad.astype(F32) * gain
    centre = jnp.mean(unit_grad * held_unit, axis=-1, keepdims=True)
    main_out = (held_grad + (unit_grad - held_unit * centre) * held_inv).astype(BF16)
    all_stats, main_out = lax.optimization_barrier((all_stats, main_out))
    inputs = after(seg, known_sent).astype(F32)
    inv_rms = lax.rsqrt(jnp.mean(inputs * inputs, axis=-1, keepdims=True) + EPSILON)
    normed = (inputs * inv_rms * gain).astype(BF16)
    grad_slab = lax.dynamic_slice_in_dim(after(grad, known_sent), block * slab, slab, 1)
    grad_rows = jnp.dot(pick, grad_slab, preferred_element_type=F32)
    core_rows = exits // 2
    share = core_rows // zs
    core_unit = lax.dynamic_slice_in_dim(after(row_unit, known_sent), core * core_rows, core_rows, 0)
    share_at = core * core_rows + z * share
    share_unit = lax.dynamic_slice_in_dim(core_unit, z * share, share, 0)
    share_inv = lax.dynamic_slice_in_dim(row_inv, share_at, share, 0)
    known_mine, normed, grad_rows, core_unit, share_unit, share_inv = lax.optimization_barrier(
        (known_mine, normed, grad_rows, core_unit, share_unit, share_inv)
    )
    known_other = swap(known_mine)
    ex_mine, main_out = lax.optimization_barrier((after(ex_mine, known_other), main_out))
    main_all = lax.all_gather(main_out, ("z", "core"), axis=0, tiled=True)
    ex_other = swap(ex_mine)

    grads = [pltpu.VMEM((zs, own, padded), BF16)]
    exit_first, kept = piped_call(
        functools.partial(exit_kernel, half, vocab_part),
        [shape((rows_all, slab), F32), shape((rows_all, 128), F32)],
        place,
        ex_mine,
        known_mine,
        all_targets,
        head_mine,
        kept=(0,),
        scratch=grads,
    )
    (exit_part,) = piped_call(
        functools.partial(exit_rest_kernel, half, vocab_part),
        [shape((pipes, exits, slab), BF16)],
        place,
        ex_other,
        known_other,
        all_targets,
        head_rest,
        exit_first,
        held=(1, 5),
        scratch=grads,
    )
    exit_got = lax.all_to_all(exit_part, "pipe", 0, 0)
    kept_all = kept
    kept = lax.dynamic_slice_in_dim(kept, pipe * exits, exits, 0)
    exit_got, kept = lax.optimization_barrier((exit_got, kept))
    row_mine, row_send, row_rounded = kernel_call(
        row_kernel,
        [shape((core_rows, slab), F32)] * 2 + [shape((exits, slab), BF16)],
        place,
        exit_got,
        hidden,
        kept,
        gain_mine,
        grad_rows,
    )

    piece = slab * 2 // share
    row_other = swap(row_send)
    row_part = lax.dot_general(
        jnp.concatenate([row_mine, row_other], axis=1).astype(BF16), joined, on_columns, preferred_element_type=F32
    )
    send = kernel_call(
        send_kernel,
        shape((zs, share, width + 4 * slab + 3 * piece), BF16),
        place,
        row_part,
        row_mine,
        row_other,
        core_unit,
        gain_part,
    )
    got = lax.all_to_all(send, "z", 0, 0)
    put = pick.T
    is_exit = jnp.any(pick > 0, axis=0)
    slab_rounded = jnp.where(
        is_exit[:, None], jnp.dot(put, after(row_rounded, send), preferred_element_type=F32).astype(BF16), grad_slab
    )
    over_rows = (((0,), (0,)), ((), ()))
    weight_grad = lax.dot_general(normed, slab_rounded, over_rows, preferred_element_type=F32).astype(BF16)
    got, weight_grad = lax.optimization_barrier((got, weight_grad))
    last = vmem_call(
        functools.partial(share_kernel, 2 * slab),
        shape((zs, share, width + 3 * piece), BF16),
        got,
        gain[None],
        share_unit,
        share_inv,
    )
    last, main_all = lax.optimization_barrier((last, main_all))
    (head_grad,) = piped_call(
        functools.partial(head_kernel, half, vocab_part),
        [shape((vocab_part, slab), BF16)],
        place,
        all_mine,
        gain_mine,
        after(kept_all, last),
        all_targets,
        ex_mine,
        ex_other,
        known_mine,
        known_other,
        scratch=grads,
    )
    last = lax.all_to_all(last, "z", 0, 0)
    main_near = pl.pallas_call(
        fetch_kernel,
        in_specs=[pl.BlockSpec(memory_space=pl.ANY)],
        out_specs=pl.BlockSpec(memory_space=pltpu.VMEM),
        out_shape=shape((tokens, width), BF16),
        scratch_shapes=[pltpu.SemaphoreType.DMA((4,))],
        compiler_params=pltpu.CompilerParams(vmem_limit_bytes=SMALL),
    )(main_all)
    last, head_grad, main_near = lax.optimization_barrier((last, head_grad, main_near))
    last_other = swap(last)
    in_vmem = pl.BlockSpec(memory_space=pltpu.VMEM)
    input_grad, gain_grad, _ = pl.pallas_call(
        last_kernel,
        in_specs=[pl.BlockSpec(memory_space=pltpu.SMEM)] * 2 + [in_vmem] * 3,
        out_specs=[pl.BlockSpec(memory_space=pl.ANY), in_vmem, in_vmem],
        out_shape=[shape((tokens, width), BF16), shape((1, width), F32), shape((tokens, width), BF16)],
        input_output_aliases={4: 2},
        scratch_shapes=[pltpu.SemaphoreType.DMA((4,))],
        compiler_params=pltpu.CompilerParams(vmem_limit_bytes=SMALL),
    )(place, my_rows, last, last_other, main_near)
    return (input_grad[None], weight_grad[None], gain_grad, head_grad)


def solution(mesh):
    pipes, tensors = mesh.devices.shape
    fine = Mesh(mesh.devices.reshape(pipes, tensors // 2, 2), ("pipe", "z", "core"))
    tensor = ("z", "core")
    in_specs = (
        P("pipe", None, None),
        P("pipe", None, tensor),
        P("pipe", None),
        P(),
        P("pipe", tensor),
        P(),
        P(),
        P(),
        P(),
        P("pipe", None, None),
    )
    out_specs = (
        P("pipe", None, None),
        P("pipe", None, tensor),
        P("pipe", None),
        P("pipe", tensor),
    )
    return jax.shard_map(local, mesh=fine, in_specs=in_specs, out_specs=out_specs, check_vma=False)
```

```python
import functools

import jax
import jax.numpy as jnp
from jax import lax
from jax.experimental import pallas as pl
from jax.experimental.pallas import tpu as pltpu
from jax.sharding import Mesh, PartitionSpec as P

F32 = jnp.float32
BF16 = jnp.bfloat16
EPSILON = 1e-05
SMALL = 20 * 1024 * 1024
VMEM = 32 * 1024 * 1024
LARGE = 56 * 1024 * 1024


def spread(values, axis, count):
    return lax.all_to_all(jnp.broadcast_to(values[None], (count,) + values.shape), axis, 0, 0)


def swap(values):
    return lax.ppermute(values, "core", [(0, 1), (1, 0)])


def kernel_call(body, out, *operands):
    return pl.pallas_call(
        body,
        out_shape=out,
        in_specs=[
            pl.BlockSpec(memory_space=pltpu.SMEM if i == 0 else pltpu.VMEM) for i in range(len(operands))
        ],
        out_specs=jax.tree.map(lambda _: pl.BlockSpec(memory_space=pltpu.VMEM), out),
        compiler_params=pltpu.CompilerParams(vmem_limit_bytes=VMEM),
    )(*operands)


def vmem_call(body, out, *operands):
    return pl.pallas_call(
        body,
        out_shape=out,
        compiler_params=pltpu.CompilerParams(vmem_limit_bytes=VMEM),
    )(*operands)


def piped_call(body, out, *operands, held=(), kept=(), scratch=(), limit=LARGE):
    def spec(value, stays):
        if stays:
            return pl.BlockSpec(memory_space=pltpu.VMEM)
        return pl.BlockSpec(value.shape, lambda i: (0,) * len(value.shape))

    return pl.pallas_call(
        body,
        grid=(1,),
        out_shape=out,
        in_specs=[pl.BlockSpec(memory_space=pltpu.SMEM)]
        + [spec(value, i in held) for i, value in enumerate(operands[1:], 1)],
        out_specs=[spec(value, i in kept) for i, value in enumerate(out)],
        scratch_shapes=list(scratch),
        compiler_params=pltpu.CompilerParams(vmem_limit_bytes=limit),
    )(*operands)


def shape(dims, dtype):
    return jax.ShapeDtypeStruct(dims, dtype)


def after(values, done):
    return lax.optimization_barrier((values, done))[0]


def pieces3(values):
    first = values.astype(BF16).astype(F32)
    rest = values - first
    second = rest.astype(BF16).astype(F32)
    return [first, second, rest - second]


def chip_term(core, grad, weight, weight_other):
    count, _, held, columns = grad.shape
    slab = columns // 2
    over = (((1,), (1,)), ((), ()))
    low = grad[:, 0, :, :slab].reshape(count * held, slab)
    high = grad[:, 0, :, slab:].reshape(count * held, slab)
    part = lax.dot_general(jnp.where(core == 0, low, high), weight[...], over, preferred_element_type=F32)
    return part + lax.dot_general(
        jnp.where(core == 0, high, low), weight_other[...], over, preferred_element_type=F32
    )


def gain_kernel(place, grad, seg, ids, weight, weight_other, gain_out, inverse):
    core = place[1]
    step = pl.program_id(0)
    count, _, held, width = seg.shape
    tokens = count * held

    @pl.when(step == 0)
    def _():
        full = seg[...].reshape(tokens, width).astype(F32)
        inv = lax.rsqrt(jnp.mean(full * full, axis=-1, keepdims=True) + EPSILON)
        index = lax.broadcasted_iota(jnp.int32, (tokens, ids.shape[1]), 0)
        index = (index // held * 2 + core) * held + index % held
        found = jnp.max((index == ids[...]).astype(F32), axis=-1, keepdims=True) > 0.0
        inverse[...] = jnp.broadcast_to(jnp.where(found, 0.0, inv), inverse.shape)

    part = chip_term(core, grad, weight, weight_other)
    chunk = part.shape[1]
    unit = seg[:, 0, :, pl.ds(pl.multiple_of(step * chunk, chunk), chunk)].reshape(tokens, chunk).astype(F32)
    gain_out[...] = jnp.sum(part * (unit * inverse[:, :1]), axis=0, keepdims=True)


def logits_kernel(half, mine, other, gain_mine, gain_other, head_mine, head_other, out):
    squares = 0.0
    part = 0.0
    for row, gain, head in ((mine, gain_mine, head_mine), (other, gain_other, head_other)):
        row = row[...].reshape(-1, row.shape[-1]).astype(F32)
        squares += jnp.sum(row * row, axis=-1, keepdims=True)
        part += lax.dot_general(
            (row * gain[...]).astype(BF16), head[...], (((1,), (1,)), ((), ())), preferred_element_type=F32
        )
    column = lax.broadcasted_iota(jnp.int32, part.shape, 1)
    for i, piece in enumerate(pieces3(squares)):
        part = jnp.where(column == half + i, piece, part)
    out[...] = part.astype(BF16).reshape(out.shape)


def softmax_kernel(width, half, vocab, place, parts, targets, expo_out, stats):
    core, start = place[1], place[2]
    total = parts[0].astype(F32)
    for i in range(1, parts.shape[0]):
        total += parts[i].astype(F32)
    inv = lax.rsqrt(jnp.sum(total[:, half : half + 3], axis=-1, keepdims=True) / width + EPSILON)
    logits = total * inv
    column = lax.broadcasted_iota(jnp.int32, logits.shape, 1)
    live = (column < half) & (column + core * half < vocab)
    top = jnp.max(jnp.where(live, logits, -jnp.inf), axis=-1, keepdims=True)
    shifted = jnp.where(live, logits - top, -jnp.inf)
    expo = jnp.exp(shifted)
    expo_out[...] = expo.astype(BF16)
    hit = live & (column == targets[...] - start)
    values = [
        top,
        jnp.sum(expo, axis=-1, keepdims=True),
        jnp.sum(jnp.where(live, expo * shifted, 0.0), axis=-1, keepdims=True),
        jnp.sum(jnp.where(hit, logits, 0.0), axis=-1, keepdims=True),
        inv,
    ]
    lane = lax.broadcasted_iota(jnp.int32, (logits.shape[0], 128), 1)
    table = jnp.zeros(lane.shape, F32)
    for i, value in enumerate(values):
        table = jnp.where(lane == i, value, table)
    table = jnp.concatenate([table, jnp.zeros((128 - table.shape[0], 128), F32)])
    stats[...] = table.T[: stats.shape[0]]


def merged(stats):
    tops, totals, alongs, hits = [stats[:, i] for i in range(4)]
    top = jnp.max(tops, axis=0, keepdims=True)
    lower = jnp.exp(tops - top)
    total = jnp.sum(totals * lower, axis=0, keepdims=True)
    along = jnp.sum((alongs + (tops - top) * totals) * lower, axis=0, keepdims=True)
    return top, total, along, jnp.sum(hits, axis=0, keepdims=True)


def finish_kernel(width, stats, own, weights, known):
    top, total, along, hits = merged(stats[...])
    weight = weights[...]
    factor = weight * (jnp.exp(own[0:1] - top) / total)
    target = weight * (jnp.exp(hits - top) / total - 1.0)
    mean = weight * (along / total - (hits - top)) / width
    rest = jnp.zeros((known.shape[1] - 4, known.shape[2]), F32)
    known[...] = jnp.broadcast_to(jnp.concatenate([factor, target, mean, own[4:5], rest])[None], known.shape)


def logit_grads(half, vocab, which, start, expo, known, targets, grad, kept):
    count, rows, columns = expo.shape
    column = lax.broadcasted_iota(jnp.int32, (rows, columns), 1)
    lane = lax.broadcasted_iota(jnp.int32, (rows, 128), 1)
    live = (column < half) & (column + which * half < vocab)
    for i in range(count):
        table = jnp.concatenate([known[i], jnp.zeros((128 - known.shape[1], 128), F32)]).T[:rows]
        hit = (column + which * half == targets[i * rows : (i + 1) * rows, :] - start) & live
        grad[i] = jnp.where(hit, table[:, 1:2], expo[i].astype(F32) * table[:, 0:1]).astype(BF16)
        if kept is not None:
            kept[i * rows : (i + 1) * rows, :] = jnp.where(lane == 0, table[:, 2:3], table[:, 3:4])
    return grad[...].reshape(count * rows, columns)


def exit_kernel(half, vocab, place, expo, known, targets, head, part, kept, grad):
    rows = logit_grads(half, vocab, place[1], place[2], expo, known, targets, grad, kept)
    part[...] = jnp.dot(rows, head[...], preferred_element_type=F32)


def exit_rest_kernel(half, vocab, place, expo, known, targets, head, before, part, grad):
    rows = logit_grads(half, vocab, 1 - place[1], place[2], expo, known, targets, grad, None)
    total = before[...] + jnp.dot(rows, head[...], preferred_element_type=F32)
    part[...] = total.astype(BF16).reshape(part.shape)


def head_kernel(half, vocab, place, row, gain, kept, targets, ex_mine, ex_other, known_mine, known_other, out, grad):
    core, start = place[1], place[2]
    row = row[...].reshape(-1, row.shape[-1]).astype(F32)
    normed = (row * kept[:, 1:2] * gain[...]).astype(BF16)
    over_rows = (((0,), (0,)), ((), ()))
    parts = []
    for which, expo, known in ((core, ex_mine, known_mine), (1 - core, ex_other, known_other)):
        rows = logit_grads(half, vocab, which, start, expo, known, targets, grad, None)
        parts.append(lax.dot_general(rows, normed, over_rows, preferred_element_type=F32))
    low, high = parts
    out[:half, :] = jnp.where(core == 0, low, high)[:half].astype(BF16)
    out[half:, :] = jnp.where(core == 0, high, low)[: out.shape[0] - half].astype(BF16)


def row_kernel(place, got, hidden, kept, gain, grad_rows, mine, other, whole):
    core = place[1]
    total = got[0].astype(F32)
    for i in range(1, got.shape[0]):
        total += got[i].astype(F32)
    mean, inv = kept[:, 0:1], kept[:, 1:2]
    back = (total * gain[...] - hidden[...].astype(F32) * inv * mean) * inv
    rows = grad_rows[...] + back
    whole[...] = rows.astype(BF16)
    half = mine.shape[0]
    mine[...] = jnp.where(core == 0, rows[:half], rows[half:])
    other[...] = jnp.where(core == 0, rows[half:], rows[:half])


def send_kernel(place, mine, other, weight, weight_other, unit, gain_part, out):
    core = place[1]
    columns = (((1,), (1,)), ((), ()))
    part = lax.dot_general(mine[...].astype(BF16), weight[...], columns, preferred_element_type=F32)
    part += lax.dot_general(other[...].astype(BF16), weight_other[...], columns, preferred_element_type=F32)
    gain = gain_part[...] + jnp.sum(part * unit[...], axis=0, keepdims=True)
    low = jnp.where(core == 0, mine[...], other[...])
    high = jnp.where(core == 0, other[...], mine[...])
    rows = jnp.concatenate([low, high], axis=1)
    rounded = rows.astype(BF16)
    rest = (rows - rounded.astype(F32)).astype(BF16)
    part = part.astype(BF16)
    gains = [values.astype(BF16) for values in pieces3(gain)]
    count, share, _ = out.shape
    width, slab = weight.shape
    piece = width // (count * share)
    for i in range(count):
        at = slice(i * share, (i + 1) * share)
        out[i, :, :width] = part[at]
        out[i, :, width : width + 2 * slab] = rounded[at]
        out[i, :, width + 2 * slab : width + 4 * slab] = rest[at]
        for j in range(share):
            first = (i * share + j) * piece
            for k in range(3):
                to = width + 4 * slab + k * piece
                out[i, j : j + 1, to : to + piece] = gains[k][:, first : first + piece]


def share_kernel(slabs, got, gain, unit, inv, out):
    total = got[0].astype(F32)
    for i in range(1, got.shape[0]):
        total += got[i].astype(F32)
    width = gain.shape[1]
    residual = jnp.concatenate(
        [
            got[i, :, width : width + slabs].astype(F32) + got[i, :, width + slabs : width + 2 * slabs].astype(F32)
            for i in range(got.shape[0])
        ],
        axis=1,
    )
    unit_grad = total[:, :width] * gain[...]
    centre = jnp.mean(unit_grad * unit[...], axis=-1, keepdims=True)
    rows = residual + (unit_grad - unit[...] * centre) * inv[...]
    gains = total[:, width + 2 * slabs :]
    piece = gains.shape[1] // 3
    gains = gains[:, :piece] + gains[:, piece : 2 * piece] + gains[:, 2 * piece :]
    whole = jnp.concatenate([rows] + pieces3(gains), axis=1)
    out[...] = jnp.broadcast_to(whole.astype(BF16)[None], out.shape)


def fetch_kernel(source, out, done):
    parts = done.shape[0]
    count = out.shape[0] // parts
    copies = [
        pltpu.make_async_copy(source.at[pl.ds(i * count, count)], out.at[pl.ds(i * count, count)], done.at[i])
        for i in range(parts)
    ]
    for copy in copies:
        copy.start()
    for copy in copies:
        copy.wait()


def last_kernel(place, ids, mine, other, main, out, gain_out, block, done):
    core = place[1]
    tokens, width = block.shape
    groups, share = mine.shape[:2]
    tile = lax.broadcasted_iota(jnp.int32, (16, width), 0)
    for rows, first in ((mine, core), (other, 1 - core)):
        for i in range(groups):
            for j in range(share):
                at = ids[first * groups * share + i * share + j]
                start = pl.multiple_of(at // 16 * 16, 16)
                row = rows[i, j : j + 1, :width]
                block[pl.ds(start, 16), :] = jnp.where(tile == at - start, row, block[pl.ds(start, 16), :])
    parts = done.shape[0]
    count = tokens // parts
    copies = [
        pltpu.make_async_copy(block.at[pl.ds(i * count, count)], out.at[pl.ds(i * count, count)], done.at[i])
        for i in range(parts)
    ]
    for copy in copies:
        copy.start()
    piece = (mine.shape[2] - width) // 3
    total = mine[:, :, width:].astype(F32) + other[:, :, width:].astype(F32)
    total = total[:, :, :piece] + total[:, :, piece : 2 * piece] + total[:, :, 2 * piece :]
    for i in range(groups):
        for j in range(share):
            at = (i * share + j) * piece
            gain_out[:, at : at + piece] = total[i, j : j + 1]
    for copy in copies:
        copy.wait()


def local(
    segment_in,
    layer_weight,
    layer_gain,
    final_gain,
    head_weight,
    exit_rows,
    exit_count,
    exit_targets,
    exit_scale,
    out_grad,
):
    pipe = lax.axis_index("pipe")
    core = lax.axis_index("core")
    z = lax.axis_index("z")
    pipes = lax.axis_size("pipe")
    zs = lax.axis_size("z")
    block = z * 2 + core
    seg = segment_in[0]
    weight = layer_weight[0]
    gain = layer_gain[0]
    grad = out_grad[0]
    tokens, width = seg.shape
    slab = weight.shape[1]
    exits = exit_rows.shape[1]
    rows_all = pipes * exits
    vocab_part = head_weight.shape[0]
    half = -(-vocab_part // 32) * 16
    padded = -(-(half + 3) // 128) * 128
    place = jnp.stack([z, core, pipe * vocab_part, block]).astype(jnp.int32)
    whole = lambda *dims: pl.BlockSpec(dims, lambda i, *_: (0,) * len(dims))

    weight_other = swap(weight)
    my_rows = exit_rows[pipe]
    pick = (my_rows[:, None] == jnp.arange(tokens, dtype=jnp.int32)[None, :]).astype(BF16)
    row_in = jnp.dot(pick, seg, preferred_element_type=F32)
    row_inv = lax.rsqrt(jnp.mean(row_in * row_in, axis=-1, keepdims=True) + EPSILON)
    row_unit = row_in * row_inv
    row_normed = (row_unit * gain).astype(BF16)
    row_update = lax.reduce_precision(jnp.dot(row_normed, weight, preferred_element_type=F32), 8, 7)
    row_block = lax.dynamic_slice_in_dim(row_in, block * slab, slab, 1)
    hidden = (row_block + row_update).astype(BF16)

    held = tokens // (zs * 2)
    steps = 4
    chunk = width // steps
    grad_spec = pl.BlockSpec((zs, 1, held, 2 * slab), lambda i, at: (0, at[1], 0, at[0]))
    weight_spec = pl.BlockSpec((chunk, slab), lambda i, at: (i, 0))
    grad_view = grad.reshape(zs, 2, held, width)
    joined = jnp.concatenate([weight, weight_other], axis=1)
    chip_grad = lax.dynamic_slice(grad_view, (0, core, 0, z * 2 * slab), (zs, 1, held, 2 * slab))
    on_columns = (((1,), (1,)), ((), ()))

    def own_first(values):
        return jnp.where(core == 0, values, jnp.roll(values, slab, axis=1))

    main_sent = lax.dot_general(
        own_first(chip_grad.reshape(zs * held, 2 * slab)), joined, on_columns, preferred_element_type=F32
    ).astype(BF16)
    hidden, main_sent = lax.optimization_barrier((hidden, main_sent))
    main_grad = lax.psum_scatter(main_sent, "z", scatter_dimension=0, tiled=True)

    halves = jnp.pad(after(head_weight, hidden), ((0, 2 * half - vocab_part), (0, 0))).reshape(2, half, slab)
    halves = jnp.pad(halves, ((0, 0), (0, padded - half), (0, 0)))
    head_mine = lax.dynamic_index_in_dim(halves, core, 0, keepdims=False)
    head_rest = lax.dynamic_index_in_dim(halves, 1 - core, 0, keepdims=False)
    head_other = swap(head_rest)

    all_mine = spread(hidden, "pipe", pipes)
    all_other = swap(all_mine)
    gain_mine = lax.dynamic_slice_in_dim(final_gain, block * slab, slab, 0)[None]
    gain_other = lax.dynamic_slice_in_dim(final_gain, (z * 2 + 1 - core) * slab, slab, 0)[None]
    own = rows_all // zs
    part = vmem_call(
        functools.partial(logits_kernel, half),
        shape((zs, own, padded), BF16),
        all_mine,
        all_other,
        gain_mine,
        gain_other,
        head_mine,
        head_other,
    )
    parts = lax.all_to_all(part, "z", 0, 0)

    gain_part = pl.pallas_call(
        gain_kernel,
        grid_spec=pltpu.PrefetchScalarGridSpec(
            num_scalar_prefetch=1,
            grid=(steps,),
            in_specs=[
                grad_spec,
                pl.BlockSpec((zs, 1, held, width), lambda i, at: (0, at[1], 0, 0)),
                whole(1, exits),
                weight_spec,
                weight_spec,
            ],
            out_specs=pl.BlockSpec((1, chunk), lambda i, at: (0, i)),
            scratch_shapes=[pltpu.VMEM((zs * held, 128), F32)],
        ),
        out_shape=shape((1, width), F32),
        compiler_params=pltpu.CompilerParams(vmem_limit_bytes=LARGE),
    )(
        place,
        after(grad, part).reshape(zs, 2, held, width),
        seg.reshape(zs, 2, held, width),
        my_rows[None],
        weight,
        weight_other,
    )
    all_targets = exit_targets.reshape(rows_all, 1)
    targets = lax.dynamic_slice_in_dim(all_targets, z * own, own, 0)
    slot = jnp.arange(exits, dtype=jnp.int32)[None, :]
    weights = jnp.where(slot < exit_count[:, None], exit_scale[:, None], F32(0.0)).reshape(1, rows_all)
    weights = jnp.pad(lax.dynamic_slice_in_dim(weights, z * own, own, 1), ((0, 0), (0, 128 - own)))
    parts, gain_part = lax.optimization_barrier((parts, gain_part))

    expo, stats = kernel_call(
        functools.partial(softmax_kernel, width, half, vocab_part),
        [shape((own, padded), BF16), shape((8, 128), F32)],
        place,
        parts,
        targets - core * half,
    )
    expo, stats, main_grad = lax.optimization_barrier((expo, stats, main_grad))
    ex_mine = lax.all_gather(expo, "z", axis=0)
    stats_other = swap(stats)
    all_stats = spread(jnp.stack([stats, stats_other]), "pipe", pipes).reshape(pipes * 2, 8, 128)
    known_mine = vmem_call(
        functools.partial(finish_kernel, width), shape((zs, 8, 128), F32), all_stats, stats, weights
    )
    known_sent = known_mine
    known_mine = lax.all_to_all(known_mine, "z", 0, 0)

    first = block * held
    held_in = lax.dynamic_slice_in_dim(after(seg, stats_other), first, held, 0).astype(F32)
    held_grad = lax.dynamic_slice_in_dim(after(grad, stats_other), first, held, 0).astype(F32)
    held_inv = lax.rsqrt(jnp.mean(held_in * held_in, axis=-1, keepdims=True) + EPSILON)
    held_unit = held_in * held_inv
    unit_grad = main_grad.astype(F32) * gain
    centre = jnp.mean(unit_grad * held_unit, axis=-1, keepdims=True)
    main_out = (held_grad + (unit_grad - held_unit * centre) * held_inv).astype(BF16)
    all_stats, main_out = lax.optimization_barrier((all_stats, main_out))
    inputs = after(seg, known_sent).astype(F32)
    inv_rms = lax.rsqrt(jnp.mean(inputs * inputs, axis=-1, keepdims=True) + EPSILON)
    normed = (inputs * inv_rms * gain).astype(BF16)
    grad_slab = lax.dynamic_slice_in_dim(after(grad, known_sent), block * slab, slab, 1)
    grad_rows = jnp.dot(pick, grad_slab, preferred_element_type=F32)
    core_rows = exits // 2
    share = core_rows // zs
    core_unit = lax.dynamic_slice_in_dim(after(row_unit, known_sent), core * core_rows, core_rows, 0)
    share_at = core * core_rows + z * share
    share_unit = lax.dynamic_slice_in_dim(core_unit, z * share, share, 0)
    share_inv = lax.dynamic_slice_in_dim(row_inv, share_at, share, 0)
    known_mine, normed, grad_rows, core_unit, share_unit, share_inv = lax.optimization_barrier(
        (known_mine, normed, grad_rows, core_unit, share_unit, share_inv)
    )
    known_other = swap(known_mine)
    ex_mine, main_out = lax.optimization_barrier((after(ex_mine, known_other), main_out))
    main_all = lax.all_gather(main_out, ("z", "core"), axis=0, tiled=True)
    ex_other = swap(ex_mine)

    grads = [pltpu.VMEM((zs, own, padded), BF16)]
    exit_first, kept = piped_call(
        functools.partial(exit_kernel, half, vocab_part),
        [shape((rows_all, slab), F32), shape((rows_all, 128), F32)],
        place,
        ex_mine,
        known_mine,
        all_targets,
        head_mine,
        kept=(0,),
        scratch=grads,
    )
    (exit_part,) = piped_call(
        functools.partial(exit_rest_kernel, half, vocab_part),
        [shape((pipes, exits, slab), BF16)],
        place,
        ex_other,
        known_other,
        all_targets,
        head_rest,
        exit_first,
        held=(1, 5),
        scratch=grads,
        limit=SMALL,
    )
    exit_got = lax.all_to_all(exit_part, "pipe", 0, 0)
    kept_all = kept
    kept = lax.dynamic_slice_in_dim(kept, pipe * exits, exits, 0)
    (head_grad,) = piped_call(
        functools.partial(head_kernel, half, vocab_part),
        [shape((vocab_part, slab), BF16)],
        place,
        all_mine,
        gain_mine,
        after(kept_all, exit_part),
        all_targets,
        ex_mine,
        ex_other,
        known_mine,
        known_other,
        scratch=grads,
        limit=SMALL,
    )
    exit_got, kept, head_grad = lax.optimization_barrier((exit_got, kept, head_grad))
    row_mine, row_send, row_rounded = kernel_call(
        row_kernel,
        [shape((core_rows, slab), F32)] * 2 + [shape((exits, slab), BF16)],
        place,
        exit_got,
        hidden,
        kept,
        gain_mine,
        grad_rows,
    )

    piece = slab * 2 // share
    send = kernel_call(
        send_kernel,
        shape((zs, share, width + 4 * slab + 3 * piece), BF16),
        place,
        row_mine,
        swap(row_send),
        weight,
        weight_other,
        core_unit,
        gain_part,
    )
    got = lax.all_to_all(send, "z", 0, 0)
    put = pick.T
    is_exit = jnp.any(pick > 0, axis=0)
    slab_rounded = jnp.where(
        is_exit[:, None], jnp.dot(put, after(row_rounded, send), preferred_element_type=F32).astype(BF16), grad_slab
    )
    over_rows = (((0,), (0,)), ((), ()))
    weight_grad = lax.dot_general(normed, slab_rounded, over_rows, preferred_element_type=F32).astype(BF16)
    got, weight_grad = lax.optimization_barrier((got, weight_grad))
    last = vmem_call(
        functools.partial(share_kernel, 2 * slab),
        shape((zs, share, width + 3 * piece), BF16),
        got,
        gain[None],
        share_unit,
        share_inv,
    )
    last, main_all = lax.optimization_barrier((last, main_all))
    last = lax.all_to_all(last, "z", 0, 0)
    main_near = pl.pallas_call(
        fetch_kernel,
        in_specs=[pl.BlockSpec(memory_space=pl.ANY)],
        out_specs=pl.BlockSpec(memory_space=pltpu.VMEM),
        out_shape=shape((tokens, width), BF16),
        scratch_shapes=[pltpu.SemaphoreType.DMA((4,))],
        compiler_params=pltpu.CompilerParams(vmem_limit_bytes=SMALL),
    )(main_all)
    last, main_near = lax.optimization_barrier((last, main_near))
    last_other = swap(last)
    in_vmem = pl.BlockSpec(memory_space=pltpu.VMEM)
    input_grad, gain_grad, _ = pl.pallas_call(
        last_kernel,
        in_specs=[pl.BlockSpec(memory_space=pltpu.SMEM)] * 2 + [in_vmem] * 3,
        out_specs=[pl.BlockSpec(memory_space=pl.ANY), in_vmem, in_vmem],
        out_shape=[shape((tokens, width), BF16), shape((1, width), F32), shape((tokens, width), BF16)],
        input_output_aliases={4: 2},
        scratch_shapes=[pltpu.SemaphoreType.DMA((4,))],
        compiler_params=pltpu.CompilerParams(vmem_limit_bytes=SMALL),
    )(place, my_rows, last, last_other, main_near)
    return (input_grad[None], weight_grad[None], gain_grad, head_grad)


def solution(mesh):
    pipes, tensors = mesh.devices.shape
    fine = Mesh(mesh.devices.reshape(pipes, tensors // 2, 2), ("pipe", "z", "core"))
    tensor = ("z", "core")
    in_specs = (
        P("pipe", None, None),
        P("pipe", None, tensor),
        P("pipe", None),
        P(),
        P("pipe", tensor),
        P(),
        P(),
        P(),
        P(),
        P("pipe", None, None),
    )
    out_specs = (
        P("pipe", None, None),
        P("pipe", None, tensor),
        P("pipe", None),
        P("pipe", tensor),
    )
    return jax.shard_map(local, mesh=fine, in_specs=in_specs, out_specs=out_specs, check_vma=False)
```

```python
import functools

import jax
import jax.numpy as jnp
from jax import lax
from jax.experimental import pallas as pl
from jax.experimental.pallas import tpu as pltpu
from jax.sharding import Mesh, PartitionSpec as P

F32 = jnp.float32
BF16 = jnp.bfloat16
EPSILON = 1e-05
VMEM = 32 * 1024 * 1024
LARGE = 63 * 1024 * 1024


def spread(values, axis, count):
    return lax.all_to_all(jnp.broadcast_to(values[None], (count,) + values.shape), axis, 0, 0)


def swap(values):
    return lax.ppermute(values, "core", [(0, 1), (1, 0)])


def kernel_call(body, out, *operands):
    return pl.pallas_call(
        body,
        out_shape=out,
        in_specs=[
            pl.BlockSpec(memory_space=pltpu.SMEM if i == 0 else pltpu.VMEM) for i in range(len(operands))
        ],
        out_specs=jax.tree.map(lambda _: pl.BlockSpec(memory_space=pltpu.VMEM), out),
        compiler_params=pltpu.CompilerParams(vmem_limit_bytes=VMEM),
    )(*operands)


def vmem_call(body, out, *operands):
    return pl.pallas_call(
        body,
        out_shape=out,
        compiler_params=pltpu.CompilerParams(vmem_limit_bytes=VMEM),
    )(*operands)


def piped_call(body, out, *operands, held=(), kept=(), scratch=(), limit=LARGE):
    def spec(value, stays):
        if stays:
            return pl.BlockSpec(memory_space=pltpu.VMEM)
        return pl.BlockSpec(value.shape, lambda i: (0,) * len(value.shape))

    return pl.pallas_call(
        body,
        grid=(1,),
        out_shape=out,
        in_specs=[pl.BlockSpec(memory_space=pltpu.SMEM)]
        + [spec(value, i in held) for i, value in enumerate(operands[1:], 1)],
        out_specs=[spec(value, i in kept) for i, value in enumerate(out)],
        scratch_shapes=list(scratch),
        compiler_params=pltpu.CompilerParams(vmem_limit_bytes=limit),
    )(*operands)


def shape(dims, dtype):
    return jax.ShapeDtypeStruct(dims, dtype)


def after(values, done):
    return lax.optimization_barrier((values, done))[0]


def pieces3(values):
    first = values.astype(BF16).astype(F32)
    rest = values - first
    second = rest.astype(BF16).astype(F32)
    return [first, second, rest - second]


def chip_term(core, grad, weight, weight_other):
    count, _, held, columns = grad.shape
    slab = columns // 2
    over = (((1,), (1,)), ((), ()))
    low = grad[:, 0, :, :slab].reshape(count * held, slab)
    high = grad[:, 0, :, slab:].reshape(count * held, slab)
    part = lax.dot_general(jnp.where(core == 0, low, high), weight[...], over, preferred_element_type=F32)
    return part + lax.dot_general(
        jnp.where(core == 0, high, low), weight_other[...], over, preferred_element_type=F32
    )


def gain_kernel(place, grad, seg, ids, weight, weight_other, gain_out, inverse):
    core = place[1]
    step = pl.program_id(0)
    count, _, held, width = seg.shape
    tokens = count * held

    @pl.when(step == 0)
    def _():
        full = seg[...].reshape(tokens, width).astype(F32)
        inv = lax.rsqrt(jnp.mean(full * full, axis=-1, keepdims=True) + EPSILON)
        index = lax.broadcasted_iota(jnp.int32, (tokens, ids.shape[1]), 0)
        index = (index // held * 2 + core) * held + index % held
        found = jnp.max((index == ids[...]).astype(F32), axis=-1, keepdims=True) > 0.0
        inverse[...] = jnp.broadcast_to(jnp.where(found, 0.0, inv), inverse.shape)

    part = chip_term(core, grad, weight, weight_other)
    chunk = part.shape[1]
    unit = seg[:, 0, :, pl.ds(pl.multiple_of(step * chunk, chunk), chunk)].reshape(tokens, chunk).astype(F32)
    gain_out[...] = jnp.sum(part * (unit * inverse[:, :1]), axis=0, keepdims=True)


def logits_kernel(half, mine, other, gain_mine, gain_other, head_mine, head_other, out):
    squares = 0.0
    part = 0.0
    for row, gain, head in ((mine, gain_mine, head_mine), (other, gain_other, head_other)):
        row = row[...].reshape(-1, row.shape[-1]).astype(F32)
        squares += jnp.sum(row * row, axis=-1, keepdims=True)
        part += lax.dot_general(
            (row * gain[...]).astype(BF16), head[...], (((1,), (1,)), ((), ())), preferred_element_type=F32
        )
    column = lax.broadcasted_iota(jnp.int32, part.shape, 1)
    for i, piece in enumerate(pieces3(squares)):
        part = jnp.where(column == half + i, piece, part)
    out[...] = part.astype(BF16).reshape(out.shape)


def softmax_kernel(width, half, vocab, place, parts, targets, expo_out, stats):
    core, start = place[1], place[2]
    total = parts[0].astype(F32)
    for i in range(1, parts.shape[0]):
        total += parts[i].astype(F32)
    inv = lax.rsqrt(jnp.sum(total[:, half : half + 3], axis=-1, keepdims=True) / width + EPSILON)
    logits = total * inv
    column = lax.broadcasted_iota(jnp.int32, logits.shape, 1)
    live = (column < half) & (column + core * half < vocab)
    top = jnp.max(jnp.where(live, logits, -jnp.inf), axis=-1, keepdims=True)
    shifted = jnp.where(live, logits - top, -jnp.inf)
    expo = jnp.exp(shifted)
    expo_out[...] = expo.astype(BF16)
    hit = live & (column == targets[...] - start)
    values = [
        top,
        jnp.sum(expo, axis=-1, keepdims=True),
        jnp.sum(jnp.where(live, expo * shifted, 0.0), axis=-1, keepdims=True),
        jnp.sum(jnp.where(hit, logits, 0.0), axis=-1, keepdims=True),
        inv,
    ]
    lane = lax.broadcasted_iota(jnp.int32, (logits.shape[0], 128), 1)
    table = jnp.zeros(lane.shape, F32)
    for i, value in enumerate(values):
        table = jnp.where(lane == i, value, table)
    table = jnp.concatenate([table, jnp.zeros((128 - table.shape[0], 128), F32)])
    stats[...] = table.T[: stats.shape[0]]


def merged(stats):
    tops, totals, alongs, hits = [stats[:, i] for i in range(4)]
    top = jnp.max(tops, axis=0, keepdims=True)
    lower = jnp.exp(tops - top)
    total = jnp.sum(totals * lower, axis=0, keepdims=True)
    along = jnp.sum((alongs + (tops - top) * totals) * lower, axis=0, keepdims=True)
    return top, total, along, jnp.sum(hits, axis=0, keepdims=True)


def finish_kernel(width, stats, own, weights, known):
    top, total, along, hits = merged(stats[...])
    weight = weights[...]
    factor = weight * (jnp.exp(own[0:1] - top) / total)
    target = weight * (jnp.exp(hits - top) / total - 1.0)
    mean = weight * (along / total - (hits - top)) / width
    rest = jnp.zeros((known.shape[1] - 4, known.shape[2]), F32)
    known[...] = jnp.broadcast_to(jnp.concatenate([factor, target, mean, own[4:5], rest])[None], known.shape)


def logit_grads(half, vocab, which, start, expo, known, targets, grad, kept):
    count, rows, columns = expo.shape
    column = lax.broadcasted_iota(jnp.int32, (rows, columns), 1)
    lane = lax.broadcasted_iota(jnp.int32, (rows, 128), 1)
    live = (column < half) & (column + which * half < vocab)
    for i in range(count):
        table = jnp.concatenate([known[i], jnp.zeros((128 - known.shape[1], 128), F32)]).T[:rows]
        hit = (column + which * half == targets[i * rows : (i + 1) * rows, :] - start) & live
        grad[i] = jnp.where(hit, table[:, 1:2], expo[i].astype(F32) * table[:, 0:1]).astype(BF16)
        if kept is not None:
            kept[i * rows : (i + 1) * rows, :] = jnp.where(lane == 0, table[:, 2:3], table[:, 3:4])
    return grad[...].reshape(count * rows, columns)


def exit_kernel(half, vocab, place, expo, known, targets, head, part, kept, grad):
    rows = logit_grads(half, vocab, place[1], place[2], expo, known, targets, grad, kept)
    part[...] = jnp.dot(rows, head[...], preferred_element_type=F32)


def exit_rest_kernel(half, vocab, place, expo, known, targets, head, before, part, grad):
    rows = logit_grads(half, vocab, 1 - place[1], place[2], expo, known, targets, grad, None)
    total = before[...] + jnp.dot(rows, head[...], preferred_element_type=F32)
    part[...] = total.astype(BF16).reshape(part.shape)


def head_kernel(half, vocab, place, row, gain, kept, targets, ex_mine, ex_other, known_mine, known_other, out, grad):
    core, start = place[1], place[2]
    row = row[...].reshape(-1, row.shape[-1]).astype(F32)
    normed = (row * kept[:, 1:2] * gain[...]).astype(BF16)
    over_rows = (((0,), (0,)), ((), ()))
    parts = []
    for which, expo, known in ((core, ex_mine, known_mine), (1 - core, ex_other, known_other)):
        rows = logit_grads(half, vocab, which, start, expo, known, targets, grad, None)
        parts.append(lax.dot_general(rows, normed, over_rows, preferred_element_type=F32))
    low, high = parts
    out[:half, :] = jnp.where(core == 0, low, high)[:half].astype(BF16)
    out[half:, :] = jnp.where(core == 0, high, low)[: out.shape[0] - half].astype(BF16)


def row_kernel(place, got, hidden, kept, gain, grad_rows, mine, other, whole):
    core = place[1]
    total = got[0].astype(F32)
    for i in range(1, got.shape[0]):
        total += got[i].astype(F32)
    mean, inv = kept[:, 0:1], kept[:, 1:2]
    back = (total * gain[...] - hidden[...].astype(F32) * inv * mean) * inv
    rows = grad_rows[...] + back
    whole[...] = rows.astype(BF16)
    half = mine.shape[0]
    mine[...] = jnp.where(core == 0, rows[:half], rows[half:])
    other[...] = jnp.where(core == 0, rows[half:], rows[:half])


def send_kernel(place, mine, other, weight, weight_other, unit, gain_part, out):
    core = place[1]
    columns = (((1,), (1,)), ((), ()))
    part = lax.dot_general(mine[...].astype(BF16), weight[...], columns, preferred_element_type=F32)
    part += lax.dot_general(other[...].astype(BF16), weight_other[...], columns, preferred_element_type=F32)
    gain = gain_part[...] + jnp.sum(part * unit[...], axis=0, keepdims=True)
    low = jnp.where(core == 0, mine[...], other[...])
    high = jnp.where(core == 0, other[...], mine[...])
    rows = jnp.concatenate([low, high], axis=1)
    rounded = rows.astype(BF16)
    rest = (rows - rounded.astype(F32)).astype(BF16)
    part = part.astype(BF16)
    gains = [values.astype(BF16) for values in pieces3(gain)]
    count, share, _ = out.shape
    width, slab = weight.shape
    piece = width // (count * share)
    for i in range(count):
        at = slice(i * share, (i + 1) * share)
        out[i, :, :width] = part[at]
        out[i, :, width : width + 2 * slab] = rounded[at]
        out[i, :, width + 2 * slab : width + 4 * slab] = rest[at]
        for j in range(share):
            first = (i * share + j) * piece
            for k in range(3):
                to = width + 4 * slab + k * piece
                out[i, j : j + 1, to : to + piece] = gains[k][:, first : first + piece]


def share_kernel(slabs, got, gain, unit, inv, out):
    total = got[0].astype(F32)
    for i in range(1, got.shape[0]):
        total += got[i].astype(F32)
    width = gain.shape[1]
    residual = jnp.concatenate(
        [
            got[i, :, width : width + slabs].astype(F32) + got[i, :, width + slabs : width + 2 * slabs].astype(F32)
            for i in range(got.shape[0])
        ],
        axis=1,
    )
    unit_grad = total[:, :width] * gain[...]
    centre = jnp.mean(unit_grad * unit[...], axis=-1, keepdims=True)
    rows = residual + (unit_grad - unit[...] * centre) * inv[...]
    gains = total[:, width + 2 * slabs :]
    piece = gains.shape[1] // 3
    gains = gains[:, :piece] + gains[:, piece : 2 * piece] + gains[:, 2 * piece :]
    whole = jnp.concatenate([rows] + pieces3(gains), axis=1)
    out[...] = jnp.broadcast_to(whole.astype(BF16)[None], out.shape)


def last_kernel(place, ids, mine, other, main, out, gain_out, block, into, outof):
    core = place[1]
    tokens, width = block.shape
    parts = into.shape[0]
    count = tokens // parts

    def copies(source, target, done):
        return [
            pltpu.make_async_copy(
                source.at[pl.ds(i * count, count)], target.at[pl.ds(i * count, count)], done.at[i]
            )
            for i in range(parts)
        ]

    loads = copies(main, block, into)
    stores = copies(block, out, outof)
    for load in loads:
        load.start()
    groups, share = mine.shape[:2]
    piece = (mine.shape[2] - width) // 3
    total = mine[:, :, width:].astype(F32) + other[:, :, width:].astype(F32)
    total = total[:, :, :piece] + total[:, :, piece : 2 * piece] + total[:, :, 2 * piece :]
    for i in range(groups):
        for j in range(share):
            at = (i * share + j) * piece
            gain_out[:, at : at + piece] = total[i, j : j + 1]
    tile = lax.broadcasted_iota(jnp.int32, (16, width), 0)
    for load in loads:
        load.wait()
    for rows, first in ((mine, core), (other, 1 - core)):
        for i in range(groups):
            for j in range(share):
                at = ids[first * groups * share + i * share + j]
                start = pl.multiple_of(at // 16 * 16, 16)
                row = rows[i, j : j + 1, :width]
                block[pl.ds(start, 16), :] = jnp.where(tile == at - start, row, block[pl.ds(start, 16), :])
    for store in stores:
        store.start()
    for store in stores:
        store.wait()


def local(
    segment_in,
    layer_weight,
    layer_gain,
    final_gain,
    head_weight,
    exit_rows,
    exit_count,
    exit_targets,
    exit_scale,
    out_grad,
):
    pipe = lax.axis_index("pipe")
    core = lax.axis_index("core")
    z = lax.axis_index("z")
    pipes = lax.axis_size("pipe")
    zs = lax.axis_size("z")
    block = z * 2 + core
    seg = segment_in[0]
    weight = layer_weight[0]
    gain = layer_gain[0]
    grad = out_grad[0]
    tokens, width = seg.shape
    slab = weight.shape[1]
    exits = exit_rows.shape[1]
    rows_all = pipes * exits
    vocab_part = head_weight.shape[0]
    half = -(-vocab_part // 32) * 16
    padded = -(-(half + 3) // 128) * 128
    place = jnp.stack([z, core, pipe * vocab_part, block]).astype(jnp.int32)
    whole = lambda *dims: pl.BlockSpec(dims, lambda i, *_: (0,) * len(dims))

    weight_other = swap(weight)
    my_rows = exit_rows[pipe]
    pick = (my_rows[:, None] == jnp.arange(tokens, dtype=jnp.int32)[None, :]).astype(BF16)
    row_in = jnp.dot(pick, seg, preferred_element_type=F32)
    row_inv = lax.rsqrt(jnp.mean(row_in * row_in, axis=-1, keepdims=True) + EPSILON)
    row_unit = row_in * row_inv
    row_normed = (row_unit * gain).astype(BF16)
    row_update = lax.reduce_precision(jnp.dot(row_normed, weight, preferred_element_type=F32), 8, 7)
    row_block = lax.dynamic_slice_in_dim(row_in, block * slab, slab, 1)
    hidden = (row_block + row_update).astype(BF16)

    held = tokens // (zs * 2)
    steps = 4
    chunk = width // steps
    grad_spec = pl.BlockSpec((zs, 1, held, 2 * slab), lambda i, at: (0, at[1], 0, at[0]))
    weight_spec = pl.BlockSpec((chunk, slab), lambda i, at: (i, 0))
    grad_view = grad.reshape(zs, 2, held, width)
    joined = jnp.concatenate([weight, weight_other], axis=1)
    chip_grad = lax.dynamic_slice(after(grad_view, hidden), (0, core, 0, z * 2 * slab), (zs, 1, held, 2 * slab))
    on_columns = (((1,), (1,)), ((), ()))

    def own_first(values):
        return jnp.where(core == 0, values, jnp.roll(values, slab, axis=1))

    main_sent = lax.dot_general(
        own_first(chip_grad.reshape(zs * held, 2 * slab)), joined, on_columns, preferred_element_type=F32
    ).astype(BF16)

    halves = jnp.pad(after(head_weight, hidden), ((0, 2 * half - vocab_part), (0, 0))).reshape(2, half, slab)
    halves = jnp.pad(halves, ((0, 0), (0, padded - half), (0, 0)))
    head_mine = lax.dynamic_index_in_dim(halves, core, 0, keepdims=False)
    head_rest = lax.dynamic_index_in_dim(halves, 1 - core, 0, keepdims=False)
    head_other = swap(head_rest)

    all_mine = spread(hidden, "pipe", pipes)
    all_mine, main_sent, head_other = lax.optimization_barrier((all_mine, main_sent, head_other))
    main_grad = lax.psum_scatter(main_sent, "z", scatter_dimension=0, tiled=True)
    all_other = swap(all_mine)
    gain_mine = lax.dynamic_slice_in_dim(final_gain, block * slab, slab, 0)[None]
    gain_other = lax.dynamic_slice_in_dim(final_gain, (z * 2 + 1 - core) * slab, slab, 0)[None]
    own = rows_all // zs
    part = vmem_call(
        functools.partial(logits_kernel, half),
        shape((zs, own, padded), BF16),
        all_mine,
        all_other,
        gain_mine,
        gain_other,
        head_mine,
        head_other,
    )
    parts = lax.all_to_all(part, "z", 0, 0)

    gain_part = pl.pallas_call(
        gain_kernel,
        grid_spec=pltpu.PrefetchScalarGridSpec(
            num_scalar_prefetch=1,
            grid=(steps,),
            in_specs=[
                grad_spec,
                pl.BlockSpec((zs, 1, held, width), lambda i, at: (0, at[1], 0, 0)),
                whole(1, exits),
                weight_spec,
                weight_spec,
            ],
            out_specs=pl.BlockSpec((1, chunk), lambda i, at: (0, i)),
            scratch_shapes=[pltpu.VMEM((zs * held, 128), F32)],
        ),
        out_shape=shape((1, width), F32),
        compiler_params=pltpu.CompilerParams(vmem_limit_bytes=LARGE),
    )(
        place,
        after(grad, part).reshape(zs, 2, held, width),
        seg.reshape(zs, 2, held, width),
        my_rows[None],
        weight,
        weight_other,
    )
    all_targets = exit_targets.reshape(rows_all, 1)
    targets = lax.dynamic_slice_in_dim(all_targets, z * own, own, 0)
    slot = jnp.arange(exits, dtype=jnp.int32)[None, :]
    weights = jnp.where(slot < exit_count[:, None], exit_scale[:, None], F32(0.0)).reshape(1, rows_all)
    weights = jnp.pad(lax.dynamic_slice_in_dim(weights, z * own, own, 1), ((0, 0), (0, 128 - own)))
    parts, gain_part = lax.optimization_barrier((parts, gain_part))

    expo, stats = kernel_call(
        functools.partial(softmax_kernel, width, half, vocab_part),
        [shape((own, padded), BF16), shape((8, 128), F32)],
        place,
        parts,
        targets - core * half,
    )
    expo, stats, main_grad = lax.optimization_barrier((expo, stats, main_grad))
    ex_mine = lax.all_gather(expo, "z", axis=0)
    stats_other = swap(stats)
    all_stats = spread(jnp.stack([stats, stats_other]), "pipe", pipes).reshape(pipes * 2, 8, 128)
    known_mine = vmem_call(
        functools.partial(finish_kernel, width), shape((zs, 8, 128), F32), all_stats, stats, weights
    )
    known_sent = known_mine
    known_mine = lax.all_to_all(known_mine, "z", 0, 0)

    first = block * held
    held_in = lax.dynamic_slice_in_dim(after(seg, stats_other), first, held, 0).astype(F32)
    held_grad = lax.dynamic_slice_in_dim(after(grad, stats_other), first, held, 0).astype(F32)
    held_inv = lax.rsqrt(jnp.mean(held_in * held_in, axis=-1, keepdims=True) + EPSILON)
    held_unit = held_in * held_inv
    unit_grad = main_grad.astype(F32) * gain
    centre = jnp.mean(unit_grad * held_unit, axis=-1, keepdims=True)
    main_out = (held_grad + (unit_grad - held_unit * centre) * held_inv).astype(BF16)
    all_stats, main_out = lax.optimization_barrier((all_stats, main_out))
    inputs = after(seg, known_sent).astype(F32)
    inv_rms = lax.rsqrt(jnp.mean(inputs * inputs, axis=-1, keepdims=True) + EPSILON)
    normed = (inputs * inv_rms * gain).astype(BF16)
    grad_slab = lax.dynamic_slice_in_dim(after(grad, known_sent), block * slab, slab, 1)
    grad_rows = jnp.dot(pick, grad_slab, preferred_element_type=F32)
    core_rows = exits // 2
    share = core_rows // zs
    core_unit = lax.dynamic_slice_in_dim(after(row_unit, known_sent), core * core_rows, core_rows, 0)
    share_at = core * core_rows + z * share
    share_unit = lax.dynamic_slice_in_dim(core_unit, z * share, share, 0)
    share_inv = lax.dynamic_slice_in_dim(row_inv, share_at, share, 0)
    known_mine, normed, grad_rows, core_unit, share_unit, share_inv = lax.optimization_barrier(
        (known_mine, normed, grad_rows, core_unit, share_unit, share_inv)
    )
    known_other = swap(known_mine)
    ex_mine, main_out = lax.optimization_barrier((after(ex_mine, known_other), main_out))
    main_all = lax.all_gather(main_out, ("z", "core"), axis=0, tiled=True)
    ex_other = swap(ex_mine)

    grads = [pltpu.VMEM((zs, own, padded), BF16)]
    exit_first, kept = piped_call(
        functools.partial(exit_kernel, half, vocab_part),
        [shape((rows_all, slab), F32), shape((rows_all, 128), F32)],
        place,
        ex_mine,
        known_mine,
        all_targets,
        head_mine,
        kept=(0,),
        scratch=grads,
    )
    (exit_part,) = piped_call(
        functools.partial(exit_rest_kernel, half, vocab_part),
        [shape((pipes, exits, slab), BF16)],
        place,
        ex_other,
        known_other,
        all_targets,
        head_rest,
        exit_first,
        held=(5,),
        scratch=grads,
    )
    exit_got = lax.all_to_all(exit_part, "pipe", 0, 0)
    kept_all = kept
    kept = lax.dynamic_slice_in_dim(kept, pipe * exits, exits, 0)
    (head_grad,) = piped_call(
        functools.partial(head_kernel, half, vocab_part),
        [shape((vocab_part, slab), BF16)],
        place,
        all_mine,
        gain_mine,
        after(kept_all, exit_part),
        all_targets,
        ex_mine,
        ex_other,
        known_mine,
        known_other,
        scratch=grads,
    )
    exit_got, kept, head_grad = lax.optimization_barrier((exit_got, kept, head_grad))
    row_mine, row_send, row_rounded = kernel_call(
        row_kernel,
        [shape((core_rows, slab), F32)] * 2 + [shape((exits, slab), BF16)],
        place,
        exit_got,
        hidden,
        kept,
        gain_mine,
        grad_rows,
    )

    piece = slab * 2 // share
    send = kernel_call(
        send_kernel,
        shape((zs, share, width + 4 * slab + 3 * piece), BF16),
        place,
        row_mine,
        swap(row_send),
        weight,
        weight_other,
        core_unit,
        gain_part,
    )
    got = lax.all_to_all(send, "z", 0, 0)
    put = pick.T
    is_exit = jnp.any(pick > 0, axis=0)
    slab_rounded = jnp.where(
        is_exit[:, None], jnp.dot(put, after(row_rounded, send), preferred_element_type=F32).astype(BF16), grad_slab
    )
    over_rows = (((0,), (0,)), ((), ()))
    weight_grad = lax.dot_general(normed, slab_rounded, over_rows, preferred_element_type=F32).astype(BF16)
    got, weight_grad = lax.optimization_barrier((got, weight_grad))
    last = vmem_call(
        functools.partial(share_kernel, 2 * slab),
        shape((zs, share, width + 3 * piece), BF16),
        got,
        gain[None],
        share_unit,
        share_inv,
    )
    last, main_all = lax.optimization_barrier((last, main_all))
    last = lax.all_to_all(last, "z", 0, 0)
    last_other = swap(last)
    in_vmem = pl.BlockSpec(memory_space=pltpu.VMEM)
    parts = 4
    input_grad, gain_grad = pl.pallas_call(
        last_kernel,
        in_specs=[pl.BlockSpec(memory_space=pltpu.SMEM)] * 2 + [in_vmem] * 2 + [pl.BlockSpec(memory_space=pl.ANY)],
        out_specs=[pl.BlockSpec(memory_space=pl.ANY), in_vmem],
        out_shape=[shape((tokens, width), BF16), shape((1, width), F32)],
        scratch_shapes=[
            pltpu.VMEM((tokens, width), BF16),
            pltpu.SemaphoreType.DMA((parts,)),
            pltpu.SemaphoreType.DMA((parts,)),
        ],
        compiler_params=pltpu.CompilerParams(vmem_limit_bytes=LARGE),
    )(place, my_rows, last, last_other, main_all)
    return (input_grad[None], weight_grad[None], gain_grad, head_grad)


def solution(mesh):
    pipes, tensors = mesh.devices.shape
    fine = Mesh(mesh.devices.reshape(pipes, tensors // 2, 2), ("pipe", "z", "core"))
    tensor = ("z", "core")
    in_specs = (
        P("pipe", None, None),
        P("pipe", None, tensor),
        P("pipe", None),
        P(),
        P("pipe", tensor),
        P(),
        P(),
        P(),
        P(),
        P("pipe", None, None),
    )
    out_specs = (
        P("pipe", None, None),
        P("pipe", None, tensor),
        P("pipe", None),
        P("pipe", tensor),
    )
    return jax.shard_map(local, mesh=fine, in_specs=in_specs, out_specs=out_specs, check_vma=False)
```

```python
import functools

import jax
import jax.numpy as jnp
from jax import lax
from jax.experimental import pallas as pl
from jax.experimental.pallas import tpu as pltpu
from jax.sharding import Mesh, PartitionSpec as P

F32 = jnp.float32
BF16 = jnp.bfloat16
EPSILON = 1e-05
SMALL = 20 * 1024 * 1024
VMEM = 32 * 1024 * 1024
LARGE = 56 * 1024 * 1024
LARGEST = 63 * 1024 * 1024


def spread(values, axis, count):
    return lax.all_to_all(jnp.broadcast_to(values[None], (count,) + values.shape), axis, 0, 0)


def swap(values):
    return lax.ppermute(values, "core", [(0, 1), (1, 0)])


def kernel_call(body, out, *operands):
    return pl.pallas_call(
        body,
        out_shape=out,
        in_specs=[
            pl.BlockSpec(memory_space=pltpu.SMEM if i == 0 else pltpu.VMEM) for i in range(len(operands))
        ],
        out_specs=jax.tree.map(lambda _: pl.BlockSpec(memory_space=pltpu.VMEM), out),
        compiler_params=pltpu.CompilerParams(vmem_limit_bytes=VMEM),
    )(*operands)


def vmem_call(body, out, *operands):
    return pl.pallas_call(
        body,
        out_shape=out,
        compiler_params=pltpu.CompilerParams(vmem_limit_bytes=VMEM),
    )(*operands)


def piped_call(body, out, *operands, held=(), kept=(), scratch=(), limit=LARGEST):
    def spec(value, stays):
        if stays:
            return pl.BlockSpec(memory_space=pltpu.VMEM)
        return pl.BlockSpec(value.shape, lambda i: (0,) * len(value.shape))

    return pl.pallas_call(
        body,
        grid=(1,),
        out_shape=out,
        in_specs=[pl.BlockSpec(memory_space=pltpu.SMEM)]
        + [spec(value, i in held) for i, value in enumerate(operands[1:], 1)],
        out_specs=[spec(value, i in kept) for i, value in enumerate(out)],
        scratch_shapes=list(scratch),
        compiler_params=pltpu.CompilerParams(vmem_limit_bytes=limit),
    )(*operands)


def shape(dims, dtype):
    return jax.ShapeDtypeStruct(dims, dtype)


def after(values, done):
    return lax.optimization_barrier((values, done))[0]


def pieces3(values):
    first = values.astype(BF16).astype(F32)
    rest = values - first
    second = rest.astype(BF16).astype(F32)
    return [first, second, rest - second]


def chip_term(core, grad, weight, weight_other):
    count, _, held, columns = grad.shape
    slab = columns // 2
    over = (((1,), (1,)), ((), ()))
    low = grad[:, 0, :, :slab].reshape(count * held, slab)
    high = grad[:, 0, :, slab:].reshape(count * held, slab)
    part = lax.dot_general(jnp.where(core == 0, low, high), weight[...], over, preferred_element_type=F32)
    return part + lax.dot_general(
        jnp.where(core == 0, high, low), weight_other[...], over, preferred_element_type=F32
    )


def gain_kernel(place, grad, seg, ids, weight, weight_other, gain_out, inverse):
    core = place[1]
    step = pl.program_id(0)
    count, _, held, width = seg.shape
    tokens = count * held

    @pl.when(step == 0)
    def _():
        full = seg[...].reshape(tokens, width).astype(F32)
        inv = lax.rsqrt(jnp.mean(full * full, axis=-1, keepdims=True) + EPSILON)
        index = lax.broadcasted_iota(jnp.int32, (tokens, ids.shape[1]), 0)
        index = (index // held * 2 + core) * held + index % held
        found = jnp.max((index == ids[...]).astype(F32), axis=-1, keepdims=True) > 0.0
        inverse[...] = jnp.broadcast_to(jnp.where(found, 0.0, inv), inverse.shape)

    part = chip_term(core, grad, weight, weight_other)
    chunk = part.shape[1]
    unit = seg[:, 0, :, pl.ds(pl.multiple_of(step * chunk, chunk), chunk)].reshape(tokens, chunk).astype(F32)
    gain_out[...] = jnp.sum(part * (unit * inverse[:, :1]), axis=0, keepdims=True)


def logits_kernel(half, mine, other, gain_mine, gain_other, head_mine, head_other, out):
    squares = 0.0
    part = 0.0
    for row, gain, head in ((mine, gain_mine, head_mine), (other, gain_other, head_other)):
        row = row[...].reshape(-1, row.shape[-1]).astype(F32)
        squares += jnp.sum(row * row, axis=-1, keepdims=True)
        part += lax.dot_general(
            (row * gain[...]).astype(BF16), head[...], (((1,), (1,)), ((), ())), preferred_element_type=F32
        )
    column = lax.broadcasted_iota(jnp.int32, part.shape, 1)
    for i, piece in enumerate(pieces3(squares)):
        part = jnp.where(column == half + i, piece, part)
    out[...] = part.astype(BF16).reshape(out.shape)


def softmax_kernel(width, half, vocab, place, parts, targets, expo_out, stats):
    core, start = place[1], place[2]
    total = parts[0].astype(F32)
    for i in range(1, parts.shape[0]):
        total += parts[i].astype(F32)
    inv = lax.rsqrt(jnp.sum(total[:, half : half + 3], axis=-1, keepdims=True) / width + EPSILON)
    logits = total * inv
    column = lax.broadcasted_iota(jnp.int32, logits.shape, 1)
    live = (column < half) & (column + core * half < vocab)
    top = jnp.max(jnp.where(live, logits, -jnp.inf), axis=-1, keepdims=True)
    shifted = jnp.where(live, logits - top, -jnp.inf)
    expo = jnp.exp(shifted)
    expo_out[...] = expo.astype(BF16)
    hit = live & (column == targets[...] - start)
    values = [
        top,
        jnp.sum(expo, axis=-1, keepdims=True),
        jnp.sum(jnp.where(live, expo * shifted, 0.0), axis=-1, keepdims=True),
        jnp.sum(jnp.where(hit, logits, 0.0), axis=-1, keepdims=True),
        inv,
    ]
    lane = lax.broadcasted_iota(jnp.int32, (logits.shape[0], 128), 1)
    table = jnp.zeros(lane.shape, F32)
    for i, value in enumerate(values):
        table = jnp.where(lane == i, value, table)
    table = jnp.concatenate([table, jnp.zeros((128 - table.shape[0], 128), F32)])
    stats[...] = table.T[: stats.shape[0]]


def merged(stats):
    tops, totals, alongs, hits = [stats[:, i] for i in range(4)]
    top = jnp.max(tops, axis=0, keepdims=True)
    lower = jnp.exp(tops - top)
    total = jnp.sum(totals * lower, axis=0, keepdims=True)
    along = jnp.sum((alongs + (tops - top) * totals) * lower, axis=0, keepdims=True)
    return top, total, along, jnp.sum(hits, axis=0, keepdims=True)


def finish_kernel(width, stats, own, weights, known):
    top, total, along, hits = merged(stats[...])
    weight = weights[...]
    factor = weight * (jnp.exp(own[0:1] - top) / total)
    target = weight * (jnp.exp(hits - top) / total - 1.0)
    mean = weight * (along / total - (hits - top)) / width
    rest = jnp.zeros((known.shape[1] - 4, known.shape[2]), F32)
    known[...] = jnp.broadcast_to(jnp.concatenate([factor, target, mean, own[4:5], rest])[None], known.shape)


def logit_grads(half, vocab, which, start, expo, known, targets, grad, kept):
    count, rows, columns = expo.shape
    column = lax.broadcasted_iota(jnp.int32, (rows, columns), 1)
    lane = lax.broadcasted_iota(jnp.int32, (rows, 128), 1)
    live = (column < half) & (column + which * half < vocab)
    for i in range(count):
        table = jnp.concatenate([known[i], jnp.zeros((128 - known.shape[1], 128), F32)]).T[:rows]
        hit = (column + which * half == targets[i * rows : (i + 1) * rows, :] - start) & live
        grad[i] = jnp.where(hit, table[:, 1:2], expo[i].astype(F32) * table[:, 0:1]).astype(BF16)
        if kept is not None:
            kept[i * rows : (i + 1) * rows, :] = jnp.where(lane == 0, table[:, 2:3], table[:, 3:4])
    return grad[...].reshape(count * rows, columns)


def exit_kernel(half, vocab, place, expo, known, targets, head, part, kept, grad):
    rows = logit_grads(half, vocab, place[1], place[2], expo, known, targets, grad, kept)
    part[...] = jnp.dot(rows, head[...], preferred_element_type=F32)


def exit_rest_kernel(half, vocab, place, expo, known, targets, head, before, part, grad):
    rows = logit_grads(half, vocab, 1 - place[1], place[2], expo, known, targets, grad, None)
    total = before[...] + jnp.dot(rows, head[...], preferred_element_type=F32)
    part[...] = total.astype(BF16).reshape(part.shape)


def head_kernel(half, vocab, place, row, gain, kept, targets, ex_mine, ex_other, known_mine, known_other, out, grad):
    core, start = place[1], place[2]
    row = row[...].reshape(-1, row.shape[-1]).astype(F32)
    normed = (row * kept[:, 1:2] * gain[...]).astype(BF16)
    over_rows = (((0,), (0,)), ((), ()))
    parts = []
    for which, expo, known in ((core, ex_mine, known_mine), (1 - core, ex_other, known_other)):
        rows = logit_grads(half, vocab, which, start, expo, known, targets, grad, None)
        parts.append(lax.dot_general(rows, normed, over_rows, preferred_element_type=F32))
    low, high = parts
    out[:half, :] = jnp.where(core == 0, low, high)[:half].astype(BF16)
    out[half:, :] = jnp.where(core == 0, high, low)[: out.shape[0] - half].astype(BF16)


def row_kernel(place, got, hidden, kept, gain, grad_rows, mine, other, whole):
    core = place[1]
    total = got[0].astype(F32)
    for i in range(1, got.shape[0]):
        total += got[i].astype(F32)
    mean, inv = kept[:, 0:1], kept[:, 1:2]
    back = (total * gain[...] - hidden[...].astype(F32) * inv * mean) * inv
    rows = grad_rows[...] + back
    whole[...] = rows.astype(BF16)
    half = mine.shape[0]
    mine[...] = jnp.where(core == 0, rows[:half], rows[half:])
    other[...] = jnp.where(core == 0, rows[half:], rows[:half])


def send_kernel(place, mine, other, weight, weight_other, unit, gain_part, out):
    core = place[1]
    columns = (((1,), (1,)), ((), ()))
    part = lax.dot_general(mine[...].astype(BF16), weight[...], columns, preferred_element_type=F32)
    part += lax.dot_general(other[...].astype(BF16), weight_other[...], columns, preferred_element_type=F32)
    gain = gain_part[...] + jnp.sum(part * unit[...], axis=0, keepdims=True)
    low = jnp.where(core == 0, mine[...], other[...])
    high = jnp.where(core == 0, other[...], mine[...])
    rows = jnp.concatenate([low, high], axis=1)
    rounded = rows.astype(BF16)
    rest = (rows - rounded.astype(F32)).astype(BF16)
    part = part.astype(BF16)
    gains = [values.astype(BF16) for values in pieces3(gain)]
    count, share, _ = out.shape
    width, slab = weight.shape
    piece = width // (count * share)
    for i in range(count):
        at = slice(i * share, (i + 1) * share)
        out[i, :, :width] = part[at]
        out[i, :, width : width + 2 * slab] = rounded[at]
        out[i, :, width + 2 * slab : width + 4 * slab] = rest[at]
        for j in range(share):
            first = (i * share + j) * piece
            for k in range(3):
                to = width + 4 * slab + k * piece
                out[i, j : j + 1, to : to + piece] = gains[k][:, first : first + piece]


def share_kernel(slabs, got, gain, unit, inv, out):
    total = got[0].astype(F32)
    for i in range(1, got.shape[0]):
        total += got[i].astype(F32)
    width = gain.shape[1]
    residual = jnp.concatenate(
        [
            got[i, :, width : width + slabs].astype(F32) + got[i, :, width + slabs : width + 2 * slabs].astype(F32)
            for i in range(got.shape[0])
        ],
        axis=1,
    )
    unit_grad = total[:, :width] * gain[...]
    centre = jnp.mean(unit_grad * unit[...], axis=-1, keepdims=True)
    rows = residual + (unit_grad - unit[...] * centre) * inv[...]
    gains = total[:, width + 2 * slabs :]
    piece = gains.shape[1] // 3
    gains = gains[:, :piece] + gains[:, piece : 2 * piece] + gains[:, 2 * piece :]
    whole = jnp.concatenate([rows] + pieces3(gains), axis=1)
    out[...] = jnp.broadcast_to(whole.astype(BF16)[None], out.shape)


def fetch_kernel(source, out, done):
    parts = done.shape[0]
    count = out.shape[0] // parts
    copies = [
        pltpu.make_async_copy(source.at[pl.ds(i * count, count)], out.at[pl.ds(i * count, count)], done.at[i])
        for i in range(parts)
    ]
    for copy in copies:
        copy.start()
    for copy in copies:
        copy.wait()


def last_kernel(place, ids, mine, other, main, out, gain_out, block, done):
    core = place[1]
    tokens, width = block.shape
    groups, share = mine.shape[:2]
    tile = lax.broadcasted_iota(jnp.int32, (16, width), 0)
    for rows, first in ((mine, core), (other, 1 - core)):
        for i in range(groups):
            for j in range(share):
                at = ids[first * groups * share + i * share + j]
                start = pl.multiple_of(at // 16 * 16, 16)
                row = rows[i, j : j + 1, :width]
                block[pl.ds(start, 16), :] = jnp.where(tile == at - start, row, block[pl.ds(start, 16), :])
    parts = done.shape[0]
    count = tokens // parts
    copies = [
        pltpu.make_async_copy(block.at[pl.ds(i * count, count)], out.at[pl.ds(i * count, count)], done.at[i])
        for i in range(parts)
    ]
    for copy in copies:
        copy.start()
    piece = (mine.shape[2] - width) // 3
    total = mine[:, :, width:].astype(F32) + other[:, :, width:].astype(F32)
    total = total[:, :, :piece] + total[:, :, piece : 2 * piece] + total[:, :, 2 * piece :]
    for i in range(groups):
        for j in range(share):
            at = (i * share + j) * piece
            gain_out[:, at : at + piece] = total[i, j : j + 1]
    for copy in copies:
        copy.wait()


def local(
    segment_in,
    layer_weight,
    layer_gain,
    final_gain,
    head_weight,
    exit_rows,
    exit_count,
    exit_targets,
    exit_scale,
    out_grad,
):
    pipe = lax.axis_index("pipe")
    core = lax.axis_index("core")
    z = lax.axis_index("z")
    pipes = lax.axis_size("pipe")
    zs = lax.axis_size("z")
    block = z * 2 + core
    seg = segment_in[0]
    weight = layer_weight[0]
    gain = layer_gain[0]
    grad = out_grad[0]
    tokens, width = seg.shape
    slab = weight.shape[1]
    exits = exit_rows.shape[1]
    rows_all = pipes * exits
    vocab_part = head_weight.shape[0]
    half = -(-vocab_part // 32) * 16
    padded = -(-(half + 3) // 128) * 128
    place = jnp.stack([z, core, pipe * vocab_part, block]).astype(jnp.int32)
    whole = lambda *dims: pl.BlockSpec(dims, lambda i, *_: (0,) * len(dims))

    weight_other = swap(weight)
    halves = jnp.pad(head_weight, ((0, 2 * half - vocab_part), (0, 0))).reshape(2, half, slab)
    halves = jnp.pad(halves, ((0, 0), (0, padded - half), (0, 0)))
    head_mine = lax.dynamic_index_in_dim(halves, core, 0, keepdims=False)
    head_rest = lax.dynamic_index_in_dim(halves, 1 - core, 0, keepdims=False)
    head_other = swap(head_rest)

    my_rows = exit_rows[pipe]
    pick = (my_rows[:, None] == jnp.arange(tokens, dtype=jnp.int32)[None, :]).astype(BF16)
    row_in = jnp.dot(pick, seg, preferred_element_type=F32)
    row_inv = lax.rsqrt(jnp.mean(row_in * row_in, axis=-1, keepdims=True) + EPSILON)
    row_unit = row_in * row_inv
    row_normed = (row_unit * gain).astype(BF16)
    row_update = lax.reduce_precision(jnp.dot(row_normed, weight, preferred_element_type=F32), 8, 7)
    row_block = lax.dynamic_slice_in_dim(row_in, block * slab, slab, 1)
    hidden = (row_block + row_update).astype(BF16)

    held = tokens // (zs * 2)
    steps = 4
    chunk = width // steps
    grad_spec = pl.BlockSpec((zs, 1, held, 2 * slab), lambda i, at: (0, at[1], 0, at[0]))
    weight_spec = pl.BlockSpec((chunk, slab), lambda i, at: (i, 0))
    grad_view = grad.reshape(zs, 2, held, width)
    joined = jnp.concatenate([weight, weight_other], axis=1)
    chip_grad = lax.dynamic_slice(grad_view, (0, core, 0, z * 2 * slab), (zs, 1, held, 2 * slab))
    on_columns = (((1,), (1,)), ((), ()))

    def own_first(values):
        return jnp.where(core == 0, values, jnp.roll(values, slab, axis=1))

    main_sent = lax.dot_general(
        own_first(chip_grad.reshape(zs * held, 2 * slab)), joined, on_columns, preferred_element_type=F32
    ).astype(BF16)
    hidden, main_sent = lax.optimization_barrier((hidden, main_sent))
    main_grad = lax.psum_scatter(main_sent, "z", scatter_dimension=0, tiled=True)

    all_mine = spread(hidden, "pipe", pipes)
    all_other = swap(all_mine)
    gain_mine = lax.dynamic_slice_in_dim(final_gain, block * slab, slab, 0)[None]
    gain_other = lax.dynamic_slice_in_dim(final_gain, (z * 2 + 1 - core) * slab, slab, 0)[None]
    own = rows_all // zs
    part = vmem_call(
        functools.partial(logits_kernel, half),
        shape((zs, own, padded), BF16),
        all_mine,
        all_other,
        gain_mine,
        gain_other,
        head_mine,
        head_other,
    )
    parts = lax.all_to_all(part, "z", 0, 0)

    gain_part = pl.pallas_call(
        gain_kernel,
        grid_spec=pltpu.PrefetchScalarGridSpec(
            num_scalar_prefetch=1,
            grid=(steps,),
            in_specs=[
                grad_spec,
                pl.BlockSpec((zs, 1, held, width), lambda i, at: (0, at[1], 0, 0)),
                whole(1, exits),
                weight_spec,
                weight_spec,
            ],
            out_specs=pl.BlockSpec((1, chunk), lambda i, at: (0, i)),
            scratch_shapes=[pltpu.VMEM((zs * held, 128), F32)],
        ),
        out_shape=shape((1, width), F32),
        compiler_params=pltpu.CompilerParams(vmem_limit_bytes=LARGE),
    )(
        place,
        after(grad, part).reshape(zs, 2, held, width),
        seg.reshape(zs, 2, held, width),
        my_rows[None],
        weight,
        weight_other,
    )
    all_targets = exit_targets.reshape(rows_all, 1)
    targets = lax.dynamic_slice_in_dim(all_targets, z * own, own, 0)
    slot = jnp.arange(exits, dtype=jnp.int32)[None, :]
    weights = jnp.where(slot < exit_count[:, None], exit_scale[:, None], F32(0.0)).reshape(1, rows_all)
    weights = jnp.pad(lax.dynamic_slice_in_dim(weights, z * own, own, 1), ((0, 0), (0, 128 - own)))
    parts, gain_part = lax.optimization_barrier((parts, gain_part))

    expo, stats = kernel_call(
        functools.partial(softmax_kernel, width, half, vocab_part),
        [shape((own, padded), BF16), shape((8, 128), F32)],
        place,
        parts,
        targets - core * half,
    )
    expo, stats, main_grad = lax.optimization_barrier((expo, stats, main_grad))
    ex_mine = lax.all_gather(expo, "z", axis=0)
    stats_other = swap(stats)
    all_stats = spread(jnp.stack([stats, stats_other]), "pipe", pipes).reshape(pipes * 2, 8, 128)
    known_mine = vmem_call(
        functools.partial(finish_kernel, width), shape((zs, 8, 128), F32), all_stats, stats, weights
    )
    known_sent = known_mine
    known_mine = lax.all_to_all(known_mine, "z", 0, 0)

    first = block * held
    held_in = lax.dynamic_slice_in_dim(after(seg, stats_other), first, held, 0).astype(F32)
    held_grad = lax.dynamic_slice_in_dim(after(grad, stats_other), first, held, 0).astype(F32)
    held_inv = lax.rsqrt(jnp.mean(held_in * held_in, axis=-1, keepdims=True) + EPSILON)
    held_unit = held_in * held_inv
    unit_grad = main_grad.astype(F32) * gain
    centre = jnp.mean(unit_grad * held_unit, axis=-1, keepdims=True)
    main_out = (held_grad + (unit_grad - held_unit * centre) * held_inv).astype(BF16)
    all_stats, main_out = lax.optimization_barrier((all_stats, main_out))
    inputs = after(seg, known_sent).astype(F32)
    inv_rms = lax.rsqrt(jnp.mean(inputs * inputs, axis=-1, keepdims=True) + EPSILON)
    normed = (inputs * inv_rms * gain).astype(BF16)
    grad_slab = lax.dynamic_slice_in_dim(after(grad, known_sent), block * slab, slab, 1)
    grad_rows = jnp.dot(pick, grad_slab, preferred_element_type=F32)
    core_rows = exits // 2
    share = core_rows // zs
    core_unit = lax.dynamic_slice_in_dim(after(row_unit, known_sent), core * core_rows, core_rows, 0)
    share_at = core * core_rows + z * share
    share_unit = lax.dynamic_slice_in_dim(core_unit, z * share, share, 0)
    share_inv = lax.dynamic_slice_in_dim(row_inv, share_at, share, 0)
    known_mine, normed, grad_rows, core_unit, share_unit, share_inv = lax.optimization_barrier(
        (known_mine, normed, grad_rows, core_unit, share_unit, share_inv)
    )
    known_other = swap(known_mine)
    ex_mine, main_out = lax.optimization_barrier((after(ex_mine, known_other), main_out))
    main_all = lax.all_gather(main_out, ("z", "core"), axis=0, tiled=True)
    ex_other = swap(ex_mine)

    grads = [pltpu.VMEM((zs, own, padded), BF16)]
    exit_first, kept = piped_call(
        functools.partial(exit_kernel, half, vocab_part),
        [shape((rows_all, slab), F32), shape((rows_all, 128), F32)],
        place,
        ex_mine,
        known_mine,
        all_targets,
        head_mine,
        kept=(0,),
        scratch=grads,
    )
    (exit_part,) = piped_call(
        functools.partial(exit_rest_kernel, half, vocab_part),
        [shape((pipes, exits, slab), BF16)],
        place,
        ex_other,
        known_other,
        all_targets,
        head_rest,
        exit_first,
        held=(5,),
        scratch=grads,
    )
    exit_got = lax.all_to_all(exit_part, "pipe", 0, 0)
    kept_all = kept
    kept = lax.dynamic_slice_in_dim(kept, pipe * exits, exits, 0)
    exit_got, kept = lax.optimization_barrier((exit_got, kept))
    row_mine, row_send, row_rounded = kernel_call(
        row_kernel,
        [shape((core_rows, slab), F32)] * 2 + [shape((exits, slab), BF16)],
        place,
        exit_got,
        hidden,
        kept,
        gain_mine,
        grad_rows,
    )

    piece = slab * 2 // share
    send = kernel_call(
        send_kernel,
        shape((zs, share, width + 4 * slab + 3 * piece), BF16),
        place,
        row_mine,
        swap(row_send),
        weight,
        weight_other,
        core_unit,
        gain_part,
    )
    got = lax.all_to_all(send, "z", 0, 0)
    put = pick.T
    is_exit = jnp.any(pick > 0, axis=0)
    slab_rounded = jnp.where(
        is_exit[:, None], jnp.dot(put, after(row_rounded, send), preferred_element_type=F32).astype(BF16), grad_slab
    )
    over_rows = (((0,), (0,)), ((), ()))
    weight_grad = lax.dot_general(normed, slab_rounded, over_rows, preferred_element_type=F32).astype(BF16)
    got, weight_grad = lax.optimization_barrier((got, weight_grad))
    last = vmem_call(
        functools.partial(share_kernel, 2 * slab),
        shape((zs, share, width + 3 * piece), BF16),
        got,
        gain[None],
        share_unit,
        share_inv,
    )
    last, main_all = lax.optimization_barrier((last, main_all))
    (head_grad,) = piped_call(
        functools.partial(head_kernel, half, vocab_part),
        [shape((vocab_part, slab), BF16)],
        place,
        all_mine,
        gain_mine,
        after(kept_all, last),
        all_targets,
        ex_mine,
        ex_other,
        known_mine,
        known_other,
        scratch=grads,
    )
    last = lax.all_to_all(last, "z", 0, 0)
    main_near = pl.pallas_call(
        fetch_kernel,
        in_specs=[pl.BlockSpec(memory_space=pl.ANY)],
        out_specs=pl.BlockSpec(memory_space=pltpu.VMEM),
        out_shape=shape((tokens, width), BF16),
        scratch_shapes=[pltpu.SemaphoreType.DMA((4,))],
        compiler_params=pltpu.CompilerParams(vmem_limit_bytes=SMALL),
    )(main_all)
    last, head_grad, main_near = lax.optimization_barrier((last, head_grad, main_near))
    last_other = swap(last)
    in_vmem = pl.BlockSpec(memory_space=pltpu.VMEM)
    input_grad, gain_grad, _ = pl.pallas_call(
        last_kernel,
        in_specs=[pl.BlockSpec(memory_space=pltpu.SMEM)] * 2 + [in_vmem] * 3,
        out_specs=[pl.BlockSpec(memory_space=pl.ANY), in_vmem, in_vmem],
        out_shape=[shape((tokens, width), BF16), shape((1, width), F32), shape((tokens, width), BF16)],
        input_output_aliases={4: 2},
        scratch_shapes=[pltpu.SemaphoreType.DMA((4,))],
        compiler_params=pltpu.CompilerParams(vmem_limit_bytes=SMALL),
    )(place, my_rows, last, last_other, main_near)
    return (input_grad[None], weight_grad[None], gain_grad, head_grad)


def solution(mesh):
    pipes, tensors = mesh.devices.shape
    fine = Mesh(mesh.devices.reshape(pipes, tensors // 2, 2), ("pipe", "z", "core"))
    tensor = ("z", "core")
    in_specs = (
        P("pipe", None, None),
        P("pipe", None, tensor),
        P("pipe", None),
        P(),
        P("pipe", tensor),
        P(),
        P(),
        P(),
        P(),
        P("pipe", None, None),
    )
    out_specs = (
        P("pipe", None, None),
        P("pipe", None, tensor),
        P("pipe", None),
        P("pipe", tensor),
    )
    return jax.shard_map(local, mesh=fine, in_specs=in_specs, out_specs=out_specs, check_vma=False)
```

```python
import functools

import jax
import jax.numpy as jnp
from jax import lax
from jax.experimental import pallas as pl
from jax.experimental.pallas import tpu as pltpu
from jax.sharding import Mesh, PartitionSpec as P

F32 = jnp.float32
BF16 = jnp.bfloat16
EPSILON = 1e-05
SMALL = 20 * 1024 * 1024
VMEM = 32 * 1024 * 1024
LARGE = 56 * 1024 * 1024
LARGEST = 63 * 1024 * 1024


def spread(values, axis, count):
    return lax.all_to_all(jnp.broadcast_to(values[None], (count,) + values.shape), axis, 0, 0)


def swap(values):
    return lax.ppermute(values, "core", [(0, 1), (1, 0)])


def kernel_call(body, out, *operands):
    return pl.pallas_call(
        body,
        out_shape=out,
        in_specs=[
            pl.BlockSpec(memory_space=pltpu.SMEM if i == 0 else pltpu.VMEM) for i in range(len(operands))
        ],
        out_specs=jax.tree.map(lambda _: pl.BlockSpec(memory_space=pltpu.VMEM), out),
        compiler_params=pltpu.CompilerParams(vmem_limit_bytes=VMEM),
    )(*operands)


def vmem_call(body, out, *operands):
    return pl.pallas_call(
        body,
        out_shape=out,
        compiler_params=pltpu.CompilerParams(vmem_limit_bytes=VMEM),
    )(*operands)


def piped_call(body, out, *operands, held=(), kept=(), scratch=(), limit=LARGEST):
    def spec(value, stays):
        if stays:
            return pl.BlockSpec(memory_space=pltpu.VMEM)
        return pl.BlockSpec(value.shape, lambda i: (0,) * len(value.shape))

    return pl.pallas_call(
        body,
        grid=(1,),
        out_shape=out,
        in_specs=[pl.BlockSpec(memory_space=pltpu.SMEM)]
        + [spec(value, i in held) for i, value in enumerate(operands[1:], 1)],
        out_specs=[spec(value, i in kept) for i, value in enumerate(out)],
        scratch_shapes=list(scratch),
        compiler_params=pltpu.CompilerParams(vmem_limit_bytes=limit),
    )(*operands)


def shape(dims, dtype):
    return jax.ShapeDtypeStruct(dims, dtype)


def after(values, done):
    return lax.optimization_barrier((values, done))[0]


def pieces3(values):
    first = values.astype(BF16).astype(F32)
    rest = values - first
    second = rest.astype(BF16).astype(F32)
    return [first, second, rest - second]


def chip_term(core, grad, weight, weight_other):
    count, _, held, columns = grad.shape
    slab = columns // 2
    over = (((1,), (1,)), ((), ()))
    low = grad[:, 0, :, :slab].reshape(count * held, slab)
    high = grad[:, 0, :, slab:].reshape(count * held, slab)
    part = lax.dot_general(jnp.where(core == 0, low, high), weight[...], over, preferred_element_type=F32)
    return part + lax.dot_general(
        jnp.where(core == 0, high, low), weight_other[...], over, preferred_element_type=F32
    )


def gain_kernel(place, grad, seg, ids, weight, weight_other, gain_out, inverse):
    core = place[1]
    step = pl.program_id(0)
    count, _, held, width = seg.shape
    tokens = count * held

    @pl.when(step == 0)
    def _():
        full = seg[...].reshape(tokens, width).astype(F32)
        inv = lax.rsqrt(jnp.mean(full * full, axis=-1, keepdims=True) + EPSILON)
        index = lax.broadcasted_iota(jnp.int32, (tokens, ids.shape[1]), 0)
        index = (index // held * 2 + core) * held + index % held
        found = jnp.max((index == ids[...]).astype(F32), axis=-1, keepdims=True) > 0.0
        inverse[...] = jnp.broadcast_to(jnp.where(found, 0.0, inv), inverse.shape)

    part = chip_term(core, grad, weight, weight_other)
    chunk = part.shape[1]
    unit = seg[:, 0, :, pl.ds(pl.multiple_of(step * chunk, chunk), chunk)].reshape(tokens, chunk).astype(F32)
    gain_out[...] = jnp.sum(part * (unit * inverse[:, :1]), axis=0, keepdims=True)


def logits_kernel(half, mine, other, gain_mine, gain_other, head_mine, head_other, out):
    squares = 0.0
    part = 0.0
    for row, gain, head in ((mine, gain_mine, head_mine), (other, gain_other, head_other)):
        row = row[...].reshape(-1, row.shape[-1]).astype(F32)
        squares += jnp.sum(row * row, axis=-1, keepdims=True)
        part += lax.dot_general(
            (row * gain[...]).astype(BF16), head[...], (((1,), (1,)), ((), ())), preferred_element_type=F32
        )
    column = lax.broadcasted_iota(jnp.int32, part.shape, 1)
    for i, piece in enumerate(pieces3(squares)):
        part = jnp.where(column == half + i, piece, part)
    out[...] = part.astype(BF16).reshape(out.shape)


def softmax_kernel(width, half, vocab, place, parts, targets, expo_out, stats):
    core, start = place[1], place[2]
    total = parts[0].astype(F32)
    for i in range(1, parts.shape[0]):
        total += parts[i].astype(F32)
    inv = lax.rsqrt(jnp.sum(total[:, half : half + 3], axis=-1, keepdims=True) / width + EPSILON)
    logits = total * inv
    column = lax.broadcasted_iota(jnp.int32, logits.shape, 1)
    live = (column < half) & (column + core * half < vocab)
    top = jnp.max(jnp.where(live, logits, -jnp.inf), axis=-1, keepdims=True)
    shifted = jnp.where(live, logits - top, -jnp.inf)
    expo = jnp.exp(shifted)
    expo_out[...] = expo.astype(BF16)
    hit = live & (column == targets[...] - start)
    values = [
        top,
        jnp.sum(expo, axis=-1, keepdims=True),
        jnp.sum(jnp.where(live, expo * shifted, 0.0), axis=-1, keepdims=True),
        jnp.sum(jnp.where(hit, logits, 0.0), axis=-1, keepdims=True),
        inv,
    ]
    lane = lax.broadcasted_iota(jnp.int32, (logits.shape[0], 128), 1)
    table = jnp.zeros(lane.shape, F32)
    for i, value in enumerate(values):
        table = jnp.where(lane == i, value, table)
    table = jnp.concatenate([table, jnp.zeros((128 - table.shape[0], 128), F32)])
    stats[...] = table.T[: stats.shape[0]]


def merged(stats):
    tops, totals, alongs, hits = [stats[:, i] for i in range(4)]
    top = jnp.max(tops, axis=0, keepdims=True)
    lower = jnp.exp(tops - top)
    total = jnp.sum(totals * lower, axis=0, keepdims=True)
    along = jnp.sum((alongs + (tops - top) * totals) * lower, axis=0, keepdims=True)
    return top, total, along, jnp.sum(hits, axis=0, keepdims=True)


def finish_kernel(width, stats, own, weights, known):
    top, total, along, hits = merged(stats[...])
    weight = weights[...]
    factor = weight * (jnp.exp(own[0:1] - top) / total)
    target = weight * (jnp.exp(hits - top) / total - 1.0)
    mean = weight * (along / total - (hits - top)) / width
    rest = jnp.zeros((known.shape[1] - 4, known.shape[2]), F32)
    known[...] = jnp.broadcast_to(jnp.concatenate([factor, target, mean, own[4:5], rest])[None], known.shape)


def logit_grads(half, vocab, which, start, expo, known, targets, grad, kept):
    count, rows, columns = expo.shape
    column = lax.broadcasted_iota(jnp.int32, (rows, columns), 1)
    lane = lax.broadcasted_iota(jnp.int32, (rows, 128), 1)
    live = (column < half) & (column + which * half < vocab)
    for i in range(count):
        table = jnp.concatenate([known[i], jnp.zeros((128 - known.shape[1], 128), F32)]).T[:rows]
        hit = (column + which * half == targets[i * rows : (i + 1) * rows, :] - start) & live
        grad[i] = jnp.where(hit, table[:, 1:2], expo[i].astype(F32) * table[:, 0:1]).astype(BF16)
        if kept is not None:
            kept[i * rows : (i + 1) * rows, :] = jnp.where(lane == 0, table[:, 2:3], table[:, 3:4])
    return grad[...].reshape(count * rows, columns)


def exit_kernel(half, vocab, place, expo, known, targets, head, part, kept, grad):
    rows = logit_grads(half, vocab, place[1], place[2], expo, known, targets, grad, kept)
    part[...] = jnp.dot(rows, head[...], preferred_element_type=F32)


def exit_rest_kernel(half, vocab, place, expo, known, targets, head, before, part, grad):
    rows = logit_grads(half, vocab, 1 - place[1], place[2], expo, known, targets, grad, None)
    total = before[...] + jnp.dot(rows, head[...], preferred_element_type=F32)
    part[...] = total.astype(BF16).reshape(part.shape)


def head_kernel(half, vocab, place, row, gain, kept, targets, ex_mine, ex_other, known_mine, known_other, out, grad):
    core, start = place[1], place[2]
    row = row[...].reshape(-1, row.shape[-1]).astype(F32)
    normed = (row * kept[:, 1:2] * gain[...]).astype(BF16)
    over_rows = (((0,), (0,)), ((), ()))
    parts = []
    for which, expo, known in ((core, ex_mine, known_mine), (1 - core, ex_other, known_other)):
        rows = logit_grads(half, vocab, which, start, expo, known, targets, grad, None)
        parts.append(lax.dot_general(rows, normed, over_rows, preferred_element_type=F32))
    low, high = parts
    out[:half, :] = jnp.where(core == 0, low, high)[:half].astype(BF16)
    out[half:, :] = jnp.where(core == 0, high, low)[: out.shape[0] - half].astype(BF16)


def row_kernel(place, got, hidden, kept, gain, grad_rows, mine, other, whole):
    core = place[1]
    total = got[0].astype(F32)
    for i in range(1, got.shape[0]):
        total += got[i].astype(F32)
    mean, inv = kept[:, 0:1], kept[:, 1:2]
    back = (total * gain[...] - hidden[...].astype(F32) * inv * mean) * inv
    rows = grad_rows[...] + back
    whole[...] = rows.astype(BF16)
    half = mine.shape[0]
    mine[...] = jnp.where(core == 0, rows[:half], rows[half:])
    other[...] = jnp.where(core == 0, rows[half:], rows[:half])


def send_kernel(place, part, mine, other, unit, gain_part, out):
    core = place[1]
    part = part[...]
    gain = gain_part[...] + jnp.sum(part * unit[...], axis=0, keepdims=True)
    low = jnp.where(core == 0, mine[...], other[...])
    high = jnp.where(core == 0, other[...], mine[...])
    rows = jnp.concatenate([low, high], axis=1)
    rounded = rows.astype(BF16)
    rest = (rows - rounded.astype(F32)).astype(BF16)
    part = part.astype(BF16)
    gains = [values.astype(BF16) for values in pieces3(gain)]
    count, share, _ = out.shape
    width, slab = part.shape[1], mine.shape[1]
    piece = width // (count * share)
    for i in range(count):
        at = slice(i * share, (i + 1) * share)
        out[i, :, :width] = part[at]
        out[i, :, width : width + 2 * slab] = rounded[at]
        out[i, :, width + 2 * slab : width + 4 * slab] = rest[at]
        for j in range(share):
            first = (i * share + j) * piece
            for k in range(3):
                to = width + 4 * slab + k * piece
                out[i, j : j + 1, to : to + piece] = gains[k][:, first : first + piece]


def share_kernel(slabs, got, gain, unit, inv, out):
    total = got[0].astype(F32)
    for i in range(1, got.shape[0]):
        total += got[i].astype(F32)
    width = gain.shape[1]
    residual = jnp.concatenate(
        [
            got[i, :, width : width + slabs].astype(F32) + got[i, :, width + slabs : width + 2 * slabs].astype(F32)
            for i in range(got.shape[0])
        ],
        axis=1,
    )
    unit_grad = total[:, :width] * gain[...]
    centre = jnp.mean(unit_grad * unit[...], axis=-1, keepdims=True)
    rows = residual + (unit_grad - unit[...] * centre) * inv[...]
    gains = total[:, width + 2 * slabs :]
    piece = gains.shape[1] // 3
    gains = gains[:, :piece] + gains[:, piece : 2 * piece] + gains[:, 2 * piece :]
    whole = jnp.concatenate([rows] + pieces3(gains), axis=1)
    out[...] = jnp.broadcast_to(whole.astype(BF16)[None], out.shape)


def last_kernel(place, ids, mine, other, main, out, gain_out, block, into, outof):
    core = place[1]
    width = block.shape[1]
    parts = into.shape[0]
    count = width // parts
    columns = [slice(k * count, (k + 1) * count) for k in range(parts)]
    loads = [pltpu.make_async_copy(main.at[:, c], block.at[:, c], into.at[k]) for k, c in enumerate(columns)]
    stores = [pltpu.make_async_copy(block.at[:, c], out.at[:, c], outof.at[k]) for k, c in enumerate(columns)]
    for load in loads:
        load.start()
    groups, share = mine.shape[:2]
    spots = []
    for rows, first in ((mine, core), (other, 1 - core)):
        for i in range(groups):
            for j in range(share):
                at = ids[first * groups * share + i * share + j]
                start = pl.multiple_of(at // 16 * 16, 16)
                spots.append((rows, i, j, start, at - start))
    tile = lax.broadcasted_iota(jnp.int32, (16, count), 0)
    for k, c in enumerate(columns):
        loads[k].wait()
        for rows, i, j, start, at in spots:
            block[pl.ds(start, 16), c] = jnp.where(tile == at, rows[i, j : j + 1, c], block[pl.ds(start, 16), c])
        stores[k].start()
    piece = (mine.shape[2] - width) // 3
    total = mine[:, :, width:].astype(F32) + other[:, :, width:].astype(F32)
    total = total[:, :, :piece] + total[:, :, piece : 2 * piece] + total[:, :, 2 * piece :]
    for i in range(groups):
        for j in range(share):
            at = (i * share + j) * piece
            gain_out[:, at : at + piece] = total[i, j : j + 1]
    for store in stores:
        store.wait()


def local(
    segment_in,
    layer_weight,
    layer_gain,
    final_gain,
    head_weight,
    exit_rows,
    exit_count,
    exit_targets,
    exit_scale,
    out_grad,
):
    pipe = lax.axis_index("pipe")
    core = lax.axis_index("core")
    z = lax.axis_index("z")
    pipes = lax.axis_size("pipe")
    zs = lax.axis_size("z")
    block = z * 2 + core
    seg = segment_in[0]
    weight = layer_weight[0]
    gain = layer_gain[0]
    grad = out_grad[0]
    tokens, width = seg.shape
    slab = weight.shape[1]
    exits = exit_rows.shape[1]
    rows_all = pipes * exits
    vocab_part = head_weight.shape[0]
    half = -(-vocab_part // 32) * 16
    padded = -(-(half + 3) // 128) * 128
    place = jnp.stack([z, core, pipe * vocab_part, block]).astype(jnp.int32)
    whole = lambda *dims: pl.BlockSpec(dims, lambda i, *_: (0,) * len(dims))

    weight_other = swap(weight)
    halves = jnp.pad(head_weight, ((0, 2 * half - vocab_part), (0, 0))).reshape(2, half, slab)
    halves = jnp.pad(halves, ((0, 0), (0, padded - half), (0, 0)))
    head_mine = lax.dynamic_index_in_dim(halves, core, 0, keepdims=False)
    head_rest = lax.dynamic_index_in_dim(halves, 1 - core, 0, keepdims=False)
    head_other = swap(head_rest)

    my_rows = exit_rows[pipe]
    pick = (my_rows[:, None] == jnp.arange(tokens, dtype=jnp.int32)[None, :]).astype(BF16)
    row_in = jnp.dot(pick, seg, preferred_element_type=F32)
    row_inv = lax.rsqrt(jnp.mean(row_in * row_in, axis=-1, keepdims=True) + EPSILON)
    row_unit = row_in * row_inv
    row_normed = (row_unit * gain).astype(BF16)
    row_update = lax.reduce_precision(jnp.dot(row_normed, weight, preferred_element_type=F32), 8, 7)
    row_block = lax.dynamic_slice_in_dim(row_in, block * slab, slab, 1)
    hidden = (row_block + row_update).astype(BF16)

    held = tokens // (zs * 2)
    steps = 4
    chunk = width // steps
    grad_spec = pl.BlockSpec((zs, 1, held, 2 * slab), lambda i, at: (0, at[1], 0, at[0]))
    weight_spec = pl.BlockSpec((chunk, slab), lambda i, at: (i, 0))
    grad_view = grad.reshape(zs, 2, held, width)
    joined = jnp.concatenate([weight, weight_other], axis=1)
    chip_grad = lax.dynamic_slice(grad_view, (0, core, 0, z * 2 * slab), (zs, 1, held, 2 * slab))
    on_columns = (((1,), (1,)), ((), ()))

    def own_first(values):
        return jnp.where(core == 0, values, jnp.roll(values, slab, axis=1))

    main_sent = lax.dot_general(
        own_first(chip_grad.reshape(zs * held, 2 * slab)), joined, on_columns, preferred_element_type=F32
    ).astype(BF16)
    hidden, main_sent = lax.optimization_barrier((hidden, main_sent))
    main_grad = lax.psum_scatter(main_sent, "z", scatter_dimension=0, tiled=True)

    all_mine = spread(hidden, "pipe", pipes)
    all_other = swap(all_mine)
    gain_mine = lax.dynamic_slice_in_dim(final_gain, block * slab, slab, 0)[None]
    gain_other = lax.dynamic_slice_in_dim(final_gain, (z * 2 + 1 - core) * slab, slab, 0)[None]
    own = rows_all // zs
    part = vmem_call(
        functools.partial(logits_kernel, half),
        shape((zs, own, padded), BF16),
        all_mine,
        all_other,
        gain_mine,
        gain_other,
        head_mine,
        head_other,
    )
    parts = lax.all_to_all(part, "z", 0, 0)

    gain_part = pl.pallas_call(
        gain_kernel,
        grid_spec=pltpu.PrefetchScalarGridSpec(
            num_scalar_prefetch=1,
            grid=(steps,),
            in_specs=[
                grad_spec,
                pl.BlockSpec((zs, 1, held, width), lambda i, at: (0, at[1], 0, 0)),
                whole(1, exits),
                weight_spec,
                weight_spec,
            ],
            out_specs=pl.BlockSpec((1, chunk), lambda i, at: (0, i)),
            scratch_shapes=[pltpu.VMEM((zs * held, 128), F32)],
        ),
        out_shape=shape((1, width), F32),
        compiler_params=pltpu.CompilerParams(vmem_limit_bytes=LARGE),
    )(
        place,
        after(grad, part).reshape(zs, 2, held, width),
        seg.reshape(zs, 2, held, width),
        my_rows[None],
        weight,
        weight_other,
    )
    all_targets = exit_targets.reshape(rows_all, 1)
    targets = lax.dynamic_slice_in_dim(all_targets, z * own, own, 0)
    slot = jnp.arange(exits, dtype=jnp.int32)[None, :]
    weights = jnp.where(slot < exit_count[:, None], exit_scale[:, None], F32(0.0)).reshape(1, rows_all)
    weights = jnp.pad(lax.dynamic_slice_in_dim(weights, z * own, own, 1), ((0, 0), (0, 128 - own)))
    parts, gain_part = lax.optimization_barrier((parts, gain_part))

    expo, stats = kernel_call(
        functools.partial(softmax_kernel, width, half, vocab_part),
        [shape((own, padded), BF16), shape((8, 128), F32)],
        place,
        parts,
        targets - core * half,
    )
    expo, stats, main_grad = lax.optimization_barrier((expo, stats, main_grad))
    ex_mine = lax.all_gather(expo, "z", axis=0)
    stats_other = swap(stats)
    all_stats = spread(jnp.stack([stats, stats_other]), "pipe", pipes).reshape(pipes * 2, 8, 128)
    known_mine = vmem_call(
        functools.partial(finish_kernel, width), shape((zs, 8, 128), F32), all_stats, stats, weights
    )
    known_sent = known_mine
    known_mine = lax.all_to_all(known_mine, "z", 0, 0)

    first = block * held
    held_in = lax.dynamic_slice_in_dim(after(seg, stats_other), first, held, 0).astype(F32)
    held_grad = lax.dynamic_slice_in_dim(after(grad, stats_other), first, held, 0).astype(F32)
    held_inv = lax.rsqrt(jnp.mean(held_in * held_in, axis=-1, keepdims=True) + EPSILON)
    held_unit = held_in * held_inv
    unit_grad = main_grad.astype(F32) * gain
    centre = jnp.mean(unit_grad * held_unit, axis=-1, keepdims=True)
    main_out = (held_grad + (unit_grad - held_unit * centre) * held_inv).astype(BF16)
    all_stats, main_out = lax.optimization_barrier((all_stats, main_out))
    inputs = after(seg, known_sent).astype(F32)
    inv_rms = lax.rsqrt(jnp.mean(inputs * inputs, axis=-1, keepdims=True) + EPSILON)
    normed = (inputs * inv_rms * gain).astype(BF16)
    grad_slab = lax.dynamic_slice_in_dim(after(grad, known_sent), block * slab, slab, 1)
    grad_rows = jnp.dot(pick, grad_slab, preferred_element_type=F32)
    core_rows = exits // 2
    share = core_rows // zs
    core_unit = lax.dynamic_slice_in_dim(after(row_unit, known_sent), core * core_rows, core_rows, 0)
    share_at = core * core_rows + z * share
    share_unit = lax.dynamic_slice_in_dim(core_unit, z * share, share, 0)
    share_inv = lax.dynamic_slice_in_dim(row_inv, share_at, share, 0)
    known_mine, normed, grad_rows, core_unit, share_unit, share_inv = lax.optimization_barrier(
        (known_mine, normed, grad_rows, core_unit, share_unit, share_inv)
    )
    known_other = swap(known_mine)
    ex_mine, main_out = lax.optimization_barrier((after(ex_mine, known_other), main_out))
    main_all = lax.all_gather(main_out, ("z", "core"), axis=0, tiled=True)
    ex_other = swap(ex_mine)

    grads = [pltpu.VMEM((zs, own, padded), BF16)]
    exit_first, kept = piped_call(
        functools.partial(exit_kernel, half, vocab_part),
        [shape((rows_all, slab), F32), shape((rows_all, 128), F32)],
        place,
        ex_mine,
        known_mine,
        all_targets,
        head_mine,
        kept=(0,),
        scratch=grads,
    )
    (exit_part,) = piped_call(
        functools.partial(exit_rest_kernel, half, vocab_part),
        [shape((pipes, exits, slab), BF16)],
        place,
        ex_other,
        known_other,
        all_targets,
        head_rest,
        exit_first,
        held=(5,),
        scratch=grads,
    )
    exit_got = lax.all_to_all(exit_part, "pipe", 0, 0)
    kept_all = kept
    kept = lax.dynamic_slice_in_dim(kept, pipe * exits, exits, 0)
    (head_grad,) = piped_call(
        functools.partial(head_kernel, half, vocab_part),
        [shape((vocab_part, slab), BF16)],
        place,
        all_mine,
        gain_mine,
        after(kept_all, exit_part),
        all_targets,
        ex_mine,
        ex_other,
        known_mine,
        known_other,
        scratch=grads,
    )
    exit_got, kept, head_grad = lax.optimization_barrier((exit_got, kept, head_grad))
    row_mine, row_send, row_rounded = kernel_call(
        row_kernel,
        [shape((core_rows, slab), F32)] * 2 + [shape((exits, slab), BF16)],
        place,
        exit_got,
        hidden,
        kept,
        gain_mine,
        grad_rows,
    )

    piece = slab * 2 // share
    row_other = swap(row_send)
    row_part = lax.dot_general(
        jnp.concatenate([row_mine, row_other], axis=1).astype(BF16), joined, on_columns, preferred_element_type=F32
    )
    send = kernel_call(
        send_kernel,
        shape((zs, share, width + 4 * slab + 3 * piece), BF16),
        place,
        row_part,
        row_mine,
        row_other,
        core_unit,
        gain_part,
    )
    got = lax.all_to_all(send, "z", 0, 0)
    put = pick.T
    is_exit = jnp.any(pick > 0, axis=0)
    slab_rounded = jnp.where(
        is_exit[:, None], jnp.dot(put, after(row_rounded, send), preferred_element_type=F32).astype(BF16), grad_slab
    )
    over_rows = (((0,), (0,)), ((), ()))
    weight_grad = lax.dot_general(normed, slab_rounded, over_rows, preferred_element_type=F32).astype(BF16)
    got, weight_grad = lax.optimization_barrier((got, weight_grad))
    last = vmem_call(
        functools.partial(share_kernel, 2 * slab),
        shape((zs, share, width + 3 * piece), BF16),
        got,
        gain[None],
        share_unit,
        share_inv,
    )
    last, main_all = lax.optimization_barrier((last, main_all))
    last = lax.all_to_all(last, "z", 0, 0)
    last_other = swap(last)
    in_vmem = pl.BlockSpec(memory_space=pltpu.VMEM)
    parts = 4
    input_grad, gain_grad = pl.pallas_call(
        last_kernel,
        in_specs=[pl.BlockSpec(memory_space=pltpu.SMEM)] * 2 + [in_vmem] * 2 + [pl.BlockSpec(memory_space=pl.ANY)],
        out_specs=[pl.BlockSpec(memory_space=pl.ANY), in_vmem],
        out_shape=[shape((tokens, width), BF16), shape((1, width), F32)],
        scratch_shapes=[
            pltpu.VMEM((tokens, width), BF16),
            pltpu.SemaphoreType.DMA((parts,)),
            pltpu.SemaphoreType.DMA((parts,)),
        ],
        compiler_params=pltpu.CompilerParams(vmem_limit_bytes=LARGE),
    )(place, my_rows, last, last_other, main_all)
    return (input_grad[None], weight_grad[None], gain_grad, head_grad)


def solution(mesh):
    pipes, tensors = mesh.devices.shape
    fine = Mesh(mesh.devices.reshape(pipes, tensors // 2, 2), ("pipe", "z", "core"))
    tensor = ("z", "core")
    in_specs = (
        P("pipe", None, None),
        P("pipe", None, tensor),
        P("pipe", None),
        P(),
        P("pipe", tensor),
        P(),
        P(),
        P(),
        P(),
        P("pipe", None, None),
    )
    out_specs = (
        P("pipe", None, None),
        P("pipe", None, tensor),
        P("pipe", None),
        P("pipe", tensor),
    )
    return jax.shard_map(local, mesh=fine, in_specs=in_specs, out_specs=out_specs, check_vma=False)
```
